32 devices in a mesh: ctx: 4 (over z), exp: 2 (over y), doc: 4 (over x, core).
Axes of the slice: x: 2, y: 2, z: 4, core: 2. Of those that a mesh axis runs over, the one named last changes fastest.
Arguments:
- projected: bfloat16 [2, 512, 4096], P(None, ('doc', 'ctx'), 'exp'), parts along dimension 1, may hold values from -6 to 6
- carried_tail: bfloat16 [12, 4096], P('doc', 'exp'), parts along dimension 0, may hold values from -6 to 6
- carried_state: float32 [64, 4096], P('doc', 'exp'), parts along dimension 0, may hold values from -6 to 6
- filter_taps: float32 [4, 4096], P(None, 'exp'), may hold values from -3 to 3
- filter_bias: float32 [4096], P('exp'), may hold values from -0.5 to 0.5
- select_weight: bfloat16 [160, 4096], P(None, 'exp'), may hold values from -0.09375 to 0.09375
- step_weight: bfloat16 [128, 4096], P(None, 'exp'), may hold values from -0.25 to 0.25
- step_bias: float32 [4096], P('exp'), may hold values from -7 to -2
- log_rate: float32 [16, 4096], P(None, 'exp'), may hold values from -1 to 1.5
- skip_gain: float32 [4096], P('exp'), may hold values from 0.5 to 1.5
- output_weight: bfloat16 [4096, 2048], P('exp', 'ctx'), may hold values from -0.09375 to 0.09375
- residual: bfloat16 [512, 2048], P(('doc', 'ctx', 'exp')), parts along dimension 0, may hold values from -6 to 6
- norm_gain: float32 [2048], replicated, may hold values from 0.5 to 1.5
- router: bfloat16 [2048, 4], replicated, may hold values from -0.125 to 0.125
- gate_weight: bfloat16 [57344, 2048], P(('ctx', 'exp')), may hold values from -0.125 to 0.125
- up_weight: bfloat16 [57344, 2048], P(('ctx', 'exp')), may hold values from -0.125 to 0.125
- down_weight: bfloat16 [57344, 2048], P(('ctx', 'exp')), may hold values from -0.046875 to 0.046875
- routes: int32 [512, 2], P(('doc', 'ctx', 'exp')), parts along dimension 0, may hold values from 0 to 3, all different within a row; in each aligned block of 16 rows (0 to 15, 16 to 31, ...) at most 10 rows name the same one
Outputs:
- layer_output: bfloat16 [512, 2048], P(('doc', 'ctx', 'exp')), parts along dimension 0
The draws below stay inside these ranges and needn't reach their ends.
There are 4 independent parts, one for each index of `doc`. The reference program is written for one: setup_inputs(seed, part) draws one part's arguments, and reference() takes and returns one part's arrays. A program takes and returns all parts, laid end to end along the dimension named above; an argument that names none is the same for every part. Nothing has to cross between parts.
Inputs may be any that keep to these rules, and one draw needn't show every extreme that they name: `routes`: the two ids of a row differ; within the 16 rows of one device no id is named more than 10 times.
All inputs are finite; a program needn't handle non-finite values.
Results may differ from the reference program's by a relative error of at most 0.0085.
Values may be sent and summed in bfloat16 or wider, within the bound.
No kernel may reach another device: no remote copies, remote signals or barrier semaphores. Data moves between devices by JAX's collectives and lax.ppermute only.
A program may use at most 192 MiB of HBM per device.

```python
import math
import jax
import jax.numpy as jnp
import numpy as np
from jax import lax

D = 2048
INNER = 4096
FF = 14336
DT_RANK = 128
STATE = 16
CONV = 4
EXPERTS = 4
TOK_DEV = 16
CAP = 10
SPAN = 7168
TOKENS = 128


def levels(rng, dims, split, smallest, top_value):
    gain = 1.0
    for position, shards_of in split:
        heights = jax.random.uniform(jax.random.fold_in(jax.random.fold_in(rng, 6), position), (shards_of,), jnp.float32, smallest / len(split), top_value / len(split))
        gain = gain * jnp.repeat(jnp.exp(heights), dims[position] // shards_of).reshape((-1,) + (1,) * (len(dims) - 1 - position))
    return gain


def assign_block(own_key, own, number, rows, amount, top, bound, slope):
    ranking = jax.random.permutation(own_key, amount)
    packed, usual = shares(amount, rows * top, bound, slope, True), shares(amount, rows * top, bound, slope, False)
    places = jnp.arange(amount)

    def named(sizes, rotation):
        used = int((sizes > 0).sum())
        fixed = max(1, used // 4)
        passed = fixed + (places - fixed + rotation * (used - fixed)) % max(1, amount - fixed)
        return jnp.zeros((amount,), jnp.int32).at[ranking[jnp.where(places < fixed, places, passed)]].set(jnp.asarray(sizes, jnp.int32))

    sizes = jnp.where(number % 4 == 0, named(packed, number // 4), named(usual, number - number // 4 - 1))
    mixed = jax.random.permutation(jax.random.fold_in(own, 3), amount)
    giver, receiver = mixed[0:amount // 2 * 2:2], mixed[1:amount // 2 * 2:2]
    slack = jnp.minimum(sizes[giver] - 1, bound - sizes[receiver]) // 2
    slack = jnp.where((giver == ranking[0]) | (receiver == ranking[0]) | (sizes[receiver] == 0), 0, jnp.maximum(slack, 0))
    passed = jax.random.randint(jax.random.fold_in(own, 4), (amount // 2,), 0, 1 << 20) % (slack + 1)
    sizes = sizes.at[giver].add(-passed).at[receiver].add(passed)
    items = jnp.searchsorted(jnp.cumsum(sizes), jnp.arange(rows * top), side="right").astype(jnp.int32)
    table = items.reshape(top, rows).T
    table = table[jax.random.permutation(jax.random.fold_in(own, 1), rows)]
    rotation = jax.random.randint(jax.random.fold_in(own, 2), (rows, 1), 0, top)
    return jnp.take_along_axis(table, (jnp.arange(top)[None, :] + rotation) % top, axis=1)


def shares(number_of, total, reach, slope, full):
    weights = [(1 << 20) // math.isqrt(rank ** slope) + 1 for rank in range(1, number_of + 1)]
    largest = reach if full else min(reach, max(-(-total // number_of), total * weights[0] // sum(weights)))
    least = 1 if total - largest >= number_of - 1 else 0
    holding, surplus = [largest] + [least] * (number_of - 1), total - largest - least * (number_of - 1)
    while surplus > 0:
        movable = [i for i in range(1, number_of) if holding[i] < largest] or [i for i in range(1, number_of) if holding[i] < reach]
        whole, left = sum([weights[i] for i in movable]), surplus
        for i in movable:
            more = min(reach - holding[i], max(1, left * weights[i] // whole), surplus)
            holding[i] = holding[i] + more
            surplus = surplus - more
    return np.array(holding)


def scatter_about(own_key, dims, deviation, limit, shards=(), kind=jnp.bfloat16):
    entries = jax.random.normal(own_key, dims, jnp.float32) * deviation
    if len(shards) > 0:
        entries = levels(own_key, dims, shards, -0.22, 0.18) * entries
    return jnp.clip(entries, min=-limit, max=limit).astype(kind)


def setup_inputs(seed: int = 0, part: int = 0) -> dict:
    key_of = jax.random.split(jax.random.key(seed), 19)
    part_splits = jax.random.split(jax.random.fold_in(key_of[18], part), 19)
    projected = scatter_about(part_splits[0], (2, TOKENS, INNER), 1.0, 6.0, ((1, 4), (2, 2)))
    carried_tail = scatter_about(part_splits[1], (CONV - 1, INNER), 1.0, 6.0, ((1, 2),))
    carried_state = scatter_about(part_splits[2], (STATE, INNER), 1.0, 6.0, ((1, 2),), jnp.float32)
    filter_taps = scatter_about(key_of[3], (CONV, INNER), 0.5, 3.0, ((1, 2),), jnp.float32)
    filter_bias = jnp.clip(jax.random.uniform(key_of[4], (INNER,), jnp.float32, -0.5, 0.5) * levels(key_of[4], (INNER,), ((0, 2),), -0.4, 0.0), -0.5, 0.5)
    select_weight = scatter_about(key_of[5], (DT_RANK + 2 * STATE, INNER), INNER ** -0.5, 0.09375, ((1, 2),))
    step_weight = scatter_about(key_of[6], (DT_RANK, INNER), (4 * DT_RANK) ** -0.5, 0.25, ((1, 2),))
    step_bias = jnp.clip(-7.0 + 5.0 * jax.random.uniform(key_of[7], (INNER,), jnp.float32) ** levels(key_of[7], (INNER,), ((0, 2),), -0.2, 0.2), -7.0, -2.0)
    log_rate = jnp.clip(-1.0 + 2.5 * jax.random.uniform(key_of[8], (STATE, INNER), jnp.float32) ** levels(key_of[8], (STATE, INNER), ((1, 2),), -0.2, 0.2), -1.0, 1.5)
    skip_gain = jnp.clip(0.5 + 1.0 * jax.random.uniform(key_of[9], (INNER,), jnp.float32) ** levels(key_of[9], (INNER,), ((0, 2),), -0.2, 0.2), 0.5, 1.5)
    output_weight = scatter_about(key_of[10], (INNER, D), INNER ** -0.5, 0.09375, ((0, 2), (1, 4)))
    residual = scatter_about(part_splits[11], (TOKENS, D), 1.0, 6.0, ((0, 8),))
    norm_gain = jnp.clip(1.0 + 0.1 * jax.random.normal(key_of[12], (D,), jnp.float32), 0.5, 1.5)
    router = scatter_about(key_of[13], (D, EXPERTS), D ** -0.5, 0.125)
    gate_weight = scatter_about(key_of[14], (EXPERTS * FF, D), D ** -0.5, 0.125, ((0, 8),))
    up_weight = scatter_about(key_of[15], (EXPERTS * FF, D), D ** -0.5, 0.125, ((0, 8),))
    down_weight = scatter_about(key_of[16], (EXPERTS * FF, D), FF ** -0.5, 0.046875, ((0, 8),))
    routes_keys = jax.random.split(jax.random.fold_in(part_splits[17], 1), TOKENS // TOK_DEV)
    routes_turns = jax.random.permutation(jax.random.fold_in(part_splits[17], 3), TOKENS // TOK_DEV)
    routes = jax.vmap(lambda own, number: assign_block(jax.random.fold_in(part_splits[17], 2), own, number, TOK_DEV, EXPERTS, 2, CAP, 1))(routes_keys, routes_turns).reshape((TOKENS, 2))
    return dict(projected=projected, carried_tail=carried_tail, carried_state=carried_state, filter_taps=filter_taps, filter_bias=filter_bias, select_weight=select_weight, step_weight=step_weight, step_bias=step_bias, log_rate=log_rate, skip_gain=skip_gain, output_weight=output_weight, residual=residual, norm_gain=norm_gain, router=router, gate_weight=gate_weight, up_weight=up_weight, down_weight=down_weight, routes=routes)


def contract_cols(left, right):
    return lax.dot_general(left, right, (((1,), (1,)), ((), ())), preferred_element_type=jnp.float32)

def reference(projected, carried_tail, carried_state, filter_taps, filter_bias, select_weight, step_weight, step_bias, log_rate, skip_gain, output_weight, residual, norm_gain, router, gate_weight, up_weight, down_weight, routes):
    x_input = projected[0]
    z_input = projected[1]
    tap_count = filter_taps.shape[0]
    padded = jnp.concatenate([carried_tail, x_input], axis=0).astype(jnp.float32)
    filtered = filter_bias[None, :] + jnp.zeros(x_input.shape, jnp.float32)
    for offset in range(tap_count):
        filtered = filtered + filter_taps[offset][None, :] * padded[offset:offset + TOKENS]
    activated = jax.nn.silu(filtered).astype(jnp.bfloat16)
    projections = contract_cols(activated, select_weight)
    delta_low = projections[:, :DT_RANK].astype(jnp.bfloat16)
    step_size = jax.nn.softplus(jnp.dot(delta_low, step_weight, preferred_element_type=jnp.float32) + step_bias[None, :])
    input_coef = projections[:, DT_RANK:DT_RANK + STATE]
    output_coef = projections[:, DT_RANK + STATE:]
    decay_rate = -jnp.exp(log_rate)
    active_values = activated.astype(jnp.float32)

    def advance(state_now, inputs):
        step_now, value_now, in_now, out_now = inputs
        state_now = jnp.exp(step_now[None, :] * decay_rate) * state_now + (step_now * value_now)[None, :] * in_now[:, None]
        return (state_now, lax.optimization_barrier(jnp.sum(out_now[:, None] * state_now, axis=0)))
    final_state, scan_out = lax.scan(advance, carried_state, (step_size, active_values, input_coef, output_coef))
    gated = ((scan_out + skip_gain[None, :] * active_values) * jax.nn.silu(z_input.astype(jnp.float32))).astype(jnp.bfloat16)
    mixer_out = jnp.dot(gated, output_weight, preferred_element_type=jnp.float32)
    mixed = (residual.astype(jnp.float32) + mixer_out).astype(jnp.bfloat16)
    mixed_values = mixed.astype(jnp.float32)
    mean_square = lax.optimization_barrier(jnp.mean(mixed_values * mixed_values, axis=-1, keepdims=True)) + 1e-06
    normed = (mixed_values * lax.rsqrt(mean_square) * norm_gain[None, :]).astype(jnp.bfloat16)
    logits = jnp.dot(normed, router, preferred_element_type=jnp.float32)
    expert_ids = jnp.arange(EXPERTS, dtype=jnp.int32)
    first_hot = (routes[:, 0:1] == expert_ids[None, :]).astype(jnp.float32)
    second_hot = (routes[:, 1:2] == expert_ids[None, :]).astype(jnp.float32)
    first_logit = lax.optimization_barrier(jnp.sum(logits * first_hot, axis=1))
    second_logit = lax.optimization_barrier(jnp.sum(logits * second_hot, axis=1))
    first_gate = 1.0 / (1.0 + jnp.exp(second_logit - first_logit))
    second_gate = 1.0 / (1.0 + jnp.exp(first_logit - second_logit))
    weights = first_gate[:, None] * first_hot + second_gate[:, None] * second_hot
    moe = jnp.zeros(mixed_values.shape, jnp.float32)
    for expert in range(EXPERTS):
        begin = expert * FF
        gate_act = contract_cols(normed, gate_weight[begin:begin + FF])
        up_act = contract_cols(normed, up_weight[begin:begin + FF])
        hidden = (jax.nn.silu(gate_act) * up_act).astype(jnp.bfloat16)
        expert_out = jnp.zeros(mixed_values.shape, jnp.float32)
        for block in range(FF // SPAN):
            lower = block * SPAN
            block_out = jnp.dot(hidden[:, lower:lower + SPAN], down_weight[begin + lower:begin + lower + SPAN], preferred_element_type=jnp.float32).astype(jnp.bfloat16)
            block_out = lax.optimization_barrier(block_out)
            expert_out = expert_out + block_out.astype(jnp.float32)
        moe = moe + weights[:, expert:expert + 1] * expert_out
    return (mixed_values + moe).astype(jnp.bfloat16)
```

```python
import functools
import math

import jax
import jax.numpy as jnp
from jax import lax
from jax.experimental import pallas as pl
from jax.experimental.pallas import tpu as pltpu
from jax.sharding import PartitionSpec as P

EXPERTS = 4
LANES = 128
FEW = 4
LOG2E = 1.4426950408889634
VMEM = pltpu.VMEM
SMEM = pltpu.SMEM
F32 = jnp.float32
BF16 = jnp.bfloat16


def contract_last(left, right):
    return lax.dot_general(left, right, (((1,), (1,)), ((), ())), preferred_element_type=F32)


def rotate(value, axis, steps):
    count = lax.axis_size(axis)
    return lax.ppermute(value, axis, [(i, (i + steps) % count) for i in range(count)])


def ring_places(axis):
    count = lax.axis_size(axis)
    if count > FEW:
        return jnp.zeros((1,), jnp.int32)
    me = lax.axis_index(axis)
    return jnp.stack([lax.rem(me + count - s, count) for s in range(count)]).astype(jnp.int32)


def spread(make, axis, join):
    count = lax.axis_size(axis)
    me = lax.axis_index(axis)
    if count <= FEW:
        return [make(me)] + [rotate(make(lax.rem(me + s, count)), axis, s) for s in range(1, count)]
    stacked = jnp.stack([make(jnp.int32(k)) for k in range(count)])
    moved = lax.all_to_all(stacked, axis, split_axis=0, concat_axis=0, tiled=True)
    return [jnp.concatenate([moved[k] for k in range(count)], axis=join)]


def pair_sum(value, axis):
    if lax.axis_size(axis) == 2:
        return [value, rotate(value, axis, 1)]
    total = lax.psum(value.astype(F32), axis).astype(value.dtype)
    return [total, jnp.zeros_like(total)]


def activate_kernel(count, places, tail, taps, bias, select, *refs):
    pieces, (active, proj, padded) = refs[:count], refs[count:]
    rows = pieces[0].shape[0]
    tap_count = taps.shape[0]
    padded[0:8, :] = tail[...]
    for index in range(count):
        start = pl.multiple_of(8 + places[index] * rows, 8)
        padded[pl.ds(start, rows), :] = pieces[index][...].astype(F32)
    tokens = active.shape[0]
    step = 32

    def block(number, carry):
        base = pl.multiple_of(number * step, step)
        window = padded[pl.ds(base, step + 8), :]
        total = jnp.broadcast_to(bias[...], (step, bias.shape[1]))
        for k in range(tap_count):
            offset = 8 - (tap_count - 1) + k
            total = total + taps[k : k + 1, :] * window[offset : offset + step, :]
        value = total / (1.0 + jnp.exp(-total))
        active[pl.ds(base, step), :] = value.astype(BF16)
        return carry

    lax.fori_loop(0, tokens // step, block, 0)
    for number in range(tokens // LANES):
        cut = slice(number * LANES, (number + 1) * LANES)
        proj[:, cut] = contract_last(select[...], active[cut, :])


def activate(places, pieces, tail, taps, bias, select):
    count = len(pieces)
    tokens = count * pieces[0].shape[0]
    channels = pieces[0].shape[1]
    return pl.pallas_call(
        functools.partial(activate_kernel, count),
        out_shape=(
            jax.ShapeDtypeStruct((tokens, channels), BF16),
            jax.ShapeDtypeStruct((select.shape[0], tokens), F32),
        ),
        in_specs=[pl.BlockSpec(memory_space=SMEM)] + [pl.BlockSpec(memory_space=VMEM)] * (4 + count),
        out_specs=(pl.BlockSpec(memory_space=VMEM),) * 2,
        scratch_shapes=[VMEM((tokens + 8, channels), F32)],
        compiler_params=pltpu.CompilerParams(vmem_limit_bytes=24 << 20),
        cost_estimate=pl.CostEstimate(
            flops=2 * tokens * channels * select.shape[0],
            bytes_accessed=4 * tokens * channels,
            transcendentals=tokens * channels,
        ),
        name="activate",
    )(places, tail, taps, bias, select, *pieces)


def scan_kernel(
    count, columns, places, parity, own, other, active, step_weight, step_bias, log_rate, skip_gain,
    state_in, out_weight, *refs,
):
    pieces = refs[:count]
    base_out, send_out, routes_out = refs[count : count + 3]
    sums, steps, scaled, decay, state, gated, coef, sem = refs[count + 3 :]
    tokens, channels = active.shape
    rank = step_weight.shape[0]
    state_size = log_rate.shape[0]
    folds = channels // LANES
    group = min(folds, 8)
    sums[...] = own[...] + other[...]
    copy = pltpu.make_async_copy(sums.at[pl.ds(rank, 2 * state_size), :], coef, sem)
    copy.start()

    for s8 in range(state_size // 8):
        for j in range(folds):
            lanes = slice(j * LANES, (j + 1) * LANES)
            there = slice((s8 * folds + j) * 8, (s8 * folds + j) * 8 + 8)
            decay[there, :] = jnp.exp(log_rate[s8 * 8 : s8 * 8 + 8, lanes]) * (-LOG2E)
            state[there, :] = state_in[s8 * 8 : s8 * 8 + 8, lanes]

    def fold_rows(row, first):
        return pl.ds((row // 8) * (folds * 8) + row % 8 + first * 8, group, stride=8)

    for number in range(tokens // LANES):
        cut = slice(number * LANES, (number + 1) * LANES)
        low = jnp.transpose(sums[0:rank, cut]).astype(BF16)
        width = min(channels, 256)
        for w in range(channels // width):
            lanes = slice(w * width, (w + 1) * width)
            raw = jnp.dot(low, step_weight[:, lanes], preferred_element_type=F32) + step_bias[:, lanes]
            size = jnp.maximum(raw, 0.0) + jnp.log1p(jnp.exp(-jnp.abs(raw)))
            times = size * active[cut, lanes].astype(F32)
            for i in range(LANES // 8):
                for j in range(width // LANES):
                    block = (number * LANES // 8 + i) * folds + w * (width // LANES) + j
                    there = slice(block * 8, block * 8 + 8)
                    part = (slice(i * 8, i * 8 + 8), slice(j * LANES, (j + 1) * LANES))
                    steps[there, :] = size[part]
                    scaled[there, :] = times[part]
    copy.wait()

    for first in range(0, folds, group):
        rates = [decay[fold_rows(s, first), :] for s in range(state_size)]
        start = tuple(state[fold_rows(s, first), :] for s in range(state_size))

        def eight(number, held):
            base = number * (folds * 8) + first * 8
            held = list(held)
            for r in range(8):
                token = number * 8 + r
                rows = pl.ds(base + r, group, stride=8)
                size, times = steps[rows, :], scaled[rows, :]
                total = None
                for s in range(state_size):
                    held[s] = jnp.exp2(size * rates[s]) * held[s] + times * coef[s, token]
                    term = held[s] * coef[state_size + s, token]
                    total = term if total is None else total + term
                steps[rows, :] = total
            return tuple(held)

        lax.fori_loop(0, tokens // 8, eight, start)

    rows = pieces[0].shape[0]
    tile = 16
    for index in range(count):
        begin = pl.multiple_of(places[index] * rows, tile)
        routes_out[pl.ds(begin, rows), :] = pieces[index][:, channels + columns :]

        def gate(number, carry):
            local = pl.multiple_of(number * tile, tile)
            here = pl.multiple_of(begin + local, tile)
            for j in range(folds):
                lanes = slice(j * LANES, (j + 1) * LANES)
                found = []
                for half in range(2):
                    block = pl.multiple_of((here // 8 + half) * (folds * 8) + j * 8, 8)
                    found.append(steps[pl.ds(block, 8), :])
                value = jnp.concatenate(found, axis=0)
                act = active[pl.ds(here, tile), lanes].astype(F32)
                z = pieces[index][pl.ds(local, tile), lanes].astype(F32)
                value = (value + skip_gain[:, lanes] * act) * (z / (1.0 + jnp.exp(-z)))
                gated[pl.ds(here, tile), lanes] = value.astype(BF16)
            return carry

        lax.fori_loop(0, rows // tile, gate, 0)

    step = LANES
    for number in range(tokens // step):
        cut = slice(number * step, (number + 1) * step)
        part = jnp.dot(gated[cut, :], out_weight[...], preferred_element_type=F32)
        sent = part.astype(BF16)
        send_out[cut, :] = sent
        base_out[cut, :] = sent.astype(F32)
    for index in range(count):
        begin = pl.multiple_of(places[index] * rows, tile)
        here = pl.ds(begin, rows)
        base_out[here, :] += pieces[index][:, channels : channels + columns].astype(F32)


def scan(places, parity, own, other, active, step_weight, step_bias, log_rate, skip_gain, state_in, out_weight, pieces):
    tokens, channels = active.shape
    columns = out_weight.shape[1]
    count = len(pieces)
    state_size = log_rate.shape[0]
    folded = (state_size * channels // LANES, LANES)
    return pl.pallas_call(
        functools.partial(scan_kernel, count, columns),
        out_shape=(
            jax.ShapeDtypeStruct((tokens, columns), F32),
            jax.ShapeDtypeStruct((tokens, columns), BF16),
            jax.ShapeDtypeStruct((tokens, LANES), BF16),
        ),
        in_specs=[pl.BlockSpec(memory_space=SMEM)] * 2 + [pl.BlockSpec(memory_space=VMEM)] * (9 + count),
        out_specs=(pl.BlockSpec(memory_space=VMEM),) * 3,
        scratch_shapes=[
            VMEM(own.shape, F32),
            VMEM((tokens * channels // LANES, LANES), F32),
            VMEM((tokens * channels // LANES, LANES), F32),
            VMEM(folded, F32),
            VMEM(folded, F32),
            VMEM((tokens, channels), BF16),
            SMEM((2 * state_size, tokens), F32),
            pltpu.SemaphoreType.DMA,
        ],
        compiler_params=pltpu.CompilerParams(vmem_limit_bytes=32 << 20),
        cost_estimate=pl.CostEstimate(
            flops=8 * tokens * channels * state_size,
            bytes_accessed=8 * tokens * channels,
            transcendentals=tokens * channels * state_size,
        ),
        name="scan",
    )(
        places, parity, own, other, active, step_weight, step_bias, log_rate, skip_gain, state_in,
        out_weight, *pieces,
    )


def expert_kernel(count, sends, places, targets, expert, gain, router, routes, gate, up, down, *refs):
    pieces = refs[:count]
    outs = refs[count : count + sends]
    own_rows = refs[count + sends]
    normed, total, weight = refs[count + sends + 1 : count + sends + 4]
    mixed = pieces[0] if count == 1 else refs[-1]
    number = pl.program_id(0)
    tokens, width = normed.shape
    chunk = LANES

    @pl.when(number == 0)
    def _():
        columns = pieces[0].shape[1]
        for index in range(count if count > 1 else 0):
            start = pl.multiple_of(places[index] * columns, LANES)
            mixed[:, pl.ds(start, columns)] = pieces[index][...]
        total[...] = jnp.zeros_like(total)
        for c in range(tokens // chunk):
            cut = slice(c * chunk, (c + 1) * chunk)
            value = mixed[cut, :].astype(F32)
            square = jnp.mean(value * value, axis=-1, keepdims=True) + 1e-06
            scaled = (value * lax.rsqrt(square) * gain[...]).astype(BF16)
            normed[cut, :] = scaled
            logits = contract_last(scaled, router[...])
            first = routes[cut, 0:1].astype(F32)
            second = routes[cut, 1:2].astype(F32)
            ids = lax.broadcasted_iota(jnp.int32, logits.shape, 1).astype(F32)
            first_logit = jnp.sum(jnp.where(ids == first, logits, 0.0), axis=1, keepdims=True)
            second_logit = jnp.sum(jnp.where(ids == second, logits, 0.0), axis=1, keepdims=True)
            mine = expert[0].astype(F32)
            first_gate = jnp.where(first == mine, 1.0 / (1.0 + jnp.exp(second_logit - first_logit)), 0.0)
            second_gate = jnp.where(second == mine, 1.0 / (1.0 + jnp.exp(first_logit - second_logit)), 0.0)
            weight[cut, :] = jnp.broadcast_to(first_gate + second_gate, (chunk, LANES))

    for c in range(tokens // chunk):
        cut = slice(c * chunk, (c + 1) * chunk)
        gate_act = contract_last(normed[cut, :], gate[...])
        up_act = contract_last(normed[cut, :], up[...])
        hidden = (gate_act / (1.0 + jnp.exp(-gate_act)) * up_act).astype(BF16)
        total[cut, :] += jnp.dot(hidden, down[...], preferred_element_type=F32)

    @pl.when(number == pl.num_programs(0) - 1)
    def _():
        rows = outs[0].shape[0]
        for index in range(sends):
            here = pl.ds(pl.multiple_of(targets[index] * rows, 16), rows)
            outs[index][...] = (total[here, :] * weight[here, 0:1]).astype(BF16)
        rows = own_rows.shape[0]
        here = pl.ds(pl.multiple_of(targets[sends] * rows, 16), rows)
        own_rows[...] = mixed[here, :]


def experts(places, targets, expert, gain, router, routes, gate, up, down, pieces, sends, rows, own):
    count = len(pieces)
    tokens = pieces[0].shape[0]
    hidden, width = gate.shape
    block = math.gcd(hidden, 512)
    whole = pl.BlockSpec(memory_space=VMEM)
    weights = pl.BlockSpec((block, width), lambda i: (i, 0))
    return pl.pallas_call(
        functools.partial(expert_kernel, count, sends),
        grid=(hidden // block,),
        out_shape=tuple([jax.ShapeDtypeStruct((rows, width), BF16)] * sends + [jax.ShapeDtypeStruct((own, width), BF16)]),
        in_specs=[pl.BlockSpec(memory_space=SMEM)] * 3 + [whole] * 3 + [weights] * 3 + [whole] * count,
        out_specs=tuple([whole] * (sends + 1)),
        scratch_shapes=[
            VMEM((tokens, width), BF16),
            VMEM((tokens, width), F32),
            VMEM((tokens, LANES), F32),
        ]
        + ([VMEM((tokens, width), BF16)] if count > 1 else []),
        compiler_params=pltpu.CompilerParams(vmem_limit_bytes=56 << 20),
        cost_estimate=pl.CostEstimate(
            flops=6 * tokens * hidden * width,
            bytes_accessed=6 * hidden * width,
            transcendentals=tokens * hidden,
        ),
        name="experts",
    )(places, targets, expert, gain, router, routes, gate, up, down, *pieces)


def body(
    projected,
    carried_tail,
    carried_state,
    filter_taps,
    filter_bias,
    select_weight,
    step_weight,
    step_bias,
    log_rate,
    skip_gain,
    output_weight,
    residual,
    norm_gain,
    router,
    gate_weight,
    up_weight,
    down_weight,
    routes,
):
    ctx, exp = lax.axis_size("ctx"), lax.axis_size("exp")
    ctx_at, exp_at = lax.axis_index("ctx"), lax.axis_index("exp")
    places = ring_places("ctx")
    x_input, z_input = projected[0], projected[1]
    own, width = residual.shape
    columns = output_weight.shape[1]

    x_pieces = spread(lambda k: x_input, "ctx", 0)
    extra = jnp.concatenate([residual, jnp.pad(routes.astype(BF16), ((0, 0), (0, LANES - 2)))], axis=1)
    if exp == 2:
        partner = rotate(extra, "exp", 1)
        extra = jnp.where(
            exp_at == 0,
            jnp.concatenate([extra, partner], axis=0),
            jnp.concatenate([partner, extra], axis=0),
        )
    else:
        extra = lax.all_gather(extra, "exp", axis=0, tiled=True)

    def bundle(k):
        piece = lax.dynamic_slice_in_dim(extra, k * columns, columns, axis=1)
        return jnp.concatenate([z_input, piece, extra[:, width:]], axis=1)

    z_pieces = spread(bundle, "ctx", 0)

    tail = jnp.pad(carried_tail.astype(F32), ((8 - carried_tail.shape[0], 0), (0, 0)))
    active, proj = activate(places, x_pieces, tail, filter_taps, filter_bias[None, :], select_weight)
    own_proj, other_proj = pair_sum(proj, "exp")
    base, sent, all_routes = scan(
        places,
        exp_at.astype(jnp.int32)[None],
        own_proj,
        other_proj,
        active,
        step_weight,
        step_bias[None, :],
        log_rate,
        skip_gain[None, :],
        carried_state,
        output_weight,
        z_pieces,
    )
    if exp == 2:
        mixed = (base + rotate(sent, "exp", 1).astype(F32)).astype(BF16)
    else:
        mixed = (base - sent.astype(F32) + lax.psum(sent.astype(F32), "exp")).astype(BF16)
    mixed_pieces = spread(lambda k: mixed, "ctx", 1)

    parts = ctx * exp
    me = ctx_at * exp + exp_at
    direct = parts <= 8
    sends = parts if direct else 1
    targets = [lax.rem(me + s, parts) for s in range(parts)] if direct else [jnp.int32(0)]
    targets = jnp.stack(targets + [me]).astype(jnp.int32)
    expert = (ctx_at // (ctx // EXPERTS)).astype(jnp.int32)[None]
    tokens = mixed_pieces[0].shape[0]
    results = experts(
        places,
        targets,
        expert,
        norm_gain[None, :],
        jnp.pad(router.T, ((0, 16 - EXPERTS), (0, 0))),
        all_routes,
        gate_weight,
        up_weight,
        down_weight,
        mixed_pieces,
        sends,
        own if direct else tokens,
        own,
    )
    outs, mine = results[:-1], results[-1]
    total = mine.astype(F32)
    axes = ("ctx", "exp")
    if direct:
        arrived = [outs[0]]
        for s in range(1, parts):
            arrived.append(lax.ppermute(outs[s], axes, [(i, (i + s) % parts) for i in range(parts)]))
        for piece in arrived:
            total = total + piece.astype(F32)
    else:
        moved = lax.all_to_all(outs[0], axes, split_axis=0, concat_axis=0, tiled=True)
        total = total + jnp.sum(moved.reshape(parts, own, width).astype(F32), axis=0)
    return total.astype(BF16)


def solution(mesh):
    placed = (
        P(None, ("doc", "ctx"), "exp"),
        P("doc", "exp"),
        P("doc", "exp"),
        P(None, "exp"),
        P("exp"),
        P(None, "exp"),
        P(None, "exp"),
        P("exp"),
        P(None, "exp"),
        P("exp"),
        P("exp", "ctx"),
        P(("doc", "ctx", "exp"), None),
        P(),
        P(),
        P(("ctx", "exp"), None),
        P(("ctx", "exp"), None),
        P(("ctx", "exp"), None),
        P(("doc", "ctx", "exp"), None),
    )
    return jax.shard_map(
        body, mesh=mesh, in_specs=placed, out_specs=P(("doc", "ctx", "exp"), None), check_vma=False
    )
```

```python
import functools
import math

import jax
import jax.numpy as jnp
from jax import lax
from jax.experimental import pallas as pl
from jax.experimental.pallas import tpu as pltpu
from jax.sharding import PartitionSpec as P

EXPERTS = 4
LANES = 128
FEW = 4
LOG2E = 1.4426950408889634
VMEM = pltpu.VMEM
SMEM = pltpu.SMEM
F32 = jnp.float32
BF16 = jnp.bfloat16


def contract_last(left, right):
    return lax.dot_general(left, right, (((1,), (1,)), ((), ())), preferred_element_type=F32)


def rotate(value, axis, steps):
    count = lax.axis_size(axis)
    return lax.ppermute(value, axis, [(i, (i + steps) % count) for i in range(count)])


def ring_places(axis):
    count = lax.axis_size(axis)
    if count > FEW:
        return jnp.zeros((1,), jnp.int32)
    me = lax.axis_index(axis)
    return jnp.stack([lax.rem(me + count - s, count) for s in range(count)]).astype(jnp.int32)


def spread(make, axis, join, after=None):
    count = lax.axis_size(axis)
    me = lax.axis_index(axis)
    if count <= FEW:
        sent = [make(lax.rem(me + s, count)) for s in range(1, count)]
        if after is not None:
            sent, _ = lax.optimization_barrier((sent, after))
        return [make(me)] + [rotate(sent[s - 1], axis, s) for s in range(1, count)]
    stacked = jnp.stack([make(jnp.int32(k)) for k in range(count)])
    moved = lax.all_to_all(stacked, axis, split_axis=0, concat_axis=0, tiled=True)
    return [jnp.concatenate([moved[k] for k in range(count)], axis=join)]


def swap(value):
    count = lax.axis_size("doc")
    return lax.ppermute(value, "doc", [(i, i + 1 - 2 * (i % 2)) for i in range(count)])


def far(value):
    return pltpu.with_memory_space_constraint(value, pltpu.HBM)


def pair_sum(value, axis):
    if lax.axis_size(axis) == 2:
        return [value, rotate(value, axis, 1)]
    total = lax.psum(value.astype(F32), axis).astype(value.dtype)
    return [total, jnp.zeros_like(total)]


FAR = pl.BlockSpec(memory_space=pltpu.HBM)
WHOLE = pl.BlockSpec(memory_space=VMEM)
SCALARS = pl.BlockSpec(memory_space=SMEM)


def activate_kernel(count, taps, places, params, select, *refs):
    pieces, (active, proj, padded, held, sem) = refs[:count], refs[count:]
    copy = pltpu.make_async_copy(select, held, sem)
    copy.start()
    rows = pieces[0].shape[0]
    padded[0:8, :] = params[8:16, :]
    for index in range(count):
        start = pl.multiple_of(8 + places[index] * rows, 8)
        padded[pl.ds(start, rows), :] = pieces[index][...].astype(F32)
    tokens = active.shape[0]
    step = 32

    def block(number, carry):
        base = pl.multiple_of(number * step, step)
        window = padded[pl.ds(base, step + 8), :]
        total = jnp.broadcast_to(params[taps : taps + 1, :], (step, params.shape[1]))
        for k in range(taps):
            offset = 8 - (taps - 1) + k
            total = total + params[k : k + 1, :] * window[offset : offset + step, :]
        value = total / (1.0 + jnp.exp(-total))
        active[pl.ds(base, step), :] = value.astype(BF16)
        return carry

    lax.fori_loop(0, tokens // step, block, 0)
    copy.wait()
    for number in range(tokens // LANES):
        cut = slice(number * LANES, (number + 1) * LANES)
        proj[:, cut] = contract_last(held[...], active[cut, :])


def activate(places, pieces, params, taps, select):
    count = len(pieces)
    tokens = count * pieces[0].shape[0]
    channels = pieces[0].shape[1]
    return pl.pallas_call(
        functools.partial(activate_kernel, count, taps),
        out_shape=(
            jax.ShapeDtypeStruct((tokens, channels), BF16),
            jax.ShapeDtypeStruct((select.shape[0], tokens), F32),
        ),
        in_specs=[SCALARS, WHOLE, FAR] + [WHOLE] * count,
        out_specs=(WHOLE,) * 2,
        scratch_shapes=[
            VMEM((tokens + 8, channels), F32),
            VMEM(select.shape, BF16),
            pltpu.SemaphoreType.DMA,
        ],
        compiler_params=pltpu.CompilerParams(vmem_limit_bytes=12 << 20),
        cost_estimate=pl.CostEstimate(
            flops=2 * tokens * channels * select.shape[0],
            bytes_accessed=4 * tokens * channels,
            transcendentals=tokens * channels,
        ),
        name="activate",
    )(places, params, far(select), *pieces)


def scan_kernel(
    taps, own, other, active, params, rates_in, step_weight_hbm, state_hbm, value_out,
    sums, steps, scaled, rates, state, coef, step_weight, state_in, sems,
):
    tokens, channels = active.shape
    rank = step_weight.shape[0]
    state_size = rates_in.shape[0]
    folds = channels // LANES
    group = min(folds, 16)
    load_weight = pltpu.make_async_copy(step_weight_hbm, step_weight, sems.at[0])
    load_state = pltpu.make_async_copy(state_hbm, state_in, sems.at[1])
    load_weight.start()
    load_state.start()
    sums[...] = own[...] + other[...]
    copy = pltpu.make_async_copy(sums.at[pl.ds(rank, 2 * state_size), :], coef, sems.at[2])
    copy.start()

    def scatter(target, source):
        for s8 in range(state_size // 8):
            for j in range(folds):
                lanes = slice(j * LANES, (j + 1) * LANES)
                there = slice((s8 * folds + j) * 8, (s8 * folds + j) * 8 + 8)
                target[there, :] = source[s8 * 8 : s8 * 8 + 8, lanes]

    def fold_rows(row, first):
        return pl.ds((row // 8) * (folds * 8) + row % 8 + first * 8, group, stride=8)

    scatter(state, rates_in)
    for s in range(state_size):
        for first in range(0, folds, group):
            rates[s * folds + first : s * folds + first + group, :] = state[fold_rows(s, first), :]
    load_state.wait()
    scatter(state, state_in)
    load_weight.wait()

    for number in range(tokens // LANES):
        cut = slice(number * LANES, (number + 1) * LANES)
        low = jnp.transpose(sums[0:rank, cut]).astype(BF16)
        width = min(channels, 256)
        for w in range(channels // width):
            lanes = slice(w * width, (w + 1) * width)
            raw = jnp.dot(low, step_weight[:, lanes], preferred_element_type=F32)
            raw = raw + params[taps + 1 : taps + 2, lanes]
            size = jnp.maximum(raw, 0.0) + jnp.log(1.0 + jnp.exp(-jnp.abs(raw)))
            times = size * active[cut, lanes].astype(F32)
            for i in range(LANES // 8):
                for j in range(width // LANES):
                    block = (number * LANES // 8 + i) * folds + w * (width // LANES) + j
                    there = slice(block * 8, block * 8 + 8)
                    part = (slice(i * 8, i * 8 + 8), slice(j * LANES, (j + 1) * LANES))
                    steps[there, :] = size[part]
                    scaled[there, :] = times[part]
    copy.wait()

    for first in range(0, folds, group):
        start = tuple(state[fold_rows(s, first), :] for s in range(state_size))

        def eight(number, held):
            base = number * (folds * 8) + first * 8
            held = list(held)
            for r in range(8):
                token = number * 8 + r
                rows = pl.ds(base + r, group, stride=8)
                size, times = steps[rows, :], scaled[rows, :]
                total = None
                for s in range(state_size):
                    rate = rates[s * folds + first : s * folds + first + group, :]
                    held[s] = jnp.exp2(size * rate) * held[s] + times * coef[s, token]
                    term = held[s] * coef[state_size + s, token]
                    total = term if total is None else total + term
                steps[rows, :] = total
            return tuple(held)

        lax.fori_loop(0, tokens // 8, eight, start)

    def unfold(number, carry):
        here = pl.ds(pl.multiple_of(number * 16, 16), 16)
        for j in range(folds):
            lanes = slice(j * LANES, (j + 1) * LANES)
            found = []
            for half in range(2):
                block = pl.multiple_of((number * 2 + half) * (folds * 8) + j * 8, 8)
                found.append(steps[pl.ds(block, 8), :])
            gain = params[taps + 2 : taps + 3, lanes]
            value_out[here, lanes] = jnp.concatenate(found, axis=0) + gain * active[here, lanes].astype(F32)
        return carry

    lax.fori_loop(0, tokens // 16, unfold, 0)


def scan(own, other, active, params, taps, rates, step_weight, state_in):
    tokens, channels = active.shape
    state_size = rates.shape[0]
    folded = (state_size * channels // LANES, LANES)
    return pl.pallas_call(
        functools.partial(scan_kernel, taps),
        out_shape=jax.ShapeDtypeStruct((tokens, channels), F32),
        in_specs=[WHOLE] * 5 + [FAR] * 2,
        out_specs=WHOLE,
        scratch_shapes=[
            VMEM(own.shape, F32),
            VMEM((tokens * channels // LANES, LANES), F32),
            VMEM((tokens * channels // LANES, LANES), F32),
            VMEM(folded, F32),
            VMEM(folded, F32),
            SMEM((2 * state_size, tokens), F32),
            VMEM(step_weight.shape, BF16),
            VMEM(state_in.shape, F32),
            pltpu.SemaphoreType.DMA((3,)),
        ],
        compiler_params=pltpu.CompilerParams(vmem_limit_bytes=16 << 20),
        cost_estimate=pl.CostEstimate(
            flops=8 * tokens * channels * state_size,
            bytes_accessed=8 * tokens * channels,
            transcendentals=tokens * channels * state_size,
        ),
        name="scan",
    )(own, other, active, params, rates, far(step_weight), far(state_in))


def project_kernel(count, columns, places, value_in, weight_hbm, *refs):
    pieces = refs[:count]
    base_out, send_out, routes_out, gated, out_weight, sem = refs[count:]
    copy = pltpu.make_async_copy(weight_hbm, out_weight, sem)
    copy.start()
    tokens, channels = value_in.shape
    rows = pieces[0].shape[0]
    tile = 16
    for index in range(count):
        begin = pl.multiple_of(places[index] * rows, tile)
        routes_out[pl.ds(begin, rows), :] = pieces[index][:, channels + columns :]

        def gate(number, carry):
            local = pl.ds(pl.multiple_of(number * tile, tile), tile)
            here = pl.ds(pl.multiple_of(begin + number * tile, tile), tile)
            z = pieces[index][local, :channels].astype(F32)
            gated[here, :] = (value_in[here, :] * (z / (1.0 + jnp.exp(-z)))).astype(BF16)
            return carry

        lax.fori_loop(0, rows // tile, gate, 0)
    copy.wait()
    for number in range(tokens // LANES):
        cut = slice(number * LANES, (number + 1) * LANES)
        sent = jnp.dot(gated[cut, :], out_weight[...], preferred_element_type=F32).astype(BF16)
        send_out[cut, :] = sent
        base_out[cut, :] = sent.astype(F32)
    for index in range(count):
        here = pl.ds(pl.multiple_of(places[index] * rows, tile), rows)
        base_out[here, :] += pieces[index][:, channels : channels + columns].astype(F32)


def project(places, value, out_weight, pieces):
    tokens, channels = value.shape
    columns = out_weight.shape[1]
    count = len(pieces)
    return pl.pallas_call(
        functools.partial(project_kernel, count, columns),
        out_shape=(
            jax.ShapeDtypeStruct((tokens, columns), F32),
            jax.ShapeDtypeStruct((tokens, columns), BF16),
            jax.ShapeDtypeStruct((tokens, LANES), BF16),
        ),
        in_specs=[SCALARS, WHOLE, FAR] + [WHOLE] * count,
        out_specs=(WHOLE,) * 3,
        scratch_shapes=[
            VMEM((tokens, channels), BF16),
            VMEM(out_weight.shape, BF16),
            pltpu.SemaphoreType.DMA,
        ],
        compiler_params=pltpu.CompilerParams(vmem_limit_bytes=16 << 20),
        cost_estimate=pl.CostEstimate(
            flops=2 * tokens * channels * columns,
            bytes_accessed=8 * tokens * channels,
            transcendentals=tokens * channels,
        ),
        name="project",
    )(places, value, far(out_weight), *pieces)


def norm_kernel(count, places, spots, gain, router, routes, *refs):
    pieces = refs[:count]
    normed, weight, own_rows = refs[count : count + 3]
    mixed = pieces[0] if count == 1 else refs[-1]
    tokens = normed.shape[0]
    columns = pieces[0].shape[1]
    for index in range(count if count > 1 else 0):
        start = pl.multiple_of(places[index] * columns, LANES)
        mixed[:, pl.ds(start, columns)] = pieces[index][...]
    mine = spots[0].astype(F32)
    step = 32

    def block(number, carry):
        cut = pl.ds(pl.multiple_of(number * step, step), step)
        value = mixed[cut, :].astype(F32)
        square = jnp.mean(value * value, axis=-1, keepdims=True) + 1e-06
        scaled = (value * lax.rsqrt(square) * gain[0:1, :]).astype(BF16)
        normed[cut, :] = scaled
        return carry

    lax.fori_loop(0, tokens // step, block, 0)
    for c in range(tokens // LANES):
        cut = slice(c * LANES, (c + 1) * LANES)
        logits = contract_last(normed[cut, :], router[...])
        first = routes[cut, 0:1].astype(F32)
        second = routes[cut, 1:2].astype(F32)
        ids = lax.broadcasted_iota(jnp.int32, logits.shape, 1).astype(F32)
        first_logit = jnp.sum(jnp.where(ids == first, logits, 0.0), axis=1, keepdims=True)
        second_logit = jnp.sum(jnp.where(ids == second, logits, 0.0), axis=1, keepdims=True)
        first_gate = jnp.where(first == mine, 1.0 / (1.0 + jnp.exp(second_logit - first_logit)), 0.0)
        second_gate = jnp.where(second == mine, 1.0 / (1.0 + jnp.exp(first_logit - second_logit)), 0.0)
        weight[cut, :] = jnp.broadcast_to(first_gate + second_gate, (LANES, LANES))
    rows = own_rows.shape[0]
    own_rows[...] = mixed[pl.ds(pl.multiple_of(spots[1] * rows, 16), rows), :]


def norm(places, spots, gain, router, routes, pieces, own):
    count = len(pieces)
    tokens = pieces[0].shape[0]
    width = count * pieces[0].shape[1]
    return pl.pallas_call(
        functools.partial(norm_kernel, count),
        out_shape=(
            jax.ShapeDtypeStruct((tokens, width), BF16),
            jax.ShapeDtypeStruct((tokens, LANES), F32),
            jax.ShapeDtypeStruct((own, width), BF16),
        ),
        in_specs=[SCALARS] * 2 + [WHOLE] * (3 + count),
        out_specs=(WHOLE,) * 3,
        scratch_shapes=[VMEM((tokens, width), BF16)] if count > 1 else [],
        compiler_params=pltpu.CompilerParams(vmem_limit_bytes=8 << 20),
        name="norm",
    )(places, spots, gain, router, routes, *pieces)


def expert_kernel(groups, half, *refs):
    tokens = refs[:groups]
    gate, up, down = refs[groups : groups + 3]
    outs = refs[groups + 3 : 2 * groups + 3]
    totals = (outs[0],) + refs[2 * groups + 3 :]
    number = pl.program_id(0)

    @pl.when(number == 0)
    def _():
        for total in totals:
            total[...] = jnp.zeros_like(total)

    rows = totals[0].shape[0]
    if groups == 2 and rows == LANES:
        work = [(totals, slice(0, rows))]
    else:
        work = [((t,), slice(c, c + LANES)) for t in totals for c in range(0, rows, LANES)]
    for index, (into, cut) in enumerate(work):
        if len(into) == 2:
            value = jnp.concatenate([tokens[0][...], tokens[1][...]], axis=0)
        else:
            value = tokens[totals.index(into[0])][cut, :]
        gate_act = contract_last(value, gate[...])
        up_act = contract_last(value, up[...])
        hidden = (gate_act / (1.0 + jnp.exp(-gate_act)) * up_act).astype(BF16)
        product = jnp.dot(hidden, down[...], preferred_element_type=F32)
        for place, total in enumerate(into):
            total[cut, :] += product[place * LANES : (place + 1) * LANES, :]

    if groups == 2:

        @pl.when(number == pl.num_programs(0) - 1)
        def _():
            outs[1][...] = totals[1][...].astype(BF16)


def experts(half, tokens, gate, up, down):
    groups = len(tokens)
    rows, width = tokens[0].shape
    hidden = gate.shape[0] // groups
    block = hidden if hidden <= 512 else math.gcd(hidden, 512)
    steps = hidden // block
    weights = pl.BlockSpec((block, width), lambda i, half: (half[0] * steps + i, 0))
    shapes = [jax.ShapeDtypeStruct((rows, width), F32), jax.ShapeDtypeStruct((rows, width), BF16)]
    return pl.pallas_call(
        functools.partial(expert_kernel, groups),
        out_shape=tuple(shapes[:groups]),
        grid_spec=pltpu.PrefetchScalarGridSpec(
            num_scalar_prefetch=1,
            grid=(steps,),
            in_specs=[WHOLE] * groups + [weights] * 3,
            out_specs=(WHOLE,) * groups,
            scratch_shapes=[VMEM((rows, width), F32)] * (groups - 1),
        ),
        compiler_params=pltpu.CompilerParams(vmem_limit_bytes=40 << 20),
        cost_estimate=pl.CostEstimate(
            flops=6 * groups * rows * hidden * width,
            bytes_accessed=6 * hidden * width,
            transcendentals=rows * hidden,
        ),
        name="experts",
    )(half, *tokens, gate, up, down)


def combine_kernel(targets, own, other, weight, *outs):
    rows = outs[0].shape[0]
    for index, out in enumerate(outs):
        here = pl.ds(pl.multiple_of(targets[index] * rows, 16), rows)
        out[...] = ((own[here, :] + other[here, :].astype(F32)) * weight[here, 0:1]).astype(BF16)


def combine(targets, own, other, weight, rows):
    width = own.shape[1]
    sends = own.shape[0] // rows
    return pl.pallas_call(
        combine_kernel,
        out_shape=tuple([jax.ShapeDtypeStruct((rows, width), BF16)] * sends),
        in_specs=[SCALARS] + [WHOLE] * 3,
        out_specs=(WHOLE,) * sends,
        compiler_params=pltpu.CompilerParams(vmem_limit_bytes=8 << 20),
        name="combine",
    )(targets, own, other, weight)


def body(
    projected,
    carried_tail,
    carried_state,
    filter_taps,
    filter_bias,
    select_weight,
    step_weight,
    step_bias,
    log_rate,
    skip_gain,
    output_weight,
    residual,
    norm_gain,
    router,
    gate_weight,
    up_weight,
    down_weight,
    routes,
):
    ctx, exp = lax.axis_size("ctx"), lax.axis_size("exp")
    ctx_at, exp_at = lax.axis_index("ctx"), lax.axis_index("exp")
    places = ring_places("ctx")
    x_input, z_input = projected[0], projected[1]
    own, width = residual.shape
    columns = output_weight.shape[1]
    taps = filter_taps.shape[0]

    x_pieces = spread(lambda k: x_input, "ctx", 0)
    extra = jnp.concatenate([residual, jnp.pad(routes.astype(BF16), ((0, 0), (0, LANES - 2)))], axis=1)
    if exp == 2:
        partner = rotate(extra, "exp", 1)
        extra = jnp.where(
            exp_at == 0,
            jnp.concatenate([extra, partner], axis=0),
            jnp.concatenate([partner, extra], axis=0),
        )
    else:
        extra = lax.all_gather(extra, "exp", axis=0, tiled=True)
    tail_pad = jnp.zeros((8 - carried_tail.shape[0], carried_tail.shape[1]), F32)
    params = jnp.concatenate(
        [filter_taps, filter_bias[None], step_bias[None], skip_gain[None], jnp.zeros_like(tail_pad)[: 5 - taps],
         tail_pad, carried_tail.astype(F32)]
    )
    rates = jnp.exp(log_rate) * (-LOG2E)
    ready = [jnp.concatenate([z_input, extra[:, width:]], axis=1), extra[:, :width]]
    router_rows = jnp.pad(router.T, ((0, 16 - EXPERTS), (0, 0)))
    gain = jnp.pad(norm_gain[None, :], ((0, 7), (0, 0)))
    params, rates, router_rows, gain = lax.optimization_barrier((params, rates, router_rows, gain))

    active, proj = activate(places, x_pieces, params, taps, select_weight)
    own_proj, other_proj = pair_sum(proj, "exp")

    def bundle(k):
        piece = lax.dynamic_slice_in_dim(ready[1], k * columns, columns, axis=1)
        channels = z_input.shape[1]
        return jnp.concatenate([ready[0][:, :channels], piece, ready[0][:, channels:]], axis=1)

    z_pieces = spread(bundle, "ctx", 0, x_pieces[min(1, len(x_pieces) - 1)])
    value = scan(own_proj, other_proj, active, params, taps, rates, step_weight, carried_state)
    base, sent, all_routes = project(places, value, output_weight, z_pieces)
    if exp == 2:
        mixed = (base + rotate(sent, "exp", 1).astype(F32)).astype(BF16)
    else:
        mixed = (base - sent.astype(F32) + lax.psum(sent.astype(F32), "exp")).astype(BF16)
    mixed_pieces = spread(lambda k: mixed, "ctx", 1)

    parts = ctx * exp
    me = ctx_at * exp + exp_at
    spots = jnp.stack([ctx_at // (ctx // EXPERTS), me]).astype(jnp.int32)
    normed, weight, mine = norm(places, spots, gain, router_rows, all_routes, mixed_pieces, own)
    total = mine.astype(F32)
    axes = ("ctx", "exp")
    if parts <= 8 and normed.shape[0] == LANES and lax.axis_size("doc") % 2 == 0:
        half = lax.rem(lax.axis_index("doc"), 2).astype(jnp.int32)[None]
        kept, given = experts(half, [normed, swap(normed)], gate_weight, up_weight, down_weight)
        targets = jnp.stack([lax.rem(me + s, parts) for s in range(parts)]).astype(jnp.int32)
        outs = combine(targets, kept, swap(given), weight, own)
        arrived = [outs[0]]
        for s in range(1, parts):
            arrived.append(lax.ppermute(outs[s], axes, [(i, (i + s) % parts) for i in range(parts)]))
        for piece in arrived:
            total = total + piece.astype(F32)
    else:
        (kept,) = experts(jnp.zeros((1,), jnp.int32), [normed], gate_weight, up_weight, down_weight)
        partial = (kept * weight[:, :1]).astype(BF16)
        moved = lax.all_to_all(partial, axes, split_axis=0, concat_axis=0, tiled=True)
        total = total + jnp.sum(moved.reshape(parts, own, width).astype(F32), axis=0)
    return total.astype(BF16)


def solution(mesh):
    placed = (
        P(None, ("doc", "ctx"), "exp"),
        P("doc", "exp"),
        P("doc", "exp"),
        P(None, "exp"),
        P("exp"),
        P(None, "exp"),
        P(None, "exp"),
        P("exp"),
        P(None, "exp"),
        P("exp"),
        P("exp", "ctx"),
        P(("doc", "ctx", "exp"), None),
        P(),
        P(),
        P(("ctx", "exp"), None),
        P(("ctx", "exp"), None),
        P(("ctx", "exp"), None),
        P(("doc", "ctx", "exp"), None),
    )
    return jax.shard_map(
        body, mesh=mesh, in_specs=placed, out_specs=P(("doc", "ctx", "exp"), None), check_vma=False
    )
```

```python
import functools
import math

import jax
import jax.numpy as jnp
from jax import lax
from jax.experimental import pallas as pl
from jax.experimental.pallas import tpu as pltpu
from jax.sharding import PartitionSpec as P

EXPERTS = 4
LANES = 128
FEW = 4
LOG2E = 1.4426950408889634
VMEM = pltpu.VMEM
SMEM = pltpu.SMEM
F32 = jnp.float32
BF16 = jnp.bfloat16


def contract_last(left, right):
    return lax.dot_general(left, right, (((1,), (1,)), ((), ())), preferred_element_type=F32)


def rotate(value, axis, steps):
    count = lax.axis_size(axis)
    return lax.ppermute(value, axis, [(i, (i + steps) % count) for i in range(count)])


def ring_places(axis):
    count = lax.axis_size(axis)
    if count > FEW:
        return jnp.zeros((1,), jnp.int32)
    me = lax.axis_index(axis)
    return jnp.stack([lax.rem(me + count - s, count) for s in range(count)]).astype(jnp.int32)


def spread(make, axis, join, after=None):
    count = lax.axis_size(axis)
    me = lax.axis_index(axis)
    if count <= FEW:
        sent = [make(lax.rem(me + s, count)) for s in range(1, count)]
        if after is not None:
            sent, _ = lax.optimization_barrier((sent, after))
        return [make(me)] + [rotate(sent[s - 1], axis, s) for s in range(1, count)]
    stacked = jnp.stack([make(jnp.int32(k)) for k in range(count)])
    moved = lax.all_to_all(stacked, axis, split_axis=0, concat_axis=0, tiled=True)
    return [jnp.concatenate([moved[k] for k in range(count)], axis=join)]


def swap(value):
    count = lax.axis_size("doc")
    return lax.ppermute(value, "doc", [(i, i + 1 - 2 * (i % 2)) for i in range(count)])


def far(value):
    return pltpu.with_memory_space_constraint(value, pltpu.HBM)


def pair_sum(value, axis):
    if lax.axis_size(axis) == 2:
        return [value, rotate(value, axis, 1)]
    total = lax.psum(value.astype(F32), axis).astype(value.dtype)
    return [total, jnp.zeros_like(total)]


FAR = pl.BlockSpec(memory_space=pltpu.HBM)
WHOLE = pl.BlockSpec(memory_space=VMEM)
SCALARS = pl.BlockSpec(memory_space=SMEM)


def activate_kernel(count, taps, places, params, select, *refs):
    pieces, (active, proj, padded, held, sem) = refs[:count], refs[count:]
    copy = pltpu.make_async_copy(select, held, sem)
    copy.start()
    rows = pieces[0].shape[0]
    padded[0:8, :] = params[8:16, :]
    for index in range(count):
        start = pl.multiple_of(8 + places[index] * rows, 8)
        padded[pl.ds(start, rows), :] = pieces[index][...].astype(F32)
    tokens = active.shape[0]
    step = 32

    def block(number, carry):
        base = pl.multiple_of(number * step, step)
        window = padded[pl.ds(base, step + 8), :]
        total = jnp.broadcast_to(params[taps : taps + 1, :], (step, params.shape[1]))
        for k in range(taps):
            offset = 8 - (taps - 1) + k
            total = total + params[k : k + 1, :] * window[offset : offset + step, :]
        value = total / (1.0 + jnp.exp(-total))
        active[pl.ds(base, step), :] = value.astype(BF16)
        return carry

    lax.fori_loop(0, tokens // step, block, 0)
    copy.wait()
    for number in range(tokens // LANES):
        cut = slice(number * LANES, (number + 1) * LANES)
        proj[:, cut] = contract_last(held[...], active[cut, :])


def activate(places, pieces, params, taps, select):
    count = len(pieces)
    tokens = count * pieces[0].shape[0]
    channels = pieces[0].shape[1]
    return pl.pallas_call(
        functools.partial(activate_kernel, count, taps),
        out_shape=(
            jax.ShapeDtypeStruct((tokens, channels), BF16),
            jax.ShapeDtypeStruct((select.shape[0], tokens), F32),
        ),
        in_specs=[SCALARS, WHOLE, FAR] + [WHOLE] * count,
        out_specs=(WHOLE,) * 2,
        scratch_shapes=[
            VMEM((tokens + 8, channels), F32),
            VMEM(select.shape, BF16),
            pltpu.SemaphoreType.DMA,
        ],
        compiler_params=pltpu.CompilerParams(vmem_limit_bytes=12 << 20),
        cost_estimate=pl.CostEstimate(
            flops=2 * tokens * channels * select.shape[0],
            bytes_accessed=4 * tokens * channels,
            transcendentals=tokens * channels,
        ),
        name="activate",
    )(places, params, far(select), *pieces)


def scan_kernel(
    taps, own, other, active, params, log_rate_hbm, step_weight_hbm, state_hbm, value_out,
    sums, steps, scaled, rates, state, coef, step_weight, state_in, log_rate, sems,
):
    tokens, channels = active.shape
    rank = step_weight.shape[0]
    state_size = log_rate.shape[0]
    folds = channels // LANES
    group = min(folds, 16)
    load_weight = pltpu.make_async_copy(step_weight_hbm, step_weight, sems.at[0])
    load_state = pltpu.make_async_copy(state_hbm, state_in, sems.at[1])
    load_rate = pltpu.make_async_copy(log_rate_hbm, log_rate, sems.at[3])
    load_rate.start()
    load_state.start()
    load_weight.start()
    sums[...] = own[...] + other[...]
    copy = pltpu.make_async_copy(sums.at[pl.ds(rank, 2 * state_size), :], coef, sems.at[2])
    copy.start()

    def scatter(target, source):
        for s8 in range(state_size // 8):
            for j in range(folds):
                lanes = slice(j * LANES, (j + 1) * LANES)
                there = slice((s8 * folds + j) * 8, (s8 * folds + j) * 8 + 8)
                target[there, :] = source[s8 * 8 : s8 * 8 + 8, lanes]

    def fold_rows(row, first):
        return pl.ds((row // 8) * (folds * 8) + row % 8 + first * 8, group, stride=8)

    load_rate.wait()
    scatter(state, log_rate)
    for s in range(state_size):
        for first in range(0, folds, group):
            rates[s * folds + first : s * folds + first + group, :] = (
                jnp.exp(state[fold_rows(s, first), :]) * (-LOG2E)
            )
    load_state.wait()
    scatter(state, state_in)
    load_weight.wait()

    for number in range(tokens // LANES):
        cut = slice(number * LANES, (number + 1) * LANES)
        low = jnp.transpose(sums[0:rank, cut]).astype(BF16)
        width = min(channels, 256)
        for w in range(channels // width):
            lanes = slice(w * width, (w + 1) * width)
            raw = jnp.dot(low, step_weight[:, lanes], preferred_element_type=F32)
            raw = raw + params[taps + 1 : taps + 2, lanes]
            size = jnp.maximum(raw, 0.0) + jnp.log(1.0 + jnp.exp(-jnp.abs(raw)))
            times = size * active[cut, lanes].astype(F32)
            for i in range(LANES // 8):
                for j in range(width // LANES):
                    block = (number * LANES // 8 + i) * folds + w * (width // LANES) + j
                    there = slice(block * 8, block * 8 + 8)
                    part = (slice(i * 8, i * 8 + 8), slice(j * LANES, (j + 1) * LANES))
                    steps[there, :] = size[part]
                    scaled[there, :] = times[part]
    copy.wait()

    for first in range(0, folds, group):
        start = tuple(state[fold_rows(s, first), :] for s in range(state_size))

        def eight(number, held):
            base = number * (folds * 8) + first * 8
            held = list(held)
            for r in range(8):
                token = number * 8 + r
                rows = pl.ds(base + r, group, stride=8)
                size, times = steps[rows, :], scaled[rows, :]
                total = None
                for s in range(state_size):
                    rate = rates[s * folds + first : s * folds + first + group, :]
                    held[s] = jnp.exp2(size * rate) * held[s] + times * coef[s, token]
                    term = held[s] * coef[state_size + s, token]
                    total = term if total is None else total + term
                steps[rows, :] = total
            return tuple(held)

        lax.fori_loop(0, tokens // 8, eight, start)

    def unfold(number, carry):
        here = pl.ds(pl.multiple_of(number * 16, 16), 16)
        for j in range(folds):
            lanes = slice(j * LANES, (j + 1) * LANES)
            found = []
            for half in range(2):
                block = pl.multiple_of((number * 2 + half) * (folds * 8) + j * 8, 8)
                found.append(steps[pl.ds(block, 8), :])
            gain = params[taps + 2 : taps + 3, lanes]
            value_out[here, lanes] = jnp.concatenate(found, axis=0) + gain * active[here, lanes].astype(F32)
        return carry

    lax.fori_loop(0, tokens // 16, unfold, 0)


def scan(own, other, active, params, taps, log_rate, step_weight, state_in):
    tokens, channels = active.shape
    state_size = log_rate.shape[0]
    folded = (state_size * channels // LANES, LANES)
    return pl.pallas_call(
        functools.partial(scan_kernel, taps),
        out_shape=jax.ShapeDtypeStruct((tokens, channels), F32),
        in_specs=[WHOLE] * 4 + [FAR] * 3,
        out_specs=WHOLE,
        scratch_shapes=[
            VMEM(own.shape, F32),
            VMEM((tokens * channels // LANES, LANES), F32),
            VMEM((tokens * channels // LANES, LANES), F32),
            VMEM(folded, F32),
            VMEM(folded, F32),
            SMEM((2 * state_size, tokens), F32),
            VMEM(step_weight.shape, BF16),
            VMEM(state_in.shape, F32),
            VMEM(log_rate.shape, F32),
            pltpu.SemaphoreType.DMA((4,)),
        ],
        compiler_params=pltpu.CompilerParams(vmem_limit_bytes=16 << 20),
        cost_estimate=pl.CostEstimate(
            flops=3000 * tokens * channels * state_size,
            bytes_accessed=8 * tokens * channels,
            transcendentals=tokens * channels * state_size,
        ),
        name="scan",
    )(own, other, active, params, far(log_rate), far(step_weight), far(state_in))


def project_kernel(count, columns, places, value_in, weight_hbm, *refs):
    pieces = refs[:count]
    base_out, send_out, routes_out, gated, out_weight, sem = refs[count:]
    copy = pltpu.make_async_copy(weight_hbm, out_weight, sem)
    copy.start()
    tokens, channels = value_in.shape
    rows = pieces[0].shape[0]
    tile = 16
    for index in range(count):
        begin = pl.multiple_of(places[index] * rows, tile)
        routes_out[pl.ds(begin, rows), :] = pieces[index][:, channels + columns :]

        def gate(number, carry):
            local = pl.ds(pl.multiple_of(number * tile, tile), tile)
            here = pl.ds(pl.multiple_of(begin + number * tile, tile), tile)
            z = pieces[index][local, :channels].astype(F32)
            gated[here, :] = (value_in[here, :] * (z / (1.0 + jnp.exp(-z)))).astype(BF16)
            return carry

        lax.fori_loop(0, rows // tile, gate, 0)
    copy.wait()
    for number in range(tokens // LANES):
        cut = slice(number * LANES, (number + 1) * LANES)
        sent = jnp.dot(gated[cut, :], out_weight[...], preferred_element_type=F32).astype(BF16)
        send_out[cut, :] = sent
        base_out[cut, :] = sent.astype(F32)
    for index in range(count):
        here = pl.ds(pl.multiple_of(places[index] * rows, tile), rows)
        base_out[here, :] += pieces[index][:, channels : channels + columns].astype(F32)


def project(places, value, out_weight, pieces):
    tokens, channels = value.shape
    columns = out_weight.shape[1]
    count = len(pieces)
    return pl.pallas_call(
        functools.partial(project_kernel, count, columns),
        out_shape=(
            jax.ShapeDtypeStruct((tokens, columns), F32),
            jax.ShapeDtypeStruct((tokens, columns), BF16),
            jax.ShapeDtypeStruct((tokens, LANES), BF16),
        ),
        in_specs=[SCALARS, WHOLE, FAR] + [WHOLE] * count,
        out_specs=(WHOLE,) * 3,
        scratch_shapes=[
            VMEM((tokens, channels), BF16),
            VMEM(out_weight.shape, BF16),
            pltpu.SemaphoreType.DMA,
        ],
        compiler_params=pltpu.CompilerParams(vmem_limit_bytes=16 << 20),
        cost_estimate=pl.CostEstimate(
            flops=2 * tokens * channels * columns,
            bytes_accessed=8 * tokens * channels,
            transcendentals=tokens * channels,
        ),
        name="project",
    )(places, value, far(out_weight), *pieces)


def norm_kernel(count, places, spots, gain, router, routes, *refs):
    pieces = refs[:count]
    normed, weight, own_rows = refs[count : count + 3]
    mixed = pieces[0] if count == 1 else refs[-1]
    tokens = normed.shape[0]
    columns = pieces[0].shape[1]
    for index in range(count if count > 1 else 0):
        start = pl.multiple_of(places[index] * columns, LANES)
        mixed[:, pl.ds(start, columns)] = pieces[index][...]
    mine = spots[0].astype(F32)
    step = 32

    def block(number, carry):
        cut = pl.ds(pl.multiple_of(number * step, step), step)
        value = mixed[cut, :].astype(F32)
        square = jnp.mean(value * value, axis=-1, keepdims=True) + 1e-06
        scaled = (value * lax.rsqrt(square) * gain[0:1, :]).astype(BF16)
        normed[cut, :] = scaled
        return carry

    lax.fori_loop(0, tokens // step, block, 0)
    for c in range(tokens // LANES):
        cut = slice(c * LANES, (c + 1) * LANES)
        logits = contract_last(normed[cut, :], router[...])
        first = routes[cut, 0:1].astype(F32)
        second = routes[cut, 1:2].astype(F32)
        ids = lax.broadcasted_iota(jnp.int32, logits.shape, 1).astype(F32)
        first_logit = jnp.sum(jnp.where(ids == first, logits, 0.0), axis=1, keepdims=True)
        second_logit = jnp.sum(jnp.where(ids == second, logits, 0.0), axis=1, keepdims=True)
        first_gate = jnp.where(first == mine, 1.0 / (1.0 + jnp.exp(second_logit - first_logit)), 0.0)
        second_gate = jnp.where(second == mine, 1.0 / (1.0 + jnp.exp(first_logit - second_logit)), 0.0)
        weight[cut, :] = jnp.broadcast_to(first_gate + second_gate, (LANES, LANES))
    rows = own_rows.shape[0]
    own_rows[...] = mixed[pl.ds(pl.multiple_of(spots[1] * rows, 16), rows), :]


def norm(places, spots, gain, router, routes, pieces, own):
    count = len(pieces)
    tokens = pieces[0].shape[0]
    width = count * pieces[0].shape[1]
    return pl.pallas_call(
        functools.partial(norm_kernel, count),
        out_shape=(
            jax.ShapeDtypeStruct((tokens, width), BF16),
            jax.ShapeDtypeStruct((tokens, LANES), F32),
            jax.ShapeDtypeStruct((own, width), BF16),
        ),
        in_specs=[SCALARS] * 2 + [WHOLE] * (3 + count),
        out_specs=(WHOLE,) * 3,
        scratch_shapes=[VMEM((tokens, width), BF16)] if count > 1 else [],
        compiler_params=pltpu.CompilerParams(vmem_limit_bytes=8 << 20),
        name="norm",
    )(places, spots, gain, router, routes, *pieces)


def fetch_kernel(parts, half, *refs):
    count = len(refs) // 2 - 1
    sources, targets, done, sems = refs[:count], refs[count : 2 * count], refs[-2], refs[-1]
    rows = targets[0].shape[0]
    part = rows // parts
    copies = []
    for index in range(count):
        for k in range(parts):
            start = pl.multiple_of(half[0] * rows + k * part, 16)
            copies.append(
                pltpu.make_async_copy(
                    sources[index].at[pl.ds(start, part), :],
                    targets[index].at[pl.ds(k * part, part), :],
                    sems.at[index * parts + k],
                )
            )
    for copy in copies:
        copy.start()
    for copy in copies:
        copy.wait()
    done[0] = half[0]


def fetch(half, weights):
    rows, width = weights[0].shape[0] // 2, weights[0].shape[1]
    parts = 4
    return pl.pallas_call(
        functools.partial(fetch_kernel, parts),
        out_shape=tuple([VMEM((rows, width), BF16)] * len(weights)) + (jax.ShapeDtypeStruct((1,), jnp.int32),),
        in_specs=[SCALARS] + [FAR] * len(weights),
        out_specs=tuple([WHOLE] * len(weights)) + (SCALARS,),
        scratch_shapes=[pltpu.SemaphoreType.DMA((parts * len(weights),))],
        compiler_params=pltpu.CompilerParams(vmem_limit_bytes=1 << 20),
        cost_estimate=pl.CostEstimate(
            flops=0, bytes_accessed=4 * rows * width * len(weights), transcendentals=0
        ),
        name="fetch",
    )(half, *[far(w) for w in weights])


def shared_kernel(steps, block, half, own, other, gate, up, down, kept, given, tokens, hidden):
    number = pl.program_id(0)
    rows = own.shape[0]

    @pl.when(number == 0)
    def _():
        tokens[0:rows, :] = own[...]
        tokens[rows:, :] = other[...]

    @pl.when(number < steps)
    def _():
        here = pl.ds(pl.multiple_of(number * block, block), block)
        gate_act = contract_last(tokens[...], gate[here, :])
        up_act = contract_last(tokens[...], up[here, :])
        value = gate_act / (1.0 + jnp.exp(-gate_act)) * up_act
        hidden[:, here] = value.astype(BF16)

    @pl.when(number >= steps)
    def _():
        width = down.shape[1]
        here = pl.ds(pl.multiple_of((number - steps) * width, width), width)
        product = jnp.dot(hidden[...], down[...], preferred_element_type=F32)
        kept[:, here] = product[0:rows, :]
        given[:, here] = product[rows:, :].astype(BF16)


def shared_experts(half, own, other, gate, up, down):
    rows, width = own.shape
    depth = gate.shape[0]
    block = math.gcd(depth, 512)
    steps = depth // block
    columns = 256
    return pl.pallas_call(
        functools.partial(shared_kernel, steps, block),
        out_shape=(jax.ShapeDtypeStruct((rows, width), F32), jax.ShapeDtypeStruct((rows, width), BF16)),
        grid_spec=pltpu.PrefetchScalarGridSpec(
            num_scalar_prefetch=1,
            grid=(steps + width // columns,),
            in_specs=[WHOLE] * 4
            + [pl.BlockSpec((depth, columns), lambda i, half: (half[0], jnp.maximum(i - steps, 0)))],
            out_specs=(WHOLE,) * 2,
            scratch_shapes=[VMEM((2 * rows, width), BF16), VMEM((2 * rows, depth), BF16)],
        ),
        compiler_params=pltpu.CompilerParams(vmem_limit_bytes=16 << 20),
        cost_estimate=pl.CostEstimate(
            flops=12 * rows * depth * width,
            bytes_accessed=6 * depth * width,
            transcendentals=2 * rows * depth,
        ),
        name="experts",
    )(half, own, other, gate, up, far(down))


def expert_kernel(tokens, gate, up, down, total):
    number = pl.program_id(0)

    @pl.when(number == 0)
    def _():
        total[...] = jnp.zeros_like(total)

    for start in range(0, total.shape[0], LANES):
        cut = slice(start, start + LANES)
        gate_act = contract_last(tokens[cut, :], gate[...])
        up_act = contract_last(tokens[cut, :], up[...])
        hidden = (gate_act / (1.0 + jnp.exp(-gate_act)) * up_act).astype(BF16)
        total[cut, :] += jnp.dot(hidden, down[...], preferred_element_type=F32)


def experts(tokens, gate, up, down):
    rows, width = tokens.shape
    hidden = gate.shape[0]
    block = hidden if hidden <= 512 else math.gcd(hidden, 512)
    weights = pl.BlockSpec((block, width), lambda i: (i, 0))
    return pl.pallas_call(
        expert_kernel,
        grid=(hidden // block,),
        out_shape=jax.ShapeDtypeStruct((rows, width), F32),
        in_specs=[WHOLE] + [weights] * 3,
        out_specs=WHOLE,
        compiler_params=pltpu.CompilerParams(vmem_limit_bytes=40 << 20),
        cost_estimate=pl.CostEstimate(
            flops=6 * rows * hidden * width,
            bytes_accessed=6 * hidden * width,
            transcendentals=rows * hidden,
        ),
        name="experts",
    )(tokens, gate, up, down)


def combine_kernel(targets, own, other, weight, *outs):
    rows = outs[0].shape[0]
    for index, out in enumerate(outs):
        here = pl.ds(pl.multiple_of(targets[index] * rows, 16), rows)
        out[...] = ((own[here, :] + other[here, :].astype(F32)) * weight[here, 0:1]).astype(BF16)


def combine(targets, own, other, weight, rows):
    width = own.shape[1]
    sends = own.shape[0] // rows
    return pl.pallas_call(
        combine_kernel,
        out_shape=tuple([jax.ShapeDtypeStruct((rows, width), BF16)] * sends),
        in_specs=[SCALARS] + [WHOLE] * 3,
        out_specs=(WHOLE,) * sends,
        compiler_params=pltpu.CompilerParams(vmem_limit_bytes=8 << 20),
        name="combine",
    )(targets, own, other, weight)


def body(
    projected,
    carried_tail,
    carried_state,
    filter_taps,
    filter_bias,
    select_weight,
    step_weight,
    step_bias,
    log_rate,
    skip_gain,
    output_weight,
    residual,
    norm_gain,
    router,
    gate_weight,
    up_weight,
    down_weight,
    routes,
):
    ctx, exp = lax.axis_size("ctx"), lax.axis_size("exp")
    ctx_at, exp_at = lax.axis_index("ctx"), lax.axis_index("exp")
    places = ring_places("ctx")
    x_input, z_input = projected[0], projected[1]
    own, width = residual.shape
    columns = output_weight.shape[1]
    taps = filter_taps.shape[0]

    x_pieces = spread(lambda k: x_input, "ctx", 0)
    extra = jnp.concatenate([residual, jnp.pad(routes.astype(BF16), ((0, 0), (0, LANES - 2)))], axis=1)
    if exp == 2:
        partner = rotate(extra, "exp", 1)
        extra = jnp.where(
            exp_at == 0,
            jnp.concatenate([extra, partner], axis=0),
            jnp.concatenate([partner, extra], axis=0),
        )
    else:
        extra = lax.all_gather(extra, "exp", axis=0, tiled=True)
    tail_pad = jnp.zeros((8 - carried_tail.shape[0], carried_tail.shape[1]), F32)
    params = jnp.concatenate(
        [filter_taps, filter_bias[None], step_bias[None], skip_gain[None], jnp.zeros_like(tail_pad)[: 5 - taps],
         tail_pad, carried_tail.astype(F32)]
    )
    ready = [jnp.concatenate([z_input, extra[:, width:]], axis=1), extra[:, :width]]
    router_rows = jnp.pad(router.T, ((0, 16 - EXPERTS), (0, 0)))
    gain = jnp.pad(norm_gain[None, :], ((0, 7), (0, 0)))
    params, router_rows, gain = lax.optimization_barrier((params, router_rows, gain))

    active, proj = activate(places, x_pieces, params, taps, select_weight)
    own_proj, other_proj = pair_sum(proj, "exp")

    def bundle(k):
        piece = lax.dynamic_slice_in_dim(ready[1], k * columns, columns, axis=1)
        channels = z_input.shape[1]
        return jnp.concatenate([ready[0][:, :channels], piece, ready[0][:, channels:]], axis=1)

    z_pieces = spread(bundle, "ctx", 0, active)
    value = scan(own_proj, other_proj, active, params, taps, log_rate, step_weight, carried_state)
    base, sent, all_routes = project(places, value, output_weight, z_pieces)
    if exp == 2:
        mixed = (base + rotate(sent, "exp", 1).astype(F32)).astype(BF16)
    else:
        mixed = (base - sent.astype(F32) + lax.psum(sent.astype(F32), "exp")).astype(BF16)
    parts = ctx * exp
    shared = parts <= 8 and mixed.shape[0] == LANES and lax.axis_size("doc") % 2 == 0
    if shared:
        half = lax.rem(lax.axis_index("doc"), 2).astype(jnp.int32)[None]
        half, mixed = lax.optimization_barrier((half, mixed))
        gate_half, up_half, half = fetch(half, [gate_weight, up_weight])
    mixed_pieces = spread(lambda k: mixed, "ctx", 1)
    me = ctx_at * exp + exp_at
    spots = jnp.stack([ctx_at // (ctx // EXPERTS), me]).astype(jnp.int32)
    if shared:
        spots, half = lax.optimization_barrier((spots, half))
    normed, weight, mine = norm(places, spots, gain, router_rows, all_routes, mixed_pieces, own)
    total = mine.astype(F32)
    axes = ("ctx", "exp")
    if shared:
        kept, given = shared_experts(half, normed, swap(normed), gate_half, up_half, down_weight)
        targets = jnp.stack([lax.rem(me + s, parts) for s in range(parts)]).astype(jnp.int32)
        outs = combine(targets, kept, swap(given), weight, own)
        arrived = [outs[0]]
        for s in range(1, parts):
            arrived.append(lax.ppermute(outs[s], axes, [(i, (i + s) % parts) for i in range(parts)]))
        for piece in arrived:
            total = total + piece.astype(F32)
    else:
        kept = experts(normed, gate_weight, up_weight, down_weight)
        partial = (kept * weight[:, :1]).astype(BF16)
        moved = lax.all_to_all(partial, axes, split_axis=0, concat_axis=0, tiled=True)
        total = total + jnp.sum(moved.reshape(parts, own, width).astype(F32), axis=0)
    return total.astype(BF16)


def solution(mesh):
    placed = (
        P(None, ("doc", "ctx"), "exp"),
        P("doc", "exp"),
        P("doc", "exp"),
        P(None, "exp"),
        P("exp"),
        P(None, "exp"),
        P(None, "exp"),
        P("exp"),
        P(None, "exp"),
        P("exp"),
        P("exp", "ctx"),
        P(("doc", "ctx", "exp"), None),
        P(),
        P(),
        P(("ctx", "exp"), None),
        P(("ctx", "exp"), None),
        P(("ctx", "exp"), None),
        P(("doc", "ctx", "exp"), None),
    )
    return jax.shard_map(
        body, mesh=mesh, in_specs=placed, out_specs=P(("doc", "ctx", "exp"), None), check_vma=False
    )
```

```python
import functools
import math

import jax
import jax.numpy as jnp
from jax import lax
from jax.experimental import pallas as pl
from jax.experimental.pallas import tpu as pltpu
from jax.sharding import PartitionSpec as P

EXPERTS = 4
LANES = 128
FEW = 4
LOG2E = 1.4426950408889634
VMEM = pltpu.VMEM
SMEM = pltpu.SMEM
F32 = jnp.float32
BF16 = jnp.bfloat16


def contract_last(left, right):
    return lax.dot_general(left, right, (((1,), (1,)), ((), ())), preferred_element_type=F32)


def rotate(value, axis, steps):
    count = lax.axis_size(axis)
    return lax.ppermute(value, axis, [(i, (i + steps) % count) for i in range(count)])


def ring_places(axis):
    count = lax.axis_size(axis)
    if count > FEW:
        return jnp.zeros((1,), jnp.int32)
    me = lax.axis_index(axis)
    return jnp.stack([lax.rem(me + count - s, count) for s in range(count)]).astype(jnp.int32)


def spread(make, axis, join, after=None):
    count = lax.axis_size(axis)
    me = lax.axis_index(axis)
    if count <= FEW:
        sent = [make(lax.rem(me + s, count)) for s in range(1, count)]
        if after is not None:
            sent, _ = lax.optimization_barrier((sent, after))
        return [make(me)] + [rotate(sent[s - 1], axis, s) for s in range(1, count)]
    stacked = jnp.stack([make(jnp.int32(k)) for k in range(count)])
    moved = lax.all_to_all(stacked, axis, split_axis=0, concat_axis=0, tiled=True)
    return [jnp.concatenate([moved[k] for k in range(count)], axis=join)]


def swap(value):
    count = lax.axis_size("doc")
    return lax.ppermute(value, "doc", [(i, i + 1 - 2 * (i % 2)) for i in range(count)])


def far(value):
    return pltpu.with_memory_space_constraint(value, pltpu.HBM)


def pair_sum(value, axis):
    if lax.axis_size(axis) == 2:
        return [value, rotate(value, axis, 1)]
    total = lax.psum(value.astype(F32), axis).astype(value.dtype)
    return [total, jnp.zeros_like(total)]


FAR = pl.BlockSpec(memory_space=pltpu.HBM)
WHOLE = pl.BlockSpec(memory_space=VMEM)
SCALARS = pl.BlockSpec(memory_space=SMEM)


def activate_kernel(count, taps, places, params, select, *refs):
    pieces, (active, proj, padded, held, sem) = refs[:count], refs[count:]
    copy = pltpu.make_async_copy(select, held, sem)
    copy.start()
    rows = pieces[0].shape[0]
    padded[0:8, :] = params[8:16, :]
    for index in range(count):
        start = pl.multiple_of(8 + places[index] * rows, 8)
        padded[pl.ds(start, rows), :] = pieces[index][...].astype(F32)
    tokens = active.shape[0]
    step = 32

    def block(number, carry):
        base = pl.multiple_of(number * step, step)
        window = padded[pl.ds(base, step + 8), :]
        total = jnp.broadcast_to(params[taps : taps + 1, :], (step, params.shape[1]))
        for k in range(taps):
            offset = 8 - (taps - 1) + k
            total = total + params[k : k + 1, :] * window[offset : offset + step, :]
        value = total / (1.0 + jnp.exp(-total))
        active[pl.ds(base, step), :] = value.astype(BF16)
        return carry

    lax.fori_loop(0, tokens // step, block, 0)
    copy.wait()
    for number in range(tokens // LANES):
        cut = slice(number * LANES, (number + 1) * LANES)
        proj[:, cut] = contract_last(held[...], active[cut, :])


def activate(places, pieces, params, taps, select):
    count = len(pieces)
    tokens = count * pieces[0].shape[0]
    channels = pieces[0].shape[1]
    return pl.pallas_call(
        functools.partial(activate_kernel, count, taps),
        out_shape=(
            jax.ShapeDtypeStruct((tokens, channels), BF16),
            jax.ShapeDtypeStruct((select.shape[0], tokens), F32),
        ),
        in_specs=[SCALARS, WHOLE, FAR] + [WHOLE] * count,
        out_specs=(WHOLE,) * 2,
        scratch_shapes=[
            VMEM((tokens + 8, channels), F32),
            VMEM(select.shape, BF16),
            pltpu.SemaphoreType.DMA,
        ],
        compiler_params=pltpu.CompilerParams(vmem_limit_bytes=12 << 20),
        cost_estimate=pl.CostEstimate(
            flops=2 * tokens * channels * select.shape[0],
            bytes_accessed=4 * tokens * channels,
            transcendentals=tokens * channels,
        ),
        name="activate",
    )(places, params, far(select), *pieces)


def scan_kernel(
    taps, own, other, active, params, log_rate_hbm, step_weight_hbm, state_hbm, value_out,
    sums, steps, scaled, rates, state, coef, step_weight, state_in, log_rate, sems,
):
    tokens, channels = active.shape
    rank = step_weight.shape[0]
    state_size = log_rate.shape[0]
    folds = channels // LANES
    group = min(folds, 16)
    load_weight = pltpu.make_async_copy(step_weight_hbm, step_weight, sems.at[0])
    load_state = pltpu.make_async_copy(state_hbm, state_in, sems.at[1])
    load_rate = pltpu.make_async_copy(log_rate_hbm, log_rate, sems.at[3])
    load_rate.start()
    load_state.start()
    load_weight.start()
    sums[...] = own[...] + other[...]
    copy = pltpu.make_async_copy(sums.at[pl.ds(rank, 2 * state_size), :], coef, sems.at[2])
    copy.start()

    def scatter(target, source):
        for s8 in range(state_size // 8):
            for j in range(folds):
                lanes = slice(j * LANES, (j + 1) * LANES)
                there = slice((s8 * folds + j) * 8, (s8 * folds + j) * 8 + 8)
                target[there, :] = source[s8 * 8 : s8 * 8 + 8, lanes]

    def fold_rows(row, first):
        return pl.ds((row // 8) * (folds * 8) + row % 8 + first * 8, group, stride=8)

    load_rate.wait()
    scatter(state, log_rate)
    for s in range(state_size):
        for first in range(0, folds, group):
            rates[s * folds + first : s * folds + first + group, :] = (
                jnp.exp(state[fold_rows(s, first), :]) * (-LOG2E)
            )
    load_state.wait()
    scatter(state, state_in)
    load_weight.wait()

    for number in range(tokens // LANES):
        cut = slice(number * LANES, (number + 1) * LANES)
        low = jnp.transpose(sums[0:rank, cut]).astype(BF16)
        width = min(channels, 256)
        for w in range(channels // width):
            lanes = slice(w * width, (w + 1) * width)
            raw = jnp.dot(low, step_weight[:, lanes], preferred_element_type=F32)
            raw = raw + params[taps + 1 : taps + 2, lanes]
            size = jnp.maximum(raw, 0.0) + jnp.log(1.0 + jnp.exp(-jnp.abs(raw)))
            times = size * active[cut, lanes].astype(F32)
            for i in range(LANES // 8):
                for j in range(width // LANES):
                    block = (number * LANES // 8 + i) * folds + w * (width // LANES) + j
                    there = slice(block * 8, block * 8 + 8)
                    part = (slice(i * 8, i * 8 + 8), slice(j * LANES, (j + 1) * LANES))
                    steps[there, :] = size[part]
                    scaled[there, :] = times[part]
    copy.wait()

    for first in range(0, folds, group):
        start = tuple(state[fold_rows(s, first), :] for s in range(state_size))

        def eight(number, held):
            base = number * (folds * 8) + first * 8
            held = list(held)
            for r in range(8):
                token = number * 8 + r
                rows = pl.ds(base + r, group, stride=8)
                size, times = steps[rows, :], scaled[rows, :]
                total = None
                for s in range(state_size):
                    rate = rates[s * folds + first : s * folds + first + group, :]
                    held[s] = jnp.exp2(size * rate) * held[s] + times * coef[s, token]
                    term = held[s] * coef[state_size + s, token]
                    total = term if total is None else total + term
                steps[rows, :] = total
            return tuple(held)

        lax.fori_loop(0, tokens // 8, eight, start)

    def unfold(number, carry):
        here = pl.ds(pl.multiple_of(number * 16, 16), 16)
        for j in range(folds):
            lanes = slice(j * LANES, (j + 1) * LANES)
            found = []
            for half in range(2):
                block = pl.multiple_of((number * 2 + half) * (folds * 8) + j * 8, 8)
                found.append(steps[pl.ds(block, 8), :])
            gain = params[taps + 2 : taps + 3, lanes]
            value_out[here, lanes] = jnp.concatenate(found, axis=0) + gain * active[here, lanes].astype(F32)
        return carry

    lax.fori_loop(0, tokens // 16, unfold, 0)


def scan(own, other, active, params, taps, log_rate, step_weight, state_in):
    tokens, channels = active.shape
    state_size = log_rate.shape[0]
    folded = (state_size * channels // LANES, LANES)
    return pl.pallas_call(
        functools.partial(scan_kernel, taps),
        out_shape=jax.ShapeDtypeStruct((tokens, channels), F32),
        in_specs=[WHOLE] * 4 + [FAR] * 3,
        out_specs=WHOLE,
        scratch_shapes=[
            VMEM(own.shape, F32),
            VMEM((tokens * channels // LANES, LANES), F32),
            VMEM((tokens * channels // LANES, LANES), F32),
            VMEM(folded, F32),
            VMEM(folded, F32),
            SMEM((2 * state_size, tokens), F32),
            VMEM(step_weight.shape, BF16),
            VMEM(state_in.shape, F32),
            VMEM(log_rate.shape, F32),
            pltpu.SemaphoreType.DMA((4,)),
        ],
        compiler_params=pltpu.CompilerParams(vmem_limit_bytes=16 << 20),
        cost_estimate=pl.CostEstimate(
            flops=3000 * tokens * channels * state_size,
            bytes_accessed=8 * tokens * channels,
            transcendentals=tokens * channels * state_size,
        ),
        name="scan",
    )(own, other, active, params, far(log_rate), far(step_weight), far(state_in))


def project_kernel(count, columns, places, value_in, weight_hbm, *refs):
    pieces = refs[:count]
    base_out, send_out, routes_out, gated, out_weight, sem = refs[count:]
    copy = pltpu.make_async_copy(weight_hbm, out_weight, sem)
    copy.start()
    tokens, channels = value_in.shape
    rows = pieces[0].shape[0]
    tile = 16
    for index in range(count):
        begin = pl.multiple_of(places[index] * rows, tile)
        routes_out[pl.ds(begin, rows), :] = pieces[index][:, channels + columns :]

        def gate(number, carry):
            local = pl.ds(pl.multiple_of(number * tile, tile), tile)
            here = pl.ds(pl.multiple_of(begin + number * tile, tile), tile)
            z = pieces[index][local, :channels].astype(F32)
            gated[here, :] = (value_in[here, :] * (z / (1.0 + jnp.exp(-z)))).astype(BF16)
            return carry

        lax.fori_loop(0, rows // tile, gate, 0)
    copy.wait()
    for number in range(tokens // LANES):
        cut = slice(number * LANES, (number + 1) * LANES)
        sent = jnp.dot(gated[cut, :], out_weight[...], preferred_element_type=F32).astype(BF16)
        send_out[cut, :] = sent
        base_out[cut, :] = sent.astype(F32)
    for index in range(count):
        here = pl.ds(pl.multiple_of(places[index] * rows, tile), rows)
        base_out[here, :] += pieces[index][:, channels : channels + columns].astype(F32)


def project(places, value, out_weight, pieces):
    tokens, channels = value.shape
    columns = out_weight.shape[1]
    count = len(pieces)
    return pl.pallas_call(
        functools.partial(project_kernel, count, columns),
        out_shape=(
            jax.ShapeDtypeStruct((tokens, columns), F32),
            jax.ShapeDtypeStruct((tokens, columns), BF16),
            jax.ShapeDtypeStruct((tokens, LANES), BF16),
        ),
        in_specs=[SCALARS, WHOLE, FAR] + [WHOLE] * count,
        out_specs=(WHOLE,) * 3,
        scratch_shapes=[
            VMEM((tokens, channels), BF16),
            VMEM(out_weight.shape, BF16),
            pltpu.SemaphoreType.DMA,
        ],
        compiler_params=pltpu.CompilerParams(vmem_limit_bytes=16 << 20),
        cost_estimate=pl.CostEstimate(
            flops=2 * tokens * channels * columns,
            bytes_accessed=8 * tokens * channels,
            transcendentals=tokens * channels,
        ),
        name="project",
    )(places, value, far(out_weight), *pieces)


def norm_kernel(count, places, spots, gain, router, routes, *refs):
    pieces = refs[:count]
    normed, weight, own_rows = refs[count : count + 3]
    mixed = pieces[0] if count == 1 else refs[-1]
    tokens = normed.shape[0]
    columns = pieces[0].shape[1]
    for index in range(count if count > 1 else 0):
        start = pl.multiple_of(places[index] * columns, LANES)
        mixed[:, pl.ds(start, columns)] = pieces[index][...]
    mine = spots[0].astype(F32)
    step = 32

    def block(number, carry):
        cut = pl.ds(pl.multiple_of(number * step, step), step)
        value = mixed[cut, :].astype(F32)
        square = jnp.mean(value * value, axis=-1, keepdims=True) + 1e-06
        scaled = (value * lax.rsqrt(square) * gain[0:1, :]).astype(BF16)
        normed[cut, :] = scaled
        return carry

    lax.fori_loop(0, tokens // step, block, 0)
    for c in range(tokens // LANES):
        cut = slice(c * LANES, (c + 1) * LANES)
        logits = contract_last(normed[cut, :], router[...])
        first = routes[cut, 0:1].astype(F32)
        second = routes[cut, 1:2].astype(F32)
        ids = lax.broadcasted_iota(jnp.int32, logits.shape, 1).astype(F32)
        first_logit = jnp.sum(jnp.where(ids == first, logits, 0.0), axis=1, keepdims=True)
        second_logit = jnp.sum(jnp.where(ids == second, logits, 0.0), axis=1, keepdims=True)
        first_gate = jnp.where(first == mine, 1.0 / (1.0 + jnp.exp(second_logit - first_logit)), 0.0)
        second_gate = jnp.where(second == mine, 1.0 / (1.0 + jnp.exp(first_logit - second_logit)), 0.0)
        weight[cut, :] = jnp.broadcast_to(first_gate + second_gate, (LANES, LANES))
    rows = own_rows.shape[0]
    own_rows[...] = mixed[pl.ds(pl.multiple_of(spots[1] * rows, 16), rows), :]


def norm(places, spots, gain, router, routes, pieces, own):
    count = len(pieces)
    tokens = pieces[0].shape[0]
    width = count * pieces[0].shape[1]
    return pl.pallas_call(
        functools.partial(norm_kernel, count),
        out_shape=(
            jax.ShapeDtypeStruct((tokens, width), BF16),
            jax.ShapeDtypeStruct((tokens, LANES), F32),
            jax.ShapeDtypeStruct((own, width), BF16),
        ),
        in_specs=[SCALARS] * 2 + [WHOLE] * (3 + count),
        out_specs=(WHOLE,) * 3,
        scratch_shapes=[VMEM((tokens, width), BF16)] if count > 1 else [],
        compiler_params=pltpu.CompilerParams(vmem_limit_bytes=8 << 20),
        name="norm",
    )(places, spots, gain, router, routes, *pieces)


def fetch_kernel(parts, half_rows, half, *refs):
    count = len(refs) // 2 - 1
    sources, targets, done, sems = refs[:count], refs[count : 2 * count], refs[-2], refs[-1]
    rows = targets[0].shape[0]
    part = rows // parts
    copies = []
    for index in range(count):
        for k in range(parts):
            start = pl.multiple_of(half[0] * half_rows + k * part, 16)
            copies.append(
                pltpu.make_async_copy(
                    sources[index].at[pl.ds(start, part), :],
                    targets[index].at[pl.ds(k * part, part), :],
                    sems.at[index * parts + k],
                )
            )
    for copy in copies:
        copy.start()
    for copy in copies:
        copy.wait()
    done[0] = half[0]


def fetch(half, weights):
    half_rows, width = weights[0].shape[0] // 2, weights[0].shape[1]
    rows = half_rows // 2
    parts = 4
    return pl.pallas_call(
        functools.partial(fetch_kernel, parts, half_rows),
        out_shape=tuple([VMEM((rows, width), BF16)] * len(weights)) + (jax.ShapeDtypeStruct((1,), jnp.int32),),
        in_specs=[SCALARS] + [FAR] * len(weights),
        out_specs=tuple([WHOLE] * len(weights)) + (SCALARS,),
        scratch_shapes=[pltpu.SemaphoreType.DMA((parts * len(weights),))],
        compiler_params=pltpu.CompilerParams(vmem_limit_bytes=1 << 20),
        cost_estimate=pl.CostEstimate(
            flops=0, bytes_accessed=4 * rows * width * len(weights), transcendentals=0
        ),
        name="fetch",
    )(half, *[far(w) for w in weights])


def shared_kernel(half, own, other, gate_first, up_first, gate, up, down, kept, given, tokens, hidden, late, last, sems):
    rows = own.shape[0]
    quarter, width = gate_first.shape
    begin = half[0] * (2 * quarter)
    copies = []
    for index, (source, offset) in enumerate(((gate, quarter), (up, quarter), (down, 0), (down, quarter))):
        here = pl.ds(pl.multiple_of(begin + offset, 16), quarter)
        target = late.at[index] if index < 2 else last.at[index - 2]
        copies.append(pltpu.make_async_copy(source.at[here, :], target, sems.at[index]))
    for copy in copies:
        copy.start()
    tokens[0:rows, :] = own[...]
    tokens[rows:, :] = other[...]

    def activate_hidden(gate_rows, up_rows, place):
        gate_act = contract_last(tokens[...], gate_rows[...])
        up_act = contract_last(tokens[...], up_rows[...])
        value = gate_act / (1.0 + jnp.exp(-gate_act)) * up_act
        hidden[:, place * quarter : (place + 1) * quarter] = value.astype(BF16)

    activate_hidden(gate_first, up_first, 0)
    copies[0].wait()
    copies[1].wait()
    activate_hidden(late.at[0], late.at[1], 1)
    copies[2].wait()
    copies[3].wait()
    step = 256
    for start in range(0, width, step):
        here = slice(start, start + step)
        product = jnp.dot(hidden[:, :quarter], last[0, :, here], preferred_element_type=F32)
        product += jnp.dot(hidden[:, quarter:], last[1, :, here], preferred_element_type=F32)
        kept[:, here] = product[0:rows, :]
        given[:, here] = product[rows:, :].astype(BF16)


def shared_experts(half, own, other, gate_first, up_first, gate, up, down):
    rows, width = own.shape
    quarter = gate_first.shape[0]
    return pl.pallas_call(
        shared_kernel,
        out_shape=(jax.ShapeDtypeStruct((rows, width), F32), jax.ShapeDtypeStruct((rows, width), BF16)),
        in_specs=[SCALARS] + [WHOLE] * 4 + [FAR] * 3,
        out_specs=(WHOLE,) * 2,
        scratch_shapes=[
            VMEM((2 * rows, width), BF16),
            VMEM((2 * rows, 2 * quarter), BF16),
            VMEM((2, quarter, width), BF16),
            VMEM((2, quarter, width), BF16),
            pltpu.SemaphoreType.DMA((4,)),
        ],
        compiler_params=pltpu.CompilerParams(vmem_limit_bytes=36 << 20),
        cost_estimate=pl.CostEstimate(
            flops=24 * rows * quarter * width,
            bytes_accessed=8 * quarter * width,
            transcendentals=4 * rows * quarter,
        ),
        name="experts",
    )(half, own, other, gate_first, up_first, far(gate), far(up), far(down))


def expert_kernel(tokens, gate, up, down, total):
    number = pl.program_id(0)

    @pl.when(number == 0)
    def _():
        total[...] = jnp.zeros_like(total)

    for start in range(0, total.shape[0], LANES):
        cut = slice(start, start + LANES)
        gate_act = contract_last(tokens[cut, :], gate[...])
        up_act = contract_last(tokens[cut, :], up[...])
        hidden = (gate_act / (1.0 + jnp.exp(-gate_act)) * up_act).astype(BF16)
        total[cut, :] += jnp.dot(hidden, down[...], preferred_element_type=F32)


def experts(tokens, gate, up, down):
    rows, width = tokens.shape
    hidden = gate.shape[0]
    block = hidden if hidden <= 512 else math.gcd(hidden, 512)
    weights = pl.BlockSpec((block, width), lambda i: (i, 0))
    return pl.pallas_call(
        expert_kernel,
        grid=(hidden // block,),
        out_shape=jax.ShapeDtypeStruct((rows, width), F32),
        in_specs=[WHOLE] + [weights] * 3,
        out_specs=WHOLE,
        compiler_params=pltpu.CompilerParams(vmem_limit_bytes=40 << 20),
        cost_estimate=pl.CostEstimate(
            flops=6 * rows * hidden * width,
            bytes_accessed=6 * hidden * width,
            transcendentals=rows * hidden,
        ),
        name="experts",
    )(tokens, gate, up, down)


def combine_kernel(targets, own, other, weight, *outs):
    rows = outs[0].shape[0]
    for index, out in enumerate(outs):
        here = pl.ds(pl.multiple_of(targets[index] * rows, 16), rows)
        out[...] = ((own[here, :] + other[here, :].astype(F32)) * weight[here, 0:1]).astype(BF16)


def combine(targets, own, other, weight, rows):
    width = own.shape[1]
    sends = own.shape[0] // rows
    return pl.pallas_call(
        combine_kernel,
        out_shape=tuple([jax.ShapeDtypeStruct((rows, width), BF16)] * sends),
        in_specs=[SCALARS] + [WHOLE] * 3,
        out_specs=(WHOLE,) * sends,
        compiler_params=pltpu.CompilerParams(vmem_limit_bytes=8 << 20),
        name="combine",
    )(targets, own, other, weight)


def body(
    projected,
    carried_tail,
    carried_state,
    filter_taps,
    filter_bias,
    select_weight,
    step_weight,
    step_bias,
    log_rate,
    skip_gain,
    output_weight,
    residual,
    norm_gain,
    router,
    gate_weight,
    up_weight,
    down_weight,
    routes,
):
    ctx, exp = lax.axis_size("ctx"), lax.axis_size("exp")
    ctx_at, exp_at = lax.axis_index("ctx"), lax.axis_index("exp")
    places = ring_places("ctx")
    x_input, z_input = projected[0], projected[1]
    own, width = residual.shape
    columns = output_weight.shape[1]
    taps = filter_taps.shape[0]

    x_pieces = spread(lambda k: x_input, "ctx", 0)
    extra = jnp.concatenate([residual, jnp.pad(routes.astype(BF16), ((0, 0), (0, LANES - 2)))], axis=1)
    if exp == 2:
        partner = rotate(extra, "exp", 1)
        extra = jnp.where(
            exp_at == 0,
            jnp.concatenate([extra, partner], axis=0),
            jnp.concatenate([partner, extra], axis=0),
        )
    else:
        extra = lax.all_gather(extra, "exp", axis=0, tiled=True)
    tail_pad = jnp.zeros((8 - carried_tail.shape[0], carried_tail.shape[1]), F32)
    params = jnp.concatenate(
        [filter_taps, filter_bias[None], step_bias[None], skip_gain[None], jnp.zeros_like(tail_pad)[: 5 - taps],
         tail_pad, carried_tail.astype(F32)]
    )
    ready = [jnp.concatenate([z_input, extra[:, width:]], axis=1), extra[:, :width]]
    router_rows = jnp.pad(router.T, ((0, 16 - EXPERTS), (0, 0)))
    gain = jnp.pad(norm_gain[None, :], ((0, 7), (0, 0)))
    params, router_rows, gain = lax.optimization_barrier((params, router_rows, gain))

    active, proj = activate(places, x_pieces, params, taps, select_weight)
    own_proj, other_proj = pair_sum(proj, "exp")

    def bundle(k):
        piece = lax.dynamic_slice_in_dim(ready[1], k * columns, columns, axis=1)
        channels = z_input.shape[1]
        return jnp.concatenate([ready[0][:, :channels], piece, ready[0][:, channels:]], axis=1)

    z_pieces = spread(bundle, "ctx", 0, active)
    value = scan(own_proj, other_proj, active, params, taps, log_rate, step_weight, carried_state)
    base, sent, all_routes = project(places, value, output_weight, z_pieces)
    if exp == 2:
        mixed = (base + rotate(sent, "exp", 1).astype(F32)).astype(BF16)
    else:
        mixed = (base - sent.astype(F32) + lax.psum(sent.astype(F32), "exp")).astype(BF16)
    parts = ctx * exp
    shared = parts <= 8 and mixed.shape[0] == LANES and lax.axis_size("doc") % 2 == 0
    if shared:
        half = lax.rem(lax.axis_index("doc"), 2).astype(jnp.int32)[None]
        half, mixed = lax.optimization_barrier((half, mixed))
        gate_first, up_first, half = fetch(half, [gate_weight, up_weight])
    mixed_pieces = spread(lambda k: mixed, "ctx", 1)
    me = ctx_at * exp + exp_at
    spots = jnp.stack([ctx_at // (ctx // EXPERTS), me]).astype(jnp.int32)
    if shared:
        spots, half = lax.optimization_barrier((spots, half))
    normed, weight, mine = norm(places, spots, gain, router_rows, all_routes, mixed_pieces, own)
    total = mine.astype(F32)
    axes = ("ctx", "exp")
    if shared:
        kept, given = shared_experts(half, normed, swap(normed), gate_first, up_first, gate_weight, up_weight, down_weight)
        targets = jnp.stack([lax.rem(me + s, parts) for s in range(parts)]).astype(jnp.int32)
        outs = combine(targets, kept, swap(given), weight, own)
        arrived = [outs[0]]
        for s in range(1, parts):
            arrived.append(lax.ppermute(outs[s], axes, [(i, (i + s) % parts) for i in range(parts)]))
        for piece in arrived:
            total = total + piece.astype(F32)
    else:
        kept = experts(normed, gate_weight, up_weight, down_weight)
        partial = (kept * weight[:, :1]).astype(BF16)
        moved = lax.all_to_all(partial, axes, split_axis=0, concat_axis=0, tiled=True)
        total = total + jnp.sum(moved.reshape(parts, own, width).astype(F32), axis=0)
    return total.astype(BF16)


def solution(mesh):
    placed = (
        P(None, ("doc", "ctx"), "exp"),
        P("doc", "exp"),
        P("doc", "exp"),
        P(None, "exp"),
        P("exp"),
        P(None, "exp"),
        P(None, "exp"),
        P("exp"),
        P(None, "exp"),
        P("exp"),
        P("exp", "ctx"),
        P(("doc", "ctx", "exp"), None),
        P(),
        P(),
        P(("ctx", "exp"), None),
        P(("ctx", "exp"), None),
        P(("ctx", "exp"), None),
        P(("doc", "ctx", "exp"), None),
    )
    return jax.shard_map(
        body, mesh=mesh, in_specs=placed, out_specs=P(("doc", "ctx", "exp"), None), check_vma=False
    )
```

```python
import functools
import math

import jax
import jax.numpy as jnp
from jax import lax
from jax.experimental import pallas as pl
from jax.experimental.pallas import tpu as pltpu
from jax.sharding import PartitionSpec as P

EXPERTS = 4
LANES = 128
FEW = 4
LOG2E = 1.4426950408889634
VMEM = pltpu.VMEM
SMEM = pltpu.SMEM
F32 = jnp.float32
BF16 = jnp.bfloat16


def contract_last(left, right):
    return lax.dot_general(left, right, (((1,), (1,)), ((), ())), preferred_element_type=F32)


def rotate(value, axis, steps):
    count = lax.axis_size(axis)
    return lax.ppermute(value, axis, [(i, (i + steps) % count) for i in range(count)])


def ring_places(axis):
    count = lax.axis_size(axis)
    if count > FEW:
        return jnp.zeros((1,), jnp.int32)
    me = lax.axis_index(axis)
    return jnp.stack([lax.rem(me + count - s, count) for s in range(count)]).astype(jnp.int32)


def layer(piece, index):
    return piece.at[index] if len(piece.shape) == 3 else piece


def spread(make, axis, join, after=None):
    count = lax.axis_size(axis)
    me = lax.axis_index(axis)
    if count <= FEW:
        sent = [make(lax.rem(me + s, count)) for s in range(1, count)]
        if after is not None:
            sent, _ = lax.optimization_barrier((sent, after))
        return [make(me)] + [rotate(sent[s - 1], axis, s) for s in range(1, count)]
    stacked = jnp.stack([make(jnp.int32(k)) for k in range(count)])
    moved = lax.all_to_all(stacked, axis, split_axis=0, concat_axis=0, tiled=True)
    return [jnp.concatenate([moved[k] for k in range(count)], axis=join)]


def swap(value):
    count = lax.axis_size("doc")
    return lax.ppermute(value, "doc", [(i, i + 1 - 2 * (i % 2)) for i in range(count)])


def far(value):
    return pltpu.with_memory_space_constraint(value, pltpu.HBM)


def pair_sum(value, axis):
    if lax.axis_size(axis) == 2:
        return [value, rotate(value, axis, 1)]
    total = lax.psum(value.astype(F32), axis).astype(value.dtype)
    return [total, jnp.zeros_like(total)]


FAR = pl.BlockSpec(memory_space=pltpu.HBM)
WHOLE = pl.BlockSpec(memory_space=VMEM)
SCALARS = pl.BlockSpec(memory_space=SMEM)


def activate_kernel(count, taps, places, params, select, *refs):
    pieces, (active, proj, padded, held, sem) = refs[:count], refs[count:]
    copy = pltpu.make_async_copy(select, held, sem)
    copy.start()
    rows = pieces[0].shape[0]
    padded[0:8, :] = params[8:16, :]
    for index in range(count):
        start = pl.multiple_of(8 + places[index] * rows, 8)
        padded[pl.ds(start, rows), :] = layer(pieces[index], 0)[...].astype(F32)
    tokens = active.shape[0]
    step = 32

    def block(number, carry):
        base = pl.multiple_of(number * step, step)
        window = padded[pl.ds(base, step + 8), :]
        total = jnp.broadcast_to(params[taps : taps + 1, :], (step, params.shape[1]))
        for k in range(taps):
            offset = 8 - (taps - 1) + k
            total = total + params[k : k + 1, :] * window[offset : offset + step, :]
        value = total / (1.0 + jnp.exp(-total))
        active[pl.ds(base, step), :] = value.astype(BF16)
        return carry

    lax.fori_loop(0, tokens // step, block, 0)
    copy.wait()
    for number in range(tokens // LANES):
        cut = slice(number * LANES, (number + 1) * LANES)
        proj[:, cut] = contract_last(held[...], active[cut, :])


def activate(places, pieces, params, taps, select):
    count = len(pieces)
    tokens = count * pieces[0].shape[0]
    channels = pieces[0].shape[1]
    return pl.pallas_call(
        functools.partial(activate_kernel, count, taps),
        out_shape=(
            jax.ShapeDtypeStruct((tokens, channels), BF16),
            jax.ShapeDtypeStruct((select.shape[0], tokens), F32),
        ),
        in_specs=[SCALARS, WHOLE, FAR] + [WHOLE] * count,
        out_specs=(WHOLE,) * 2,
        scratch_shapes=[
            VMEM((tokens + 8, channels), F32),
            VMEM(select.shape, BF16),
            pltpu.SemaphoreType.DMA,
        ],
        compiler_params=pltpu.CompilerParams(vmem_limit_bytes=12 << 20),
        cost_estimate=pl.CostEstimate(
            flops=2 * tokens * channels * select.shape[0],
            bytes_accessed=4 * tokens * channels,
            transcendentals=tokens * channels,
        ),
        name="activate",
    )(places, params, far(select), *pieces)


def scan_kernel(
    taps, own, other, active, params, log_rate_hbm, step_weight_hbm, state_hbm, value_out,
    sums, steps, scaled, rates, state, coef, step_weight, state_in, log_rate, sems,
):
    tokens, channels = active.shape
    rank = step_weight.shape[0]
    state_size = log_rate.shape[0]
    folds = channels // LANES
    group = min(folds, 16)
    load_weight = pltpu.make_async_copy(step_weight_hbm, step_weight, sems.at[0])
    load_state = pltpu.make_async_copy(state_hbm, state_in, sems.at[1])
    load_rate = pltpu.make_async_copy(log_rate_hbm, log_rate, sems.at[3])
    load_rate.start()
    load_state.start()
    load_weight.start()
    sums[...] = own[...] + other[...]
    copy = pltpu.make_async_copy(sums.at[pl.ds(rank, 2 * state_size), :], coef, sems.at[2])
    copy.start()

    def scatter(target, source):
        for s8 in range(state_size // 8):
            for j in range(folds):
                lanes = slice(j * LANES, (j + 1) * LANES)
                there = slice((s8 * folds + j) * 8, (s8 * folds + j) * 8 + 8)
                target[there, :] = source[s8 * 8 : s8 * 8 + 8, lanes]

    def fold_rows(row, first):
        return pl.ds((row // 8) * (folds * 8) + row % 8 + first * 8, group, stride=8)

    load_rate.wait()
    scatter(state, log_rate)
    for s in range(state_size):
        for first in range(0, folds, group):
            rates[s * folds + first : s * folds + first + group, :] = (
                jnp.exp(state[fold_rows(s, first), :]) * (-LOG2E)
            )
    load_state.wait()
    scatter(state, state_in)
    load_weight.wait()

    for number in range(tokens // LANES):
        cut = slice(number * LANES, (number + 1) * LANES)
        low = jnp.transpose(sums[0:rank, cut]).astype(BF16)
        width = min(channels, 256)
        for w in range(channels // width):
            lanes = slice(w * width, (w + 1) * width)
            raw = jnp.dot(low, step_weight[:, lanes], preferred_element_type=F32)
            raw = raw + params[taps + 1 : taps + 2, lanes]
            size = jnp.maximum(raw, 0.0) + jnp.log(1.0 + jnp.exp(-jnp.abs(raw)))
            times = size * active[cut, lanes].astype(F32)
            for i in range(LANES // 8):
                for j in range(width // LANES):
                    block = (number * LANES // 8 + i) * folds + w * (width // LANES) + j
                    there = slice(block * 8, block * 8 + 8)
                    part = (slice(i * 8, i * 8 + 8), slice(j * LANES, (j + 1) * LANES))
                    steps[there, :] = size[part]
                    scaled[there, :] = times[part]
    copy.wait()

    for first in range(0, folds, group):
        start = tuple(state[fold_rows(s, first), :] for s in range(state_size))

        def eight(number, held):
            base = number * (folds * 8) + first * 8
            held = list(held)
            for r in range(8):
                token = number * 8 + r
                rows = pl.ds(base + r, group, stride=8)
                size, times = steps[rows, :], scaled[rows, :]
                total = None
                for s in range(state_size):
                    rate = rates[s * folds + first : s * folds + first + group, :]
                    held[s] = jnp.exp2(size * rate) * held[s] + times * coef[s, token]
                    term = held[s] * coef[state_size + s, token]
                    total = term if total is None else total + term
                steps[rows, :] = total
            return tuple(held)

        lax.fori_loop(0, tokens // 8, eight, start)

    def unfold(number, carry):
        here = pl.ds(pl.multiple_of(number * 16, 16), 16)
        for j in range(folds):
            lanes = slice(j * LANES, (j + 1) * LANES)
            found = []
            for half in range(2):
                block = pl.multiple_of((number * 2 + half) * (folds * 8) + j * 8, 8)
                found.append(steps[pl.ds(block, 8), :])
            gain = params[taps + 2 : taps + 3, lanes]
            value_out[here, lanes] = jnp.concatenate(found, axis=0) + gain * active[here, lanes].astype(F32)
        return carry

    lax.fori_loop(0, tokens // 16, unfold, 0)


def scan(own, other, active, params, taps, log_rate, step_weight, state_in):
    tokens, channels = active.shape
    state_size = log_rate.shape[0]
    folded = (state_size * channels // LANES, LANES)
    return pl.pallas_call(
        functools.partial(scan_kernel, taps),
        out_shape=jax.ShapeDtypeStruct((tokens, channels), F32),
        in_specs=[WHOLE] * 4 + [FAR] * 3,
        out_specs=WHOLE,
        scratch_shapes=[
            VMEM(own.shape, F32),
            VMEM((tokens * channels // LANES, LANES), F32),
            VMEM((tokens * channels // LANES, LANES), F32),
            VMEM(folded, F32),
            VMEM(folded, F32),
            SMEM((2 * state_size, tokens), F32),
            VMEM(step_weight.shape, BF16),
            VMEM(state_in.shape, F32),
            VMEM(log_rate.shape, F32),
            pltpu.SemaphoreType.DMA((4,)),
        ],
        compiler_params=pltpu.CompilerParams(vmem_limit_bytes=16 << 20),
        cost_estimate=pl.CostEstimate(
            flops=3000 * tokens * channels * state_size,
            bytes_accessed=8 * tokens * channels,
            transcendentals=tokens * channels * state_size,
        ),
        name="scan",
    )(own, other, active, params, far(log_rate), far(step_weight), far(state_in))


def project_kernel(count, places, value_in, weight_hbm, *refs):
    pieces, extras = refs[:count], refs[count : 2 * count]
    base_out, send_out, routes_out, gated, out_weight, sem = refs[2 * count :]
    copy = pltpu.make_async_copy(weight_hbm, out_weight, sem)
    copy.start()
    tokens = value_in.shape[0]
    columns = base_out.shape[1]
    rows = pieces[0].shape[0]
    tile = 16
    for index in range(count):
        begin = pl.multiple_of(places[index] * rows, tile)
        routes_out[pl.ds(begin, rows), :] = extras[index][:, columns:]
        source = layer(pieces[index], 1)

        def gate(number, carry):
            local = pl.ds(pl.multiple_of(number * tile, tile), tile)
            here = pl.ds(pl.multiple_of(begin + number * tile, tile), tile)
            z = source[local, :].astype(F32)
            gated[here, :] = (value_in[here, :] * (z / (1.0 + jnp.exp(-z)))).astype(BF16)
            return carry

        lax.fori_loop(0, rows // tile, gate, 0)
    copy.wait()
    for number in range(tokens // LANES):
        cut = slice(number * LANES, (number + 1) * LANES)
        sent = jnp.dot(gated[cut, :], out_weight[...], preferred_element_type=F32).astype(BF16)
        send_out[cut, :] = sent
        base_out[cut, :] = sent.astype(F32)
    for index in range(count):
        here = pl.ds(pl.multiple_of(places[index] * rows, tile), rows)
        base_out[here, :] += extras[index][:, :columns].astype(F32)


def project(places, value, out_weight, pieces, extras):
    tokens, channels = value.shape
    columns = out_weight.shape[1]
    count = len(pieces)
    return pl.pallas_call(
        functools.partial(project_kernel, count),
        out_shape=(
            jax.ShapeDtypeStruct((tokens, columns), F32),
            jax.ShapeDtypeStruct((tokens, columns), BF16),
            jax.ShapeDtypeStruct((tokens, LANES), BF16),
        ),
        in_specs=[SCALARS, WHOLE, FAR] + [WHOLE] * (2 * count),
        out_specs=(WHOLE,) * 3,
        scratch_shapes=[
            VMEM((tokens, channels), BF16),
            VMEM(out_weight.shape, BF16),
            pltpu.SemaphoreType.DMA,
        ],
        compiler_params=pltpu.CompilerParams(vmem_limit_bytes=16 << 20),
        cost_estimate=pl.CostEstimate(
            flops=2 * tokens * channels * columns,
            bytes_accessed=8 * tokens * channels,
            transcendentals=tokens * channels,
        ),
        name="project",
    )(places, value, far(out_weight), *pieces, *extras)


def norm_kernel(count, early, places, spots, gain, router, routes, *refs):
    pieces, sources = refs[:count], refs[count : count + early]
    normed, weight, own_rows = refs[count + early : count + early + 3]
    firsts, rest = refs[count + early + 3 : count + 2 * early + 3], refs[count + 2 * early + 3 :]
    mixed = pieces[0] if count == 1 else rest[0]
    copies = []
    for index in range(early):
        first = firsts[index].shape[0]
        begin = pl.multiple_of(spots[2] * (sources[index].shape[0] // 2), 16)
        part = first // 2
        for k in range(2):
            copies.append(
                pltpu.make_async_copy(
                    sources[index].at[pl.ds(begin + k * part, part), :],
                    firsts[index].at[pl.ds(k * part, part), :],
                    rest[-1].at[2 * index + k],
                )
            )
    for copy in copies:
        copy.start()
    tokens = normed.shape[0]
    columns = pieces[0].shape[1]
    for index in range(count if count > 1 else 0):
        start = pl.multiple_of(places[index] * columns, LANES)
        mixed[:, pl.ds(start, columns)] = pieces[index][...]
    mine = spots[0].astype(F32)
    step = 32

    def block(number, carry):
        cut = pl.ds(pl.multiple_of(number * step, step), step)
        value = mixed[cut, :].astype(F32)
        square = jnp.mean(value * value, axis=-1, keepdims=True) + 1e-06
        scaled = (value * lax.rsqrt(square) * gain[0:1, :]).astype(BF16)
        normed[cut, :] = scaled
        return carry

    lax.fori_loop(0, tokens // step, block, 0)
    for c in range(tokens // LANES):
        cut = slice(c * LANES, (c + 1) * LANES)
        logits = contract_last(normed[cut, :], router[...])
        first = routes[cut, 0:1].astype(F32)
        second = routes[cut, 1:2].astype(F32)
        ids = lax.broadcasted_iota(jnp.int32, logits.shape, 1).astype(F32)
        first_logit = jnp.sum(jnp.where(ids == first, logits, 0.0), axis=1, keepdims=True)
        second_logit = jnp.sum(jnp.where(ids == second, logits, 0.0), axis=1, keepdims=True)
        first_gate = jnp.where(first == mine, 1.0 / (1.0 + jnp.exp(second_logit - first_logit)), 0.0)
        second_gate = jnp.where(second == mine, 1.0 / (1.0 + jnp.exp(first_logit - second_logit)), 0.0)
        weight[cut, :] = jnp.broadcast_to(first_gate + second_gate, (LANES, LANES))
    rows = own_rows.shape[0]
    own_rows[...] = mixed[pl.ds(pl.multiple_of(spots[1] * rows, 16), rows), :]
    for copy in copies:
        copy.wait()


def norm(places, spots, gain, router, routes, pieces, own, weights, first):
    count, early = len(pieces), len(weights)
    tokens = pieces[0].shape[0]
    width = count * pieces[0].shape[1]
    return pl.pallas_call(
        functools.partial(norm_kernel, count, early),
        out_shape=(
            jax.ShapeDtypeStruct((tokens, width), BF16),
            jax.ShapeDtypeStruct((tokens, LANES), F32),
            jax.ShapeDtypeStruct((own, width), BF16),
        )
        + tuple(VMEM((first, width), BF16) for _ in weights),
        in_specs=[SCALARS] * 2 + [WHOLE] * (3 + count) + [FAR] * early,
        out_specs=(WHOLE,) * (3 + early),
        scratch_shapes=([VMEM((tokens, width), BF16)] if count > 1 else [])
        + ([pltpu.SemaphoreType.DMA((2 * early,))] if early else []),
        compiler_params=pltpu.CompilerParams(vmem_limit_bytes=8 << 20),
        name="norm",
    )(places, spots, gain, router, routes, *pieces, *[far(w) for w in weights])


def shared_kernel(half, own, other, gate_first, up_first, gate, up, down, kept, given, tokens, hidden, late, last, sems):
    rows = own.shape[0]
    first, width = gate_first.shape
    block = late.shape[2]
    depth = hidden.shape[1]
    begin = half[0] * depth
    copies = []

    def bring(source, offset, count, target):
        here = pl.ds(pl.multiple_of(begin + offset, 16), count)
        copies.append(pltpu.make_async_copy(source.at[here, :], target, sems.at[len(copies)]))
        copies[-1].start()

    for place in range(2):
        bring(gate, first + place * block, block, late.at[place, 0])
        bring(up, first + place * block, block, late.at[place, 1])
    part = depth // 2
    for place in range(2):
        bring(down, place * part, part, last.at[pl.ds(place * part, part), :])
    tokens[0:rows, :] = own[...]
    tokens[rows:, :] = other[...]

    def activate_hidden(gate_rows, up_rows, start):
        gate_act = contract_last(tokens[...], gate_rows[...])
        up_act = contract_last(tokens[...], up_rows[...])
        value = gate_act / (1.0 + jnp.exp(-gate_act)) * up_act
        hidden[:, start : start + gate_rows.shape[0]] = value.astype(BF16)

    activate_hidden(gate_first, up_first, 0)
    for place in range(2):
        copies[2 * place].wait()
        copies[2 * place + 1].wait()
        activate_hidden(late.at[place, 0], late.at[place, 1], first + place * block)
    copies[4].wait()
    copies[5].wait()
    step = 256
    for start in range(0, width, step):
        here = slice(start, start + step)
        product = jnp.dot(hidden[...], last[:, here], preferred_element_type=F32)
        kept[:, here] = product[0:rows, :]
        given[:, here] = product[rows:, :].astype(BF16)


def first_rows(depth):
    first = 768
    return first if depth > first and (depth - first) % (2 * LANES) == 0 else 0


def shared_experts(half, own, other, gate_first, up_first, gate, up, down):
    rows, width = own.shape
    first = gate_first.shape[0]
    depth = gate.shape[0] // 2
    return pl.pallas_call(
        shared_kernel,
        out_shape=(jax.ShapeDtypeStruct((rows, width), F32), jax.ShapeDtypeStruct((rows, width), BF16)),
        in_specs=[SCALARS] + [WHOLE] * 4 + [FAR] * 3,
        out_specs=(WHOLE,) * 2,
        scratch_shapes=[
            VMEM((2 * rows, width), BF16),
            VMEM((2 * rows, depth), BF16),
            VMEM((2, 2, (depth - first) // 2, width), BF16),
            VMEM((depth, width), BF16),
            pltpu.SemaphoreType.DMA((6,)),
        ],
        compiler_params=pltpu.CompilerParams(vmem_limit_bytes=43 << 20),
        cost_estimate=pl.CostEstimate(
            flops=12 * rows * depth * width,
            bytes_accessed=6 * depth * width,
            transcendentals=2 * rows * depth,
        ),
        name="experts",
    )(half, own, other, gate_first, up_first, far(gate), far(up), far(down))


def expert_kernel(tokens, gate, up, down, total):
    number = pl.program_id(0)

    @pl.when(number == 0)
    def _():
        total[...] = jnp.zeros_like(total)

    for start in range(0, total.shape[0], LANES):
        cut = slice(start, start + LANES)
        gate_act = contract_last(tokens[cut, :], gate[...])
        up_act = contract_last(tokens[cut, :], up[...])
        hidden = (gate_act / (1.0 + jnp.exp(-gate_act)) * up_act).astype(BF16)
        total[cut, :] += jnp.dot(hidden, down[...], preferred_element_type=F32)


def experts(tokens, gate, up, down):
    rows, width = tokens.shape
    hidden = gate.shape[0]
    block = hidden if hidden <= 512 else math.gcd(hidden, 512)
    weights = pl.BlockSpec((block, width), lambda i: (i, 0))
    return pl.pallas_call(
        expert_kernel,
        grid=(hidden // block,),
        out_shape=jax.ShapeDtypeStruct((rows, width), F32),
        in_specs=[WHOLE] + [weights] * 3,
        out_specs=WHOLE,
        compiler_params=pltpu.CompilerParams(vmem_limit_bytes=40 << 20),
        cost_estimate=pl.CostEstimate(
            flops=6 * rows * hidden * width,
            bytes_accessed=6 * hidden * width,
            transcendentals=rows * hidden,
        ),
        name="experts",
    )(tokens, gate, up, down)


def combine_kernel(targets, own, other, weight, *outs):
    rows = outs[0].shape[0]
    for index, out in enumerate(outs):
        here = pl.ds(pl.multiple_of(targets[index] * rows, 16), rows)
        out[...] = ((own[here, :] + other[here, :].astype(F32)) * weight[here, 0:1]).astype(BF16)


def combine(targets, own, other, weight, rows):
    width = own.shape[1]
    sends = own.shape[0] // rows
    return pl.pallas_call(
        combine_kernel,
        out_shape=tuple([jax.ShapeDtypeStruct((rows, width), BF16)] * sends),
        in_specs=[SCALARS] + [WHOLE] * 3,
        out_specs=(WHOLE,) * sends,
        compiler_params=pltpu.CompilerParams(vmem_limit_bytes=8 << 20),
        name="combine",
    )(targets, own, other, weight)


def body(
    projected,
    carried_tail,
    carried_state,
    filter_taps,
    filter_bias,
    select_weight,
    step_weight,
    step_bias,
    log_rate,
    skip_gain,
    output_weight,
    residual,
    norm_gain,
    router,
    gate_weight,
    up_weight,
    down_weight,
    routes,
):
    ctx, exp = lax.axis_size("ctx"), lax.axis_size("exp")
    ctx_at, exp_at = lax.axis_index("ctx"), lax.axis_index("exp")
    places = ring_places("ctx")
    x_input, z_input = projected[0], projected[1]
    own, width = residual.shape
    columns = output_weight.shape[1]
    taps = filter_taps.shape[0]

    if ctx <= FEW:
        passed = [rotate(projected, "ctx", s) for s in range(1, ctx)]
        x_pieces, z_pieces = [x_input] + passed, [z_input] + passed
    else:
        passed = lax.all_gather(projected, "ctx", axis=1, tiled=True)
        x_pieces, z_pieces = [passed[0]], [passed[1]]
    extra = jnp.concatenate([residual, jnp.pad(routes.astype(BF16), ((0, 0), (0, LANES - 2)))], axis=1)
    if exp == 2:
        partner = rotate(extra, "exp", 1)
        extra = jnp.where(
            exp_at == 0,
            jnp.concatenate([extra, partner], axis=0),
            jnp.concatenate([partner, extra], axis=0),
        )
    else:
        extra = lax.all_gather(extra, "exp", axis=0, tiled=True)
    tail_pad = jnp.zeros((8 - carried_tail.shape[0], carried_tail.shape[1]), F32)
    params = jnp.concatenate(
        [filter_taps, filter_bias[None], step_bias[None], skip_gain[None], jnp.zeros_like(tail_pad)[: 5 - taps],
         tail_pad, carried_tail.astype(F32)]
    )
    router_rows = jnp.pad(router.T, ((0, 16 - EXPERTS), (0, 0)))
    gain = jnp.pad(norm_gain[None, :], ((0, 7), (0, 0)))
    params, router_rows, gain = lax.optimization_barrier((params, router_rows, gain))

    active, proj = activate(places, x_pieces, params, taps, select_weight)
    own_proj, other_proj = pair_sum(proj, "exp")

    def bundle(k):
        piece = lax.dynamic_slice_in_dim(extra, k * columns, columns, axis=1)
        return jnp.concatenate([piece, extra[:, width:]], axis=1)

    extras = spread(bundle, "ctx", 0, active)
    value = scan(own_proj, other_proj, active, params, taps, log_rate, step_weight, carried_state)
    base, sent, all_routes = project(places, value, output_weight, z_pieces, extras)
    if exp == 2:
        mixed = (base + rotate(sent, "exp", 1).astype(F32)).astype(BF16)
    else:
        mixed = (base - sent.astype(F32) + lax.psum(sent.astype(F32), "exp")).astype(BF16)
    parts = ctx * exp
    first = first_rows(gate_weight.shape[0] // 2)
    shared = parts <= 8 and mixed.shape[0] == LANES and lax.axis_size("doc") % 2 == 0 and first > 0
    half = lax.rem(lax.axis_index("doc"), 2)
    mixed_pieces = spread(lambda k: mixed, "ctx", 1)
    me = ctx_at * exp + exp_at
    spots = jnp.stack([ctx_at // (ctx // EXPERTS), me, half]).astype(jnp.int32)
    early = [gate_weight, up_weight] if shared else []
    normed, weight, mine, *firsts = norm(
        places, spots, gain, router_rows, all_routes, mixed_pieces, own, early, first
    )
    total = mine.astype(F32)
    axes = ("ctx", "exp")
    if shared:
        kept, given = shared_experts(
            half.astype(jnp.int32)[None], normed, swap(normed), *firsts, gate_weight, up_weight, down_weight
        )
        targets = jnp.stack([lax.rem(me + s, parts) for s in range(parts)]).astype(jnp.int32)
        outs = combine(targets, kept, swap(given), weight, own)
        arrived = [outs[0]]
        for s in range(1, parts):
            arrived.append(lax.ppermute(outs[s], axes, [(i, (i + s) % parts) for i in range(parts)]))
        for piece in arrived:
            total = total + piece.astype(F32)
    else:
        kept = experts(normed, gate_weight, up_weight, down_weight)
        partial = (kept * weight[:, :1]).astype(BF16)
        moved = lax.all_to_all(partial, axes, split_axis=0, concat_axis=0, tiled=True)
        total = total + jnp.sum(moved.reshape(parts, own, width).astype(F32), axis=0)
    return total.astype(BF16)


def solution(mesh):
    placed = (
        P(None, ("doc", "ctx"), "exp"),
        P("doc", "exp"),
        P("doc", "exp"),
        P(None, "exp"),
        P("exp"),
        P(None, "exp"),
        P(None, "exp"),
        P("exp"),
        P(None, "exp"),
        P("exp"),
        P("exp", "ctx"),
        P(("doc", "ctx", "exp"), None),
        P(),
        P(),
        P(("ctx", "exp"), None),
        P(("ctx", "exp"), None),
        P(("ctx", "exp"), None),
        P(("doc", "ctx", "exp"), None),
    )
    return jax.shard_map(
        body, mesh=mesh, in_specs=placed, out_specs=P(("doc", "ctx", "exp"), None), check_vma=False
    )
```

```python
import functools
import math

import jax
import jax.numpy as jnp
from jax import lax
from jax.experimental import pallas as pl
from jax.experimental.pallas import tpu as pltpu
from jax.sharding import PartitionSpec as P

EXPERTS = 4
LANES = 128
FEW = 4
LOG2E = 1.4426950408889634
VMEM = pltpu.VMEM
SMEM = pltpu.SMEM
F32 = jnp.float32
BF16 = jnp.bfloat16


def contract_last(left, right):
    return lax.dot_general(left, right, (((1,), (1,)), ((), ())), preferred_element_type=F32)


def rotate(value, axis, steps):
    count = lax.axis_size(axis)
    return lax.ppermute(value, axis, [(i, (i + steps) % count) for i in range(count)])


def partner(place, step, count):
    paired = count & (count - 1) == 0
    return place ^ step if paired else (place + step) % count


def source(place, step, count):
    paired = count & (count - 1) == 0
    return place ^ step if paired else (place - step) % count


def exchange(value, axes, step, count):
    return lax.ppermute(value, axes, [(i, partner(i, step, count)) for i in range(count)])


def ring_places(axis):
    count = lax.axis_size(axis)
    if count > FEW:
        return jnp.zeros((1,), jnp.int32)
    me = lax.axis_index(axis)
    return jnp.stack([source(me, s, count) for s in range(count)]).astype(jnp.int32)


def spread(make, axis, join, after=None):
    count = lax.axis_size(axis)
    me = lax.axis_index(axis)
    if count <= FEW:
        sent = [make(partner(me, s, count)) for s in range(1, count)]
        if after is not None:
            sent, _ = lax.optimization_barrier((sent, after))
        return [make(me)] + [exchange(sent[s - 1], axis, s, count) for s in range(1, count)]
    stacked = jnp.stack([make(jnp.int32(k)) for k in range(count)])
    moved = lax.all_to_all(stacked, axis, split_axis=0, concat_axis=0, tiled=True)
    return [jnp.concatenate([moved[k] for k in range(count)], axis=join)]


def swap(value):
    count = lax.axis_size("doc")
    return lax.ppermute(value, "doc", [(i, i + 1 - 2 * (i % 2)) for i in range(count)])


def far(value):
    return pltpu.with_memory_space_constraint(value, pltpu.HBM)


def pair_sum(value, axis):
    if lax.axis_size(axis) == 2:
        return [value, rotate(value, axis, 1)]
    total = lax.psum(value.astype(F32), axis).astype(value.dtype)
    return [total, jnp.zeros_like(total)]


FAR = pl.BlockSpec(memory_space=pltpu.HBM)
WHOLE = pl.BlockSpec(memory_space=VMEM)
SCALARS = pl.BlockSpec(memory_space=SMEM)


def activate_kernel(count, taps, places, params, select, *refs):
    pieces, (active, proj, padded, held, sem) = refs[:count], refs[count:]
    copy = pltpu.make_async_copy(select, held, sem)
    copy.start()
    rows = pieces[0].shape[0]
    padded[0:8, :] = params[8:16, :]
    for index in range(count):
        start = pl.multiple_of(8 + places[index] * rows, 8)
        padded[pl.ds(start, rows), :] = pieces[index][...].astype(F32)
    tokens = active.shape[0]
    step = 32

    def block(number, carry):
        base = pl.multiple_of(number * step, step)
        window = padded[pl.ds(base, step + 8), :]
        total = jnp.broadcast_to(params[taps : taps + 1, :], (step, params.shape[1]))
        for k in range(taps):
            offset = 8 - (taps - 1) + k
            total = total + params[k : k + 1, :] * window[offset : offset + step, :]
        value = total / (1.0 + jnp.exp(-total))
        active[pl.ds(base, step), :] = value.astype(BF16)
        return carry

    lax.fori_loop(0, tokens // step, block, 0)
    copy.wait()
    for number in range(tokens // LANES):
        cut = slice(number * LANES, (number + 1) * LANES)
        proj[:, cut] = contract_last(held[...], active[cut, :])


def activate(places, pieces, params, taps, select):
    count = len(pieces)
    tokens = count * pieces[0].shape[0]
    channels = pieces[0].shape[1]
    return pl.pallas_call(
        functools.partial(activate_kernel, count, taps),
        out_shape=(
            jax.ShapeDtypeStruct((tokens, channels), BF16),
            jax.ShapeDtypeStruct((select.shape[0], tokens), F32),
        ),
        in_specs=[SCALARS, WHOLE, FAR] + [WHOLE] * count,
        out_specs=(WHOLE,) * 2,
        scratch_shapes=[
            VMEM((tokens + 8, channels), F32),
            VMEM(select.shape, BF16),
            pltpu.SemaphoreType.DMA,
        ],
        compiler_params=pltpu.CompilerParams(vmem_limit_bytes=12 << 20),
        cost_estimate=pl.CostEstimate(
            flops=2 * tokens * channels * select.shape[0],
            bytes_accessed=4 * tokens * channels,
            transcendentals=tokens * channels,
        ),
        name="activate",
    )(places, params, far(select), *pieces)


def scan_kernel(
    taps, own, other, active, params, log_rate_hbm, step_weight_hbm, state_hbm, value_out,
    sums, steps, scaled, rates, state, coef, step_weight, state_in, log_rate, sems,
):
    tokens, channels = active.shape
    rank = step_weight.shape[0]
    state_size = log_rate.shape[0]
    folds = channels // LANES
    group = min(folds, 16)
    load_weight = pltpu.make_async_copy(step_weight_hbm, step_weight, sems.at[0])
    load_state = pltpu.make_async_copy(state_hbm, state_in, sems.at[1])
    load_rate = pltpu.make_async_copy(log_rate_hbm, log_rate, sems.at[3])
    load_rate.start()
    load_state.start()
    load_weight.start()
    sums[...] = own[...] + other[...]
    copy = pltpu.make_async_copy(sums.at[pl.ds(rank, 2 * state_size), :], coef, sems.at[2])
    copy.start()

    def scatter(target, source):
        for s8 in range(state_size // 8):
            for j in range(folds):
                lanes = slice(j * LANES, (j + 1) * LANES)
                there = slice((s8 * folds + j) * 8, (s8 * folds + j) * 8 + 8)
                target[there, :] = source[s8 * 8 : s8 * 8 + 8, lanes]

    def fold_rows(row, first):
        return pl.ds((row // 8) * (folds * 8) + row % 8 + first * 8, group, stride=8)

    load_rate.wait()
    scatter(state, log_rate)
    for s in range(state_size):
        for first in range(0, folds, group):
            rates[s * folds + first : s * folds + first + group, :] = (
                jnp.exp(state[fold_rows(s, first), :]) * (-LOG2E)
            )
    load_state.wait()
    scatter(state, state_in)
    load_weight.wait()

    for number in range(tokens // LANES):
        cut = slice(number * LANES, (number + 1) * LANES)
        low = jnp.transpose(sums[0:rank, cut]).astype(BF16)
        width = min(channels, 256)
        for w in range(channels // width):
            lanes = slice(w * width, (w + 1) * width)
            raw = jnp.dot(low, step_weight[:, lanes], preferred_element_type=F32)
            raw = raw + params[taps + 1 : taps + 2, lanes]
            size = jnp.maximum(raw, 0.0) + jnp.log(1.0 + jnp.exp(-jnp.abs(raw)))
            times = size * active[cut, lanes].astype(F32)
            for i in range(LANES // 8):
                for j in range(width // LANES):
                    block = (number * LANES // 8 + i) * folds + w * (width // LANES) + j
                    there = slice(block * 8, block * 8 + 8)
                    part = (slice(i * 8, i * 8 + 8), slice(j * LANES, (j + 1) * LANES))
                    steps[there, :] = size[part]
                    scaled[there, :] = times[part]
    copy.wait()

    for first in range(0, folds, group):
        start = tuple(state[fold_rows(s, first), :] for s in range(state_size))

        def eight(number, held):
            base = number * (folds * 8) + first * 8
            held = list(held)
            for r in range(8):
                token = number * 8 + r
                rows = pl.ds(base + r, group, stride=8)
                size, times = steps[rows, :], scaled[rows, :]
                total = None
                for s in range(state_size):
                    rate = rates[s * folds + first : s * folds + first + group, :]
                    held[s] = jnp.exp2(size * rate) * held[s] + times * coef[s, token]
                    term = held[s] * coef[state_size + s, token]
                    total = term if total is None else total + term
                steps[rows, :] = total
            return tuple(held)

        lax.fori_loop(0, tokens // 8, eight, start)

    def unfold(number, carry):
        here = pl.ds(pl.multiple_of(number * 16, 16), 16)
        for j in range(folds):
            lanes = slice(j * LANES, (j + 1) * LANES)
            found = []
            for half in range(2):
                block = pl.multiple_of((number * 2 + half) * (folds * 8) + j * 8, 8)
                found.append(steps[pl.ds(block, 8), :])
            gain = params[taps + 2 : taps + 3, lanes]
            value_out[here, lanes] = jnp.concatenate(found, axis=0) + gain * active[here, lanes].astype(F32)
        return carry

    lax.fori_loop(0, tokens // 16, unfold, 0)


def scan(own, other, active, params, taps, log_rate, step_weight, state_in):
    tokens, channels = active.shape
    state_size = log_rate.shape[0]
    folded = (state_size * channels // LANES, LANES)
    return pl.pallas_call(
        functools.partial(scan_kernel, taps),
        out_shape=jax.ShapeDtypeStruct((tokens, channels), F32),
        in_specs=[WHOLE] * 4 + [FAR] * 3,
        out_specs=WHOLE,
        scratch_shapes=[
            VMEM(own.shape, F32),
            VMEM((tokens * channels // LANES, LANES), F32),
            VMEM((tokens * channels // LANES, LANES), F32),
            VMEM(folded, F32),
            VMEM(folded, F32),
            SMEM((2 * state_size, tokens), F32),
            VMEM(step_weight.shape, BF16),
            VMEM(state_in.shape, F32),
            VMEM(log_rate.shape, F32),
            pltpu.SemaphoreType.DMA((4,)),
        ],
        compiler_params=pltpu.CompilerParams(vmem_limit_bytes=16 << 20),
        cost_estimate=pl.CostEstimate(
            flops=3000 * tokens * channels * state_size,
            bytes_accessed=8 * tokens * channels,
            transcendentals=tokens * channels * state_size,
        ),
        name="scan",
    )(own, other, active, params, far(log_rate), far(step_weight), far(state_in))


def project_kernel(count, columns, places, value_in, weight_hbm, *refs):
    pieces = refs[:count]
    base_out, send_out, routes_out, gated, out_weight, sem = refs[count:]
    copy = pltpu.make_async_copy(weight_hbm, out_weight, sem)
    copy.start()
    tokens, channels = value_in.shape
    rows = pieces[0].shape[0]
    tile = 16
    for index in range(count):
        begin = pl.multiple_of(places[index] * rows, tile)
        routes_out[pl.ds(begin, rows), :] = pieces[index][:, channels + columns :]

        def gate(number, carry):
            local = pl.ds(pl.multiple_of(number * tile, tile), tile)
            here = pl.ds(pl.multiple_of(begin + number * tile, tile), tile)
            z = pieces[index][local, :channels].astype(F32)
            gated[here, :] = (value_in[here, :] * (z / (1.0 + jnp.exp(-z)))).astype(BF16)
            return carry

        lax.fori_loop(0, rows // tile, gate, 0)
    copy.wait()
    for number in range(tokens // LANES):
        cut = slice(number * LANES, (number + 1) * LANES)
        sent = jnp.dot(gated[cut, :], out_weight[...], preferred_element_type=F32).astype(BF16)
        send_out[cut, :] = sent
        base_out[cut, :] = sent.astype(F32)
    for index in range(count):
        here = pl.ds(pl.multiple_of(places[index] * rows, tile), rows)
        base_out[here, :] += pieces[index][:, channels : channels + columns].astype(F32)


def project(places, value, out_weight, pieces):
    tokens, channels = value.shape
    columns = out_weight.shape[1]
    count = len(pieces)
    return pl.pallas_call(
        functools.partial(project_kernel, count, columns),
        out_shape=(
            jax.ShapeDtypeStruct((tokens, columns), F32),
            jax.ShapeDtypeStruct((tokens, columns), BF16),
            jax.ShapeDtypeStruct((tokens, LANES), BF16),
        ),
        in_specs=[SCALARS, WHOLE, FAR] + [WHOLE] * count,
        out_specs=(WHOLE,) * 3,
        scratch_shapes=[
            VMEM((tokens, channels), BF16),
            VMEM(out_weight.shape, BF16),
            pltpu.SemaphoreType.DMA,
        ],
        compiler_params=pltpu.CompilerParams(vmem_limit_bytes=16 << 20),
        cost_estimate=pl.CostEstimate(
            flops=2 * tokens * channels * columns,
            bytes_accessed=8 * tokens * channels,
            transcendentals=tokens * channels,
        ),
        name="project",
    )(places, value, far(out_weight), *pieces)


def mix_kernel(base, summand, mixed):
    mixed[...] = (base[...] + summand[...].astype(F32)).astype(BF16)


def mix(base, summand):
    return pl.pallas_call(
        mix_kernel,
        out_shape=jax.ShapeDtypeStruct(base.shape, BF16),
        in_specs=[WHOLE] * 2,
        out_specs=WHOLE,
        compiler_params=pltpu.CompilerParams(vmem_limit_bytes=4 << 20),
        name="mix",
    )(base, summand)


def norm_kernel(count, places, spots, gain, router, routes, *refs):
    pieces = refs[:count]
    normed, weight, own_rows = refs[count : count + 3]
    mixed = pieces[0] if count == 1 else refs[-1]
    tokens = normed.shape[0]
    columns = pieces[0].shape[1]
    for index in range(count if count > 1 else 0):
        start = pl.multiple_of(places[index] * columns, LANES)
        mixed[:, pl.ds(start, columns)] = pieces[index][...]
    mine = spots[0].astype(F32)
    step = 32

    def block(number, carry):
        cut = pl.ds(pl.multiple_of(number * step, step), step)
        value = mixed[cut, :].astype(F32)
        square = jnp.mean(value * value, axis=-1, keepdims=True) + 1e-06
        scaled = (value * lax.rsqrt(square) * gain[0:1, :]).astype(BF16)
        normed[cut, :] = scaled
        return carry

    lax.fori_loop(0, tokens // step, block, 0)
    for c in range(tokens // LANES):
        cut = slice(c * LANES, (c + 1) * LANES)
        logits = contract_last(normed[cut, :], router[...])
        first = routes[cut, 0:1].astype(F32)
        second = routes[cut, 1:2].astype(F32)
        ids = lax.broadcasted_iota(jnp.int32, logits.shape, 1).astype(F32)
        first_logit = jnp.sum(jnp.where(ids == first, logits, 0.0), axis=1, keepdims=True)
        second_logit = jnp.sum(jnp.where(ids == second, logits, 0.0), axis=1, keepdims=True)
        first_gate = jnp.where(first == mine, 1.0 / (1.0 + jnp.exp(second_logit - first_logit)), 0.0)
        second_gate = jnp.where(second == mine, 1.0 / (1.0 + jnp.exp(first_logit - second_logit)), 0.0)
        weight[cut, :] = jnp.broadcast_to(first_gate + second_gate, (LANES, LANES))
    rows = own_rows.shape[0]
    own_rows[...] = mixed[pl.ds(pl.multiple_of(spots[1] * rows, 16), rows), :]


def norm(places, spots, gain, router, routes, pieces, own):
    count = len(pieces)
    tokens = pieces[0].shape[0]
    width = count * pieces[0].shape[1]
    return pl.pallas_call(
        functools.partial(norm_kernel, count),
        out_shape=(
            jax.ShapeDtypeStruct((tokens, width), BF16),
            jax.ShapeDtypeStruct((tokens, LANES), F32),
            jax.ShapeDtypeStruct((own, width), BF16),
        ),
        in_specs=[SCALARS] * 2 + [WHOLE] * (3 + count),
        out_specs=(WHOLE,) * 3,
        scratch_shapes=[VMEM((tokens, width), BF16)] if count > 1 else [],
        compiler_params=pltpu.CompilerParams(vmem_limit_bytes=8 << 20),
        name="norm",
    )(places, spots, gain, router, routes, *pieces)


def fetch_kernel(parts, half_rows, half, *refs):
    count = len(refs) // 2 - 1
    sources, targets, done, sems = refs[:count], refs[count : 2 * count], refs[-2], refs[-1]
    rows = targets[0].shape[0]
    part = rows // parts
    copies = []
    for index in range(count):
        for k in range(parts):
            start = pl.multiple_of(half[0] * half_rows + k * part, 16)
            copies.append(
                pltpu.make_async_copy(
                    sources[index].at[pl.ds(start, part), :],
                    targets[index].at[pl.ds(k * part, part), :],
                    sems.at[index * parts + k],
                )
            )
    for copy in copies:
        copy.start()
    for copy in copies:
        copy.wait()
    done[0] = half[0]


def fetch(half, weights):
    half_rows, width = weights[0].shape[0] // 2, weights[0].shape[1]
    rows = half_rows // 2
    parts = 4
    return pl.pallas_call(
        functools.partial(fetch_kernel, parts, half_rows),
        out_shape=tuple([VMEM((rows, width), BF16)] * len(weights)) + (jax.ShapeDtypeStruct((1,), jnp.int32),),
        in_specs=[SCALARS] + [FAR] * len(weights),
        out_specs=tuple([WHOLE] * len(weights)) + (SCALARS,),
        scratch_shapes=[pltpu.SemaphoreType.DMA((parts * len(weights),))],
        compiler_params=pltpu.CompilerParams(vmem_limit_bytes=1 << 20),
        cost_estimate=pl.CostEstimate(
            flops=0, bytes_accessed=4 * rows * width * len(weights), transcendentals=0
        ),
        name="fetch",
    )(half, *[far(w) for w in weights])


def shared_kernel(half, own, other, gate_first, up_first, gate, up, down, kept, given, tokens, hidden, late, last, sems):
    rows = own.shape[0]
    quarter, width = gate_first.shape
    begin = half[0] * (2 * quarter)
    copies = []
    for index, (source, offset) in enumerate(((gate, quarter), (up, quarter), (down, 0), (down, quarter))):
        here = pl.ds(pl.multiple_of(begin + offset, 16), quarter)
        target = late.at[index] if index < 2 else last.at[index - 2]
        copies.append(pltpu.make_async_copy(source.at[here, :], target, sems.at[index]))
    for copy in copies:
        copy.start()
    tokens[0:rows, :] = own[...]
    tokens[rows:, :] = other[...]

    def activate_hidden(gate_rows, up_rows, place):
        gate_act = contract_last(tokens[...], gate_rows[...])
        up_act = contract_last(tokens[...], up_rows[...])
        value = gate_act / (1.0 + jnp.exp(-gate_act)) * up_act
        hidden[:, place * quarter : (place + 1) * quarter] = value.astype(BF16)

    activate_hidden(gate_first, up_first, 0)
    copies[0].wait()
    copies[1].wait()
    activate_hidden(late.at[0], late.at[1], 1)
    copies[2].wait()
    copies[3].wait()
    step = 256
    for start in range(0, width, step):
        here = slice(start, start + step)
        product = jnp.dot(hidden[:, :quarter], last[0, :, here], preferred_element_type=F32)
        product += jnp.dot(hidden[:, quarter:], last[1, :, here], preferred_element_type=F32)
        kept[:, here] = product[0:rows, :]
        given[:, here] = product[rows:, :].astype(BF16)


def shared_experts(half, own, other, gate_first, up_first, gate, up, down):
    rows, width = own.shape
    quarter = gate_first.shape[0]
    return pl.pallas_call(
        shared_kernel,
        out_shape=(jax.ShapeDtypeStruct((rows, width), F32), jax.ShapeDtypeStruct((rows, width), BF16)),
        in_specs=[SCALARS] + [WHOLE] * 4 + [FAR] * 3,
        out_specs=(WHOLE,) * 2,
        scratch_shapes=[
            VMEM((2 * rows, width), BF16),
            VMEM((2 * rows, 2 * quarter), BF16),
            VMEM((2, quarter, width), BF16),
            VMEM((2, quarter, width), BF16),
            pltpu.SemaphoreType.DMA((4,)),
        ],
        compiler_params=pltpu.CompilerParams(vmem_limit_bytes=36 << 20),
        cost_estimate=pl.CostEstimate(
            flops=24 * rows * quarter * width,
            bytes_accessed=8 * quarter * width,
            transcendentals=4 * rows * quarter,
        ),
        name="experts",
    )(half, own, other, gate_first, up_first, far(gate), far(up), far(down))


def expert_kernel(tokens, gate, up, down, total):
    number = pl.program_id(0)

    @pl.when(number == 0)
    def _():
        total[...] = jnp.zeros_like(total)

    for start in range(0, total.shape[0], LANES):
        cut = slice(start, start + LANES)
        gate_act = contract_last(tokens[cut, :], gate[...])
        up_act = contract_last(tokens[cut, :], up[...])
        hidden = (gate_act / (1.0 + jnp.exp(-gate_act)) * up_act).astype(BF16)
        total[cut, :] += jnp.dot(hidden, down[...], preferred_element_type=F32)


def experts(tokens, gate, up, down):
    rows, width = tokens.shape
    hidden = gate.shape[0]
    block = hidden if hidden <= 512 else math.gcd(hidden, 512)
    weights = pl.BlockSpec((block, width), lambda i: (i, 0))
    return pl.pallas_call(
        expert_kernel,
        grid=(hidden // block,),
        out_shape=jax.ShapeDtypeStruct((rows, width), F32),
        in_specs=[WHOLE] + [weights] * 3,
        out_specs=WHOLE,
        compiler_params=pltpu.CompilerParams(vmem_limit_bytes=40 << 20),
        cost_estimate=pl.CostEstimate(
            flops=6 * rows * hidden * width,
            bytes_accessed=6 * hidden * width,
            transcendentals=rows * hidden,
        ),
        name="experts",
    )(tokens, gate, up, down)


def combine_kernel(targets, own, other, weight, *outs):
    rows = outs[0].shape[0]
    for index, out in enumerate(outs):
        here = pl.ds(pl.multiple_of(targets[index] * rows, 16), rows)
        out[...] = ((own[here, :] + other[here, :].astype(F32)) * weight[here, 0:1]).astype(BF16)


def combine(targets, own, other, weight, rows):
    width = own.shape[1]
    sends = own.shape[0] // rows
    return pl.pallas_call(
        combine_kernel,
        out_shape=tuple([jax.ShapeDtypeStruct((rows, width), BF16)] * sends),
        in_specs=[SCALARS] + [WHOLE] * 3,
        out_specs=(WHOLE,) * sends,
        compiler_params=pltpu.CompilerParams(vmem_limit_bytes=8 << 20),
        name="combine",
    )(targets, own, other, weight)


def body(
    projected,
    carried_tail,
    carried_state,
    filter_taps,
    filter_bias,
    select_weight,
    step_weight,
    step_bias,
    log_rate,
    skip_gain,
    output_weight,
    residual,
    norm_gain,
    router,
    gate_weight,
    up_weight,
    down_weight,
    routes,
):
    ctx, exp = lax.axis_size("ctx"), lax.axis_size("exp")
    ctx_at, exp_at = lax.axis_index("ctx"), lax.axis_index("exp")
    places = ring_places("ctx")
    x_input, z_input = projected[0], projected[1]
    own, width = residual.shape
    columns = output_weight.shape[1]
    taps = filter_taps.shape[0]
    parts = ctx * exp
    me = ctx_at * exp + exp_at
    spots = jnp.stack([ctx_at // (ctx // EXPERTS), me]).astype(jnp.int32)
    targets = jnp.stack([partner(me, s, parts) for s in range(parts)]).astype(jnp.int32)

    x_pieces = spread(lambda k: x_input, "ctx", 0)
    extra = jnp.concatenate([residual, jnp.pad(routes.astype(BF16), ((0, 0), (0, LANES - 2)))], axis=1)
    if exp == 2:
        other = rotate(extra, "exp", 1)
        extra = jnp.where(
            exp_at == 0,
            jnp.concatenate([extra, other], axis=0),
            jnp.concatenate([other, extra], axis=0),
        )
    else:
        extra = lax.all_gather(extra, "exp", axis=0, tiled=True)
    tail_pad = jnp.zeros((8 - carried_tail.shape[0], carried_tail.shape[1]), F32)
    params = jnp.concatenate(
        [filter_taps, filter_bias[None], step_bias[None], skip_gain[None], jnp.zeros_like(tail_pad)[: 5 - taps],
         tail_pad, carried_tail.astype(F32)]
    )
    ready = [jnp.concatenate([z_input, extra[:, width:]], axis=1), extra[:, :width]]
    router_rows = jnp.pad(router.T, ((0, 16 - EXPERTS), (0, 0)))
    gain = jnp.pad(norm_gain[None, :], ((0, 7), (0, 0)))
    params, router_rows, gain, spots, targets = lax.optimization_barrier(
        (params, router_rows, gain, spots, targets)
    )

    active, proj = activate(places, x_pieces, params, taps, select_weight)
    own_proj, other_proj = pair_sum(proj, "exp")

    def bundle(k):
        piece = lax.dynamic_slice_in_dim(ready[1], k * columns, columns, axis=1)
        channels = z_input.shape[1]
        return jnp.concatenate([ready[0][:, :channels], piece, ready[0][:, channels:]], axis=1)

    z_pieces = spread(bundle, "ctx", 0, active)
    value = scan(own_proj, other_proj, active, params, taps, log_rate, step_weight, carried_state)
    base, sent, all_routes = project(places, value, output_weight, z_pieces)
    shared = parts <= 8 and base.shape[0] == LANES and lax.axis_size("doc") % 2 == 0
    half = lax.rem(lax.axis_index("doc"), 2).astype(jnp.int32)[None]
    if exp == 2:
        summand = rotate(sent, "exp", 1)
    else:
        summand = lax.psum(sent.astype(F32), "exp") - sent.astype(F32)
    if shared:
        half, base = lax.optimization_barrier((half, base))
        gate_first, up_first, half = fetch(half, [gate_weight, up_weight])
        half, base = lax.optimization_barrier((half, base))
    mixed = mix(base, summand)
    mixed_pieces = spread(lambda k: mixed, "ctx", 1)
    normed, weight, mine = norm(places, spots, gain, router_rows, all_routes, mixed_pieces, own)
    total = mine.astype(F32)
    axes = ("ctx", "exp")
    if shared:
        kept, given = shared_experts(half, normed, swap(normed), gate_first, up_first, gate_weight, up_weight, down_weight)
        outs = combine(targets, kept, swap(given), weight, own)
        arrived = [outs[0]]
        for s in range(1, parts):
            arrived.append(exchange(outs[s], axes, s, parts))
        for piece in arrived:
            total = total + piece.astype(F32)
    else:
        kept = experts(normed, gate_weight, up_weight, down_weight)
        partial = (kept * weight[:, :1]).astype(BF16)
        moved = lax.all_to_all(partial, axes, split_axis=0, concat_axis=0, tiled=True)
        total = total + jnp.sum(moved.reshape(parts, own, width).astype(F32), axis=0)
    return total.astype(BF16)


def solution(mesh):
    placed = (
        P(None, ("doc", "ctx"), "exp"),
        P("doc", "exp"),
        P("doc", "exp"),
        P(None, "exp"),
        P("exp"),
        P(None, "exp"),
        P(None, "exp"),
        P("exp"),
        P(None, "exp"),
        P("exp"),
        P("exp", "ctx"),
        P(("doc", "ctx", "exp"), None),
        P(),
        P(),
        P(("ctx", "exp"), None),
        P(("ctx", "exp"), None),
        P(("ctx", "exp"), None),
        P(("doc", "ctx", "exp"), None),
    )
    return jax.shard_map(
        body, mesh=mesh, in_specs=placed, out_specs=P(("doc", "ctx", "exp"), None), check_vma=False
    )
```

```python
import functools
import math

import jax
import jax.numpy as jnp
from jax import lax
from jax.experimental import pallas as pl
from jax.experimental.pallas import tpu as pltpu
from jax.sharding import PartitionSpec as P

EXPERTS = 4
LANES = 128
FEW = 4
LOG2E = 1.4426950408889634
VMEM = pltpu.VMEM
SMEM = pltpu.SMEM
F32 = jnp.float32
BF16 = jnp.bfloat16


def contract_last(left, right):
    return lax.dot_general(left, right, (((1,), (1,)), ((), ())), preferred_element_type=F32)


def rotate(value, axis, steps):
    count = lax.axis_size(axis)
    return lax.ppermute(value, axis, [(i, (i + steps) % count) for i in range(count)])


def partner(place, step, count):
    return (place + step) % count


def source(place, step, count):
    return (place - step) % count


def exchange(value, axes, step, count):
    return lax.ppermute(value, axes, [(i, partner(i, step, count)) for i in range(count)])


def ring_places(axis):
    count = lax.axis_size(axis)
    if count > FEW:
        return jnp.zeros((1,), jnp.int32)
    me = lax.axis_index(axis)
    return jnp.stack([source(me, s, count) for s in range(count)]).astype(jnp.int32)


def spread(make, axis, join, after=None):
    count = lax.axis_size(axis)
    me = lax.axis_index(axis)
    if count <= FEW:
        sent = [make(partner(me, s, count)) for s in range(1, count)]
        if after is not None:
            sent, _ = lax.optimization_barrier((sent, after))
        return [make(me)] + [exchange(sent[s - 1], axis, s, count) for s in range(1, count)]
    stacked = jnp.stack([make(jnp.int32(k)) for k in range(count)])
    moved = lax.all_to_all(stacked, axis, split_axis=0, concat_axis=0, tiled=True)
    return [jnp.concatenate([moved[k] for k in range(count)], axis=join)]


def swap(value):
    count = lax.axis_size("doc")
    return lax.ppermute(value, "doc", [(i, i + 1 - 2 * (i % 2)) for i in range(count)])


def far(value):
    return pltpu.with_memory_space_constraint(value, pltpu.HBM)


def pair_sum(value, axis):
    if lax.axis_size(axis) == 2:
        return [value, rotate(value, axis, 1)]
    total = lax.psum(value.astype(F32), axis).astype(value.dtype)
    return [total, jnp.zeros_like(total)]


FAR = pl.BlockSpec(memory_space=pltpu.HBM)
WHOLE = pl.BlockSpec(memory_space=VMEM)
SCALARS = pl.BlockSpec(memory_space=SMEM)


def activate_kernel(count, taps, places, params, select, *refs):
    pieces, (active, proj, padded, held, sem) = refs[:count], refs[count:]
    copy = pltpu.make_async_copy(select, held, sem)
    copy.start()
    rows = pieces[0].shape[0]
    padded[0:8, :] = params[8:16, :]
    for index in range(count):
        start = pl.multiple_of(8 + places[index] * rows, 8)
        padded[pl.ds(start, rows), :] = pieces[index][...].astype(F32)
    tokens = active.shape[0]
    step = 32

    def block(number, carry):
        base = pl.multiple_of(number * step, step)
        window = padded[pl.ds(base, step + 8), :]
        total = jnp.broadcast_to(params[taps : taps + 1, :], (step, params.shape[1]))
        for k in range(taps):
            offset = 8 - (taps - 1) + k
            total = total + params[k : k + 1, :] * window[offset : offset + step, :]
        value = total / (1.0 + jnp.exp(-total))
        active[pl.ds(base, step), :] = value.astype(BF16)
        return carry

    lax.fori_loop(0, tokens // step, block, 0)
    copy.wait()
    for number in range(tokens // LANES):
        cut = slice(number * LANES, (number + 1) * LANES)
        proj[:, cut] = contract_last(held[...], active[cut, :])


def activate(places, pieces, params, taps, select):
    count = len(pieces)
    tokens = count * pieces[0].shape[0]
    channels = pieces[0].shape[1]
    return pl.pallas_call(
        functools.partial(activate_kernel, count, taps),
        out_shape=(
            jax.ShapeDtypeStruct((tokens, channels), BF16),
            jax.ShapeDtypeStruct((select.shape[0], tokens), F32),
        ),
        in_specs=[SCALARS, WHOLE, FAR] + [WHOLE] * count,
        out_specs=(WHOLE,) * 2,
        scratch_shapes=[
            VMEM((tokens + 8, channels), F32),
            VMEM(select.shape, BF16),
            pltpu.SemaphoreType.DMA,
        ],
        compiler_params=pltpu.CompilerParams(vmem_limit_bytes=12 << 20),
        cost_estimate=pl.CostEstimate(
            flops=2 * tokens * channels * select.shape[0],
            bytes_accessed=4 * tokens * channels,
            transcendentals=tokens * channels,
        ),
        name="activate",
    )(places, params, far(select), *pieces)


def scan_kernel(
    taps, own, other, active, params, log_rate_hbm, step_weight_hbm, state_hbm, value_out,
    sums, steps, scaled, rates, state, coef, step_weight, state_in, log_rate, sems,
):
    tokens, channels = active.shape
    rank = step_weight.shape[0]
    state_size = log_rate.shape[0]
    folds = channels // LANES
    group = min(folds, 16)
    load_weight = pltpu.make_async_copy(step_weight_hbm, step_weight, sems.at[0])
    load_state = pltpu.make_async_copy(state_hbm, state_in, sems.at[1])
    load_rate = pltpu.make_async_copy(log_rate_hbm, log_rate, sems.at[3])
    load_rate.start()
    load_state.start()
    load_weight.start()
    sums[...] = own[...] + other[...]
    copy = pltpu.make_async_copy(sums.at[pl.ds(rank, 2 * state_size), :], coef, sems.at[2])
    copy.start()

    def scatter(target, source):
        for s8 in range(state_size // 8):
            for j in range(folds):
                lanes = slice(j * LANES, (j + 1) * LANES)
                there = slice((s8 * folds + j) * 8, (s8 * folds + j) * 8 + 8)
                target[there, :] = source[s8 * 8 : s8 * 8 + 8, lanes]

    def fold_rows(row, first):
        return pl.ds((row // 8) * (folds * 8) + row % 8 + first * 8, group, stride=8)

    load_rate.wait()
    scatter(state, log_rate)
    for s in range(state_size):
        for first in range(0, folds, group):
            rates[s * folds + first : s * folds + first + group, :] = (
                jnp.exp(state[fold_rows(s, first), :]) * (-LOG2E)
            )
    load_state.wait()
    scatter(state, state_in)
    load_weight.wait()

    for number in range(tokens // LANES):
        cut = slice(number * LANES, (number + 1) * LANES)
        low = jnp.transpose(sums[0:rank, cut]).astype(BF16)
        width = min(channels, 256)
        for w in range(channels // width):
            lanes = slice(w * width, (w + 1) * width)
            raw = jnp.dot(low, step_weight[:, lanes], preferred_element_type=F32)
            raw = raw + params[taps + 1 : taps + 2, lanes]
            size = jnp.maximum(raw, 0.0) + jnp.log(1.0 + jnp.exp(-jnp.abs(raw)))
            times = size * active[cut, lanes].astype(F32)
            for i in range(LANES // 8):
                for j in range(width // LANES):
                    block = (number * LANES // 8 + i) * folds + w * (width // LANES) + j
                    there = slice(block * 8, block * 8 + 8)
                    part = (slice(i * 8, i * 8 + 8), slice(j * LANES, (j + 1) * LANES))
                    steps[there, :] = size[part]
                    scaled[there, :] = times[part]
    copy.wait()

    for first in range(0, folds, group):
        start = tuple(state[fold_rows(s, first), :] for s in range(state_size))

        def eight(number, held):
            base = number * (folds * 8) + first * 8
            held = list(held)
            for r in range(8):
                token = number * 8 + r
                rows = pl.ds(base + r, group, stride=8)
                size, times = steps[rows, :], scaled[rows, :]
                total = None
                for s in range(state_size):
                    rate = rates[s * folds + first : s * folds + first + group, :]
                    held[s] = jnp.exp2(size * rate) * held[s] + times * coef[s, token]
                    term = held[s] * coef[state_size + s, token]
                    total = term if total is None else total + term
                steps[rows, :] = total
            return tuple(held)

        lax.fori_loop(0, tokens // 8, eight, start)

    def unfold(number, carry):
        here = pl.ds(pl.multiple_of(number * 16, 16), 16)
        for j in range(folds):
            lanes = slice(j * LANES, (j + 1) * LANES)
            found = []
            for half in range(2):
                block = pl.multiple_of((number * 2 + half) * (folds * 8) + j * 8, 8)
                found.append(steps[pl.ds(block, 8), :])
            gain = params[taps + 2 : taps + 3, lanes]
            value_out[here, lanes] = jnp.concatenate(found, axis=0) + gain * active[here, lanes].astype(F32)
        return carry

    lax.fori_loop(0, tokens // 16, unfold, 0)


def scan(own, other, active, params, taps, log_rate, step_weight, state_in):
    tokens, channels = active.shape
    state_size = log_rate.shape[0]
    folded = (state_size * channels // LANES, LANES)
    return pl.pallas_call(
        functools.partial(scan_kernel, taps),
        out_shape=jax.ShapeDtypeStruct((tokens, channels), F32),
        in_specs=[WHOLE] * 4 + [FAR] * 3,
        out_specs=WHOLE,
        scratch_shapes=[
            VMEM(own.shape, F32),
            VMEM((tokens * channels // LANES, LANES), F32),
            VMEM((tokens * channels // LANES, LANES), F32),
            VMEM(folded, F32),
            VMEM(folded, F32),
            SMEM((2 * state_size, tokens), F32),
            VMEM(step_weight.shape, BF16),
            VMEM(state_in.shape, F32),
            VMEM(log_rate.shape, F32),
            pltpu.SemaphoreType.DMA((4,)),
        ],
        compiler_params=pltpu.CompilerParams(vmem_limit_bytes=16 << 20),
        cost_estimate=pl.CostEstimate(
            flops=3000 * tokens * channels * state_size,
            bytes_accessed=8 * tokens * channels,
            transcendentals=tokens * channels * state_size,
        ),
        name="scan",
    )(own, other, active, params, far(log_rate), far(step_weight), far(state_in))


def project_kernel(count, columns, splits, places, value_in, weight_hbm, *refs):
    pieces = refs[:count]
    send_out, routes_out, base_out, gated, out_weight, sem = refs[count:]
    lanes = columns // splits
    copy = pltpu.make_async_copy(weight_hbm, out_weight, sem)
    copy.start()
    tokens, channels = value_in.shape
    rows = pieces[0].shape[0]
    tile = 16
    for index in range(count):
        begin = pl.multiple_of(places[index] * rows, tile)
        routes_out[pl.ds(begin, rows), :] = pieces[index][:, channels + lanes :]

        def gate(number, carry):
            local = pl.ds(pl.multiple_of(number * tile, tile), tile)
            here = pl.ds(pl.multiple_of(begin + number * tile, tile), tile)
            z = pieces[index][local, :channels].astype(F32)
            gated[here, :] = (value_in[here, :] * (z / (1.0 + jnp.exp(-z)))).astype(BF16)
            return carry

        lax.fori_loop(0, rows // tile, gate, 0)
    copy.wait()
    for number in range(tokens // LANES):
        cut = slice(number * LANES, (number + 1) * LANES)
        base_out[cut, :] = jnp.dot(gated[cut, :], out_weight[...], preferred_element_type=F32)
    part = rows // splits
    for index in range(count):
        begin = places[index] * rows + (places[count] * part if splits > 1 else 0)
        here = pl.ds(pl.multiple_of(begin, tile), part)
        for k in range(splits):
            piece = pieces[index][k * part : (k + 1) * part, channels : channels + lanes]
            base_out[here, k * lanes : (k + 1) * lanes] += piece.astype(F32)
    for number in range(tokens // LANES):
        cut = slice(number * LANES, (number + 1) * LANES)
        send_out[cut, :] = base_out[cut, :].astype(BF16)


def project(places, value, out_weight, pieces, splits):
    tokens, channels = value.shape
    columns = out_weight.shape[1]
    count = len(pieces)
    return pl.pallas_call(
        functools.partial(project_kernel, count, columns, splits),
        out_shape=(
            jax.ShapeDtypeStruct((tokens, columns), BF16),
            jax.ShapeDtypeStruct((tokens, LANES), BF16),
        ),
        in_specs=[SCALARS, WHOLE, FAR] + [WHOLE] * count,
        out_specs=(WHOLE,) * 2,
        scratch_shapes=[
            VMEM((tokens, columns), F32),
            VMEM((tokens, channels), BF16),
            VMEM(out_weight.shape, BF16),
            pltpu.SemaphoreType.DMA,
        ],
        compiler_params=pltpu.CompilerParams(vmem_limit_bytes=16 << 20),
        cost_estimate=pl.CostEstimate(
            flops=2 * tokens * channels * columns,
            bytes_accessed=8 * tokens * channels,
            transcendentals=tokens * channels,
        ),
        name="project",
    )(places, value, far(out_weight), *pieces)


def mix_kernel(base, summand, mixed):
    mixed[...] = (base[...].astype(F32) + summand[...].astype(F32)).astype(BF16)


def mix(base, summand):
    return pl.pallas_call(
        mix_kernel,
        out_shape=jax.ShapeDtypeStruct(base.shape, BF16),
        in_specs=[WHOLE] * 2,
        out_specs=WHOLE,
        compiler_params=pltpu.CompilerParams(vmem_limit_bytes=4 << 20),
        name="mix",
    )(base, summand)


def norm_kernel(count, places, spots, gain, router, routes, *refs):
    pieces = refs[:count]
    normed, weight, own_rows = refs[count : count + 3]
    mixed = pieces[0] if count == 1 else refs[-1]
    tokens = normed.shape[0]
    columns = pieces[0].shape[1]
    for index in range(count if count > 1 else 0):
        start = pl.multiple_of(places[index] * columns, LANES)
        mixed[:, pl.ds(start, columns)] = pieces[index][...]
    mine = spots[0].astype(F32)
    step = 32

    def block(number, carry):
        cut = pl.ds(pl.multiple_of(number * step, step), step)
        value = mixed[cut, :].astype(F32)
        square = jnp.mean(value * value, axis=-1, keepdims=True) + 1e-06
        scaled = (value * lax.rsqrt(square) * gain[0:1, :]).astype(BF16)
        normed[cut, :] = scaled
        return carry

    lax.fori_loop(0, tokens // step, block, 0)
    for c in range(tokens // LANES):
        cut = slice(c * LANES, (c + 1) * LANES)
        logits = contract_last(normed[cut, :], router[...])
        first = routes[cut, 0:1].astype(F32)
        second = routes[cut, 1:2].astype(F32)
        ids = lax.broadcasted_iota(jnp.int32, logits.shape, 1).astype(F32)
        first_logit = jnp.sum(jnp.where(ids == first, logits, 0.0), axis=1, keepdims=True)
        second_logit = jnp.sum(jnp.where(ids == second, logits, 0.0), axis=1, keepdims=True)
        first_gate = jnp.where(first == mine, 1.0 / (1.0 + jnp.exp(second_logit - first_logit)), 0.0)
        second_gate = jnp.where(second == mine, 1.0 / (1.0 + jnp.exp(first_logit - second_logit)), 0.0)
        weight[cut, :] = jnp.broadcast_to(first_gate + second_gate, (LANES, LANES))
    rows = own_rows.shape[0]
    own_rows[...] = mixed[pl.ds(pl.multiple_of(spots[1] * rows, 16), rows), :]


def norm(places, spots, gain, router, routes, pieces, own):
    count = len(pieces)
    tokens = pieces[0].shape[0]
    width = count * pieces[0].shape[1]
    return pl.pallas_call(
        functools.partial(norm_kernel, count),
        out_shape=(
            jax.ShapeDtypeStruct((tokens, width), BF16),
            jax.ShapeDtypeStruct((tokens, LANES), F32),
            jax.ShapeDtypeStruct((own, width), BF16),
        ),
        in_specs=[SCALARS] * 2 + [WHOLE] * (3 + count),
        out_specs=(WHOLE,) * 3,
        scratch_shapes=[VMEM((tokens, width), BF16)] if count > 1 else [],
        compiler_params=pltpu.CompilerParams(vmem_limit_bytes=8 << 20),
        name="norm",
    )(places, spots, gain, router, routes, *pieces)


def fetch_kernel(parts, half_rows, half, *refs):
    count = len(refs) // 2 - 1
    sources, targets, done, sems = refs[:count], refs[count : 2 * count], refs[-2], refs[-1]
    rows = targets[0].shape[0]
    part = rows // parts
    copies = []
    for index in range(count):
        for k in range(parts):
            start = pl.multiple_of(half[0] * half_rows + k * part, 16)
            copies.append(
                pltpu.make_async_copy(
                    sources[index].at[pl.ds(start, part), :],
                    targets[index].at[pl.ds(k * part, part), :],
                    sems.at[index * parts + k],
                )
            )
    for copy in copies:
        copy.start()
    for copy in copies:
        copy.wait()
    done[0] = half[0]


def fetch(half, weights):
    half_rows, width = weights[0].shape[0] // 2, weights[0].shape[1]
    rows = half_rows // 2
    parts = 4
    return pl.pallas_call(
        functools.partial(fetch_kernel, parts, half_rows),
        out_shape=tuple([VMEM((rows, width), BF16)] * len(weights)) + (jax.ShapeDtypeStruct((1,), jnp.int32),),
        in_specs=[SCALARS] + [FAR] * len(weights),
        out_specs=tuple([WHOLE] * len(weights)) + (SCALARS,),
        scratch_shapes=[pltpu.SemaphoreType.DMA((parts * len(weights),))],
        compiler_params=pltpu.CompilerParams(vmem_limit_bytes=1 << 20),
        cost_estimate=pl.CostEstimate(
            flops=0, bytes_accessed=4 * rows * width * len(weights), transcendentals=0
        ),
        name="fetch",
    )(half, *[far(w) for w in weights])


def shared_kernel(half, own, other, gate_first, up_first, gate, up, down, kept, given, tokens, hidden, late, last, sems):
    rows = own.shape[0]
    quarter, width = gate_first.shape
    begin = half[0] * (2 * quarter)
    copies = []
    for index, (source, offset) in enumerate(((gate, quarter), (up, quarter), (down, 0), (down, quarter))):
        here = pl.ds(pl.multiple_of(begin + offset, 16), quarter)
        target = late.at[index] if index < 2 else last.at[index - 2]
        copies.append(pltpu.make_async_copy(source.at[here, :], target, sems.at[index]))
    for copy in copies:
        copy.start()
    tokens[0:rows, :] = own[...]
    tokens[rows:, :] = other[...]

    def activate_hidden(gate_rows, up_rows, place):
        gate_act = contract_last(tokens[...], gate_rows[...])
        up_act = contract_last(tokens[...], up_rows[...])
        value = gate_act / (1.0 + jnp.exp(-gate_act)) * up_act
        hidden[:, place * quarter : (place + 1) * quarter] = value.astype(BF16)

    activate_hidden(gate_first, up_first, 0)
    copies[0].wait()
    copies[1].wait()
    activate_hidden(late.at[0], late.at[1], 1)
    copies[2].wait()
    copies[3].wait()
    step = 256
    for start in range(0, width, step):
        here = slice(start, start + step)
        product = jnp.dot(hidden[:, :quarter], last[0, :, here], preferred_element_type=F32)
        product += jnp.dot(hidden[:, quarter:], last[1, :, here], preferred_element_type=F32)
        kept[:, here] = product[0:rows, :]
        given[:, here] = product[rows:, :].astype(BF16)


def shared_experts(half, own, other, gate_first, up_first, gate, up, down):
    rows, width = own.shape
    quarter = gate_first.shape[0]
    return pl.pallas_call(
        shared_kernel,
        out_shape=(jax.ShapeDtypeStruct((rows, width), F32), jax.ShapeDtypeStruct((rows, width), BF16)),
        in_specs=[SCALARS] + [WHOLE] * 4 + [FAR] * 3,
        out_specs=(WHOLE,) * 2,
        scratch_shapes=[
            VMEM((2 * rows, width), BF16),
            VMEM((2 * rows, 2 * quarter), BF16),
            VMEM((2, quarter, width), BF16),
            VMEM((2, quarter, width), BF16),
            pltpu.SemaphoreType.DMA((4,)),
        ],
        compiler_params=pltpu.CompilerParams(vmem_limit_bytes=36 << 20),
        cost_estimate=pl.CostEstimate(
            flops=24 * rows * quarter * width,
            bytes_accessed=8 * quarter * width,
            transcendentals=4 * rows * quarter,
        ),
        name="experts",
    )(half, own, other, gate_first, up_first, far(gate), far(up), far(down))


def expert_kernel(tokens, gate, up, down, total):
    number = pl.program_id(0)

    @pl.when(number == 0)
    def _():
        total[...] = jnp.zeros_like(total)

    for start in range(0, total.shape[0], LANES):
        cut = slice(start, start + LANES)
        gate_act = contract_last(tokens[cut, :], gate[...])
        up_act = contract_last(tokens[cut, :], up[...])
        hidden = (gate_act / (1.0 + jnp.exp(-gate_act)) * up_act).astype(BF16)
        total[cut, :] += jnp.dot(hidden, down[...], preferred_element_type=F32)


def experts(tokens, gate, up, down):
    rows, width = tokens.shape
    hidden = gate.shape[0]
    block = hidden if hidden <= 512 else math.gcd(hidden, 512)
    weights = pl.BlockSpec((block, width), lambda i: (i, 0))
    return pl.pallas_call(
        expert_kernel,
        grid=(hidden // block,),
        out_shape=jax.ShapeDtypeStruct((rows, width), F32),
        in_specs=[WHOLE] + [weights] * 3,
        out_specs=WHOLE,
        compiler_params=pltpu.CompilerParams(vmem_limit_bytes=40 << 20),
        cost_estimate=pl.CostEstimate(
            flops=6 * rows * hidden * width,
            bytes_accessed=6 * hidden * width,
            transcendentals=rows * hidden,
        ),
        name="experts",
    )(tokens, gate, up, down)


def combine_kernel(targets, own, other, weight, *outs):
    rows = outs[0].shape[0]
    for index, out in enumerate(outs):
        here = pl.ds(pl.multiple_of(targets[index] * rows, 16), rows)
        out[...] = ((own[here, :] + other[here, :].astype(F32)) * weight[here, 0:1]).astype(BF16)


def combine(targets, own, other, weight, rows):
    width = own.shape[1]
    sends = own.shape[0] // rows
    return pl.pallas_call(
        combine_kernel,
        out_shape=tuple([jax.ShapeDtypeStruct((rows, width), BF16)] * sends),
        in_specs=[SCALARS] + [WHOLE] * 3,
        out_specs=(WHOLE,) * sends,
        compiler_params=pltpu.CompilerParams(vmem_limit_bytes=8 << 20),
        name="combine",
    )(targets, own, other, weight)


def body(
    projected,
    carried_tail,
    carried_state,
    filter_taps,
    filter_bias,
    select_weight,
    step_weight,
    step_bias,
    log_rate,
    skip_gain,
    output_weight,
    residual,
    norm_gain,
    router,
    gate_weight,
    up_weight,
    down_weight,
    routes,
):
    ctx, exp = lax.axis_size("ctx"), lax.axis_size("exp")
    ctx_at, exp_at = lax.axis_index("ctx"), lax.axis_index("exp")
    places = ring_places("ctx")
    x_input, z_input = projected[0], projected[1]
    own, width = residual.shape
    columns = output_weight.shape[1]
    taps = filter_taps.shape[0]
    parts = ctx * exp
    me = ctx_at * exp + exp_at
    spots = jnp.stack([ctx_at // (ctx // EXPERTS), me]).astype(jnp.int32)
    targets = jnp.stack([partner(me, s, parts) for s in range(parts)]).astype(jnp.int32)

    x_pieces = spread(lambda k: x_input, "ctx", 0)
    extra = jnp.pad(routes.astype(BF16), ((0, 0), (0, LANES - 2)))
    if exp == 2:
        other = rotate(extra, "exp", 1)
        extra = jnp.where(
            exp_at == 0,
            jnp.concatenate([extra, other], axis=0),
            jnp.concatenate([other, extra], axis=0),
        )
    else:
        extra = lax.all_gather(jnp.concatenate([residual, extra], axis=1), "exp", axis=0, tiled=True)
    tail_pad = jnp.zeros((8 - carried_tail.shape[0], carried_tail.shape[1]), F32)
    params = jnp.concatenate(
        [filter_taps, filter_bias[None], step_bias[None], skip_gain[None], jnp.zeros_like(tail_pad)[: 5 - taps],
         tail_pad, carried_tail.astype(F32)]
    )
    router_rows = jnp.pad(router.T, ((0, 16 - EXPERTS), (0, 0)))
    gain = jnp.pad(norm_gain[None, :], ((0, 7), (0, 0)))
    params, router_rows, gain, spots, targets = lax.optimization_barrier(
        (params, router_rows, gain, spots, targets)
    )

    active, proj = activate(places, x_pieces, params, taps, select_weight)
    own_proj, other_proj = pair_sum(proj, "exp")

    splits = exp if exp == 2 else 1

    def bundle(k):
        rows = residual if splits > 1 else jnp.where(exp_at == 0, extra[:, :width], 0)
        piece = lax.dynamic_slice_in_dim(rows, k * columns, columns, axis=1)
        lanes = columns // splits
        piece = jnp.concatenate([piece[:, i * lanes : (i + 1) * lanes] for i in range(splits)], axis=0)
        return jnp.concatenate([z_input, piece, extra[:, -LANES:]], axis=1)

    z_pieces = spread(bundle, "ctx", 0, active)
    value = scan(own_proj, other_proj, active, params, taps, log_rate, step_weight, carried_state)
    spread_places = jnp.concatenate([places, exp_at.astype(jnp.int32)[None]])
    sent, all_routes = project(spread_places, value, output_weight, z_pieces, splits)
    shared = exp == 2 and parts <= 8 and sent.shape[0] == LANES and lax.axis_size("doc") % 2 == 0
    half = lax.rem(lax.axis_index("doc"), 2).astype(jnp.int32)[None]
    if exp == 2:
        summand = rotate(sent, "exp", 1)
        if shared:
            half, sent = lax.optimization_barrier((half, sent))
            gate_first, up_first, half = fetch(half, [gate_weight, up_weight])
            half, sent = lax.optimization_barrier((half, sent))
        mixed = mix(sent, summand)
    else:
        mixed = lax.psum(sent.astype(F32), "exp").astype(BF16)
    mixed_pieces = spread(lambda k: mixed, "ctx", 1)
    normed, weight, mine = norm(places, spots, gain, router_rows, all_routes, mixed_pieces, own)
    total = mine.astype(F32)
    axes = ("ctx", "exp")
    if shared:
        kept, given = shared_experts(half, normed, swap(normed), gate_first, up_first, gate_weight, up_weight, down_weight)
        outs = combine(targets, kept, swap(given), weight, own)
        arrived = [outs[0]]
        for s in range(1, parts):
            arrived.append(exchange(outs[s], axes, s, parts))
        for piece in arrived:
            total = total + piece.astype(F32)
    else:
        kept = experts(normed, gate_weight, up_weight, down_weight)
        partial = (kept * weight[:, :1]).astype(BF16)
        moved = lax.all_to_all(partial, axes, split_axis=0, concat_axis=0, tiled=True)
        total = total + jnp.sum(moved.reshape(parts, own, width).astype(F32), axis=0)
    return total.astype(BF16)


def solution(mesh):
    placed = (
        P(None, ("doc", "ctx"), "exp"),
        P("doc", "exp"),
        P("doc", "exp"),
        P(None, "exp"),
        P("exp"),
        P(None, "exp"),
        P(None, "exp"),
        P("exp"),
        P(None, "exp"),
        P("exp"),
        P("exp", "ctx"),
        P(("doc", "ctx", "exp"), None),
        P(),
        P(),
        P(("ctx", "exp"), None),
        P(("ctx", "exp"), None),
        P(("ctx", "exp"), None),
        P(("doc", "ctx", "exp"), None),
    )
    return jax.shard_map(
        body, mesh=mesh, in_specs=placed, out_specs=P(("doc", "ctx", "exp"), None), check_vma=False
    )
```

```python
import functools
import math

import jax
import jax.numpy as jnp
from jax import lax
from jax.experimental import pallas as pl
from jax.experimental.pallas import tpu as pltpu
from jax.sharding import PartitionSpec as P

EXPERTS = 4
LANES = 128
FEW = 4
LOG2E = 1.4426950408889634
VMEM = pltpu.VMEM
SMEM = pltpu.SMEM
F32 = jnp.float32
BF16 = jnp.bfloat16


def contract_last(left, right):
    return lax.dot_general(left, right, (((1,), (1,)), ((), ())), preferred_element_type=F32)


def rotate(value, axis, steps):
    count = lax.axis_size(axis)
    return lax.ppermute(value, axis, [(i, (i + steps) % count) for i in range(count)])


def partner(place, step, count):
    paired = count & (count - 1) == 0
    return place ^ step if paired else (place + step) % count


def source(place, step, count):
    paired = count & (count - 1) == 0
    return place ^ step if paired else (place - step) % count


def exchange(value, axis, step, count):
    return lax.ppermute(value, axis, [(i, partner(i, step, count)) for i in range(count)])


def ring_places(axis):
    count = lax.axis_size(axis)
    if count > FEW:
        return jnp.zeros((1,), jnp.int32)
    me = lax.axis_index(axis)
    return jnp.stack([source(me, s, count) for s in range(count)]).astype(jnp.int32)


def spread(make, axis, join, after=None):
    count = lax.axis_size(axis)
    me = lax.axis_index(axis)
    if count <= FEW:
        sent = [make(partner(me, s, count)) for s in range(1, count)]
        if after is not None:
            sent, _ = lax.optimization_barrier((sent, after))
        return [make(me)] + [exchange(sent[s - 1], axis, s, count) for s in range(1, count)]
    stacked = jnp.stack([make(jnp.int32(k)) for k in range(count)])
    moved = lax.all_to_all(stacked, axis, split_axis=0, concat_axis=0, tiled=True)
    return [jnp.concatenate([moved[k] for k in range(count)], axis=join)]


def swap(value):
    count = lax.axis_size("doc")
    return lax.ppermute(value, "doc", [(i, i + 1 - 2 * (i % 2)) for i in range(count)])


def far(value):
    return pltpu.with_memory_space_constraint(value, pltpu.HBM)


def pair_sum(value, axis):
    if lax.axis_size(axis) == 2:
        return [value, rotate(value, axis, 1)]
    total = lax.psum(value.astype(F32), axis).astype(value.dtype)
    return [total, jnp.zeros_like(total)]


FAR = pl.BlockSpec(memory_space=pltpu.HBM)
WHOLE = pl.BlockSpec(memory_space=VMEM)
SCALARS = pl.BlockSpec(memory_space=SMEM)


def activate_kernel(count, taps, places, params, select, *refs):
    pieces, (active, proj, padded, held, sem) = refs[:count], refs[count:]
    copy = pltpu.make_async_copy(select, held, sem)
    copy.start()
    rows = pieces[0].shape[0]
    padded[0:8, :] = params[8:16, :]
    for index in range(count):
        start = pl.multiple_of(8 + places[index] * rows, 8)
        padded[pl.ds(start, rows), :] = pieces[index][...].astype(F32)
    tokens = active.shape[0]
    step = 32

    def block(number, carry):
        base = pl.multiple_of(number * step, step)
        window = padded[pl.ds(base, step + 8), :]
        total = jnp.broadcast_to(params[taps : taps + 1, :], (step, params.shape[1]))
        for k in range(taps):
            offset = 8 - (taps - 1) + k
            total = total + params[k : k + 1, :] * window[offset : offset + step, :]
        value = total / (1.0 + jnp.exp(-total))
        active[pl.ds(base, step), :] = value.astype(BF16)
        return carry

    lax.fori_loop(0, tokens // step, block, 0)
    copy.wait()
    for number in range(tokens // LANES):
        cut = slice(number * LANES, (number + 1) * LANES)
        proj[:, cut] = contract_last(held[...], active[cut, :])


def activate(places, pieces, params, taps, select):
    count = len(pieces)
    tokens = count * pieces[0].shape[0]
    channels = pieces[0].shape[1]
    return pl.pallas_call(
        functools.partial(activate_kernel, count, taps),
        out_shape=(
            jax.ShapeDtypeStruct((tokens, channels), BF16),
            jax.ShapeDtypeStruct((select.shape[0], tokens), F32),
        ),
        in_specs=[SCALARS, WHOLE, FAR] + [WHOLE] * count,
        out_specs=(WHOLE,) * 2,
        scratch_shapes=[
            VMEM((tokens + 8, channels), F32),
            VMEM(select.shape, BF16),
            pltpu.SemaphoreType.DMA,
        ],
        compiler_params=pltpu.CompilerParams(vmem_limit_bytes=12 << 20),
        cost_estimate=pl.CostEstimate(
            flops=2 * tokens * channels * select.shape[0],
            bytes_accessed=4 * tokens * channels,
            transcendentals=tokens * channels,
        ),
        name="activate",
    )(places, params, far(select), *pieces)


def scan_kernel(
    taps, own, other, active, params, log_rate_hbm, step_weight_hbm, state_hbm, value_out,
    sums, steps, scaled, rates, state, coef, step_weight, state_in, log_rate, sems,
):
    tokens, channels = active.shape
    rank = step_weight.shape[0]
    state_size = log_rate.shape[0]
    folds = channels // LANES
    group = min(folds, 16)
    load_weight = pltpu.make_async_copy(step_weight_hbm, step_weight, sems.at[0])
    load_state = pltpu.make_async_copy(state_hbm, state_in, sems.at[1])
    load_rate = pltpu.make_async_copy(log_rate_hbm, log_rate, sems.at[3])
    load_rate.start()
    load_state.start()
    load_weight.start()
    sums[...] = own[...] + other[...]
    copy = pltpu.make_async_copy(sums.at[pl.ds(rank, 2 * state_size), :], coef, sems.at[2])
    copy.start()

    def scatter(target, source):
        for s8 in range(state_size // 8):
            for j in range(folds):
                lanes = slice(j * LANES, (j + 1) * LANES)
                there = slice((s8 * folds + j) * 8, (s8 * folds + j) * 8 + 8)
                target[there, :] = source[s8 * 8 : s8 * 8 + 8, lanes]

    def fold_rows(row, first):
        return pl.ds((row // 8) * (folds * 8) + row % 8 + first * 8, group, stride=8)

    load_rate.wait()
    scatter(state, log_rate)
    for s in range(state_size):
        for first in range(0, folds, group):
            rates[s * folds + first : s * folds + first + group, :] = (
                jnp.exp(state[fold_rows(s, first), :]) * (-LOG2E)
            )
    load_state.wait()
    scatter(state, state_in)
    load_weight.wait()

    for number in range(tokens // LANES):
        cut = slice(number * LANES, (number + 1) * LANES)
        low = jnp.transpose(sums[0:rank, cut]).astype(BF16)
        width = min(channels, 256)
        for w in range(channels // width):
            lanes = slice(w * width, (w + 1) * width)
            raw = jnp.dot(low, step_weight[:, lanes], preferred_element_type=F32)
            raw = raw + params[taps + 1 : taps + 2, lanes]
            size = jnp.maximum(raw, 0.0) + jnp.log(1.0 + jnp.exp(-jnp.abs(raw)))
            times = size * active[cut, lanes].astype(F32)
            for i in range(LANES // 8):
                for j in range(width // LANES):
                    block = (number * LANES // 8 + i) * folds + w * (width // LANES) + j
                    there = slice(block * 8, block * 8 + 8)
                    part = (slice(i * 8, i * 8 + 8), slice(j * LANES, (j + 1) * LANES))
                    steps[there, :] = size[part]
                    scaled[there, :] = times[part]
    copy.wait()

    for first in range(0, folds, group):
        start = tuple(state[fold_rows(s, first), :] for s in range(state_size))

        def eight(number, held):
            base = number * (folds * 8) + first * 8
            held = list(held)
            for r in range(8):
                token = number * 8 + r
                rows = pl.ds(base + r, group, stride=8)
                size, times = steps[rows, :], scaled[rows, :]
                total = None
                for s in range(state_size):
                    rate = rates[s * folds + first : s * folds + first + group, :]
                    held[s] = jnp.exp2(size * rate) * held[s] + times * coef[s, token]
                    term = held[s] * coef[state_size + s, token]
                    total = term if total is None else total + term
                steps[rows, :] = total
            return tuple(held)

        lax.fori_loop(0, tokens // 8, eight, start)

    def unfold(number, carry):
        here = pl.ds(pl.multiple_of(number * 16, 16), 16)
        for j in range(folds):
            lanes = slice(j * LANES, (j + 1) * LANES)
            found = []
            for half in range(2):
                block = pl.multiple_of((number * 2 + half) * (folds * 8) + j * 8, 8)
                found.append(steps[pl.ds(block, 8), :])
            gain = params[taps + 2 : taps + 3, lanes]
            value_out[here, lanes] = jnp.concatenate(found, axis=0) + gain * active[here, lanes].astype(F32)
        return carry

    lax.fori_loop(0, tokens // 16, unfold, 0)


def scan(own, other, active, params, taps, log_rate, step_weight, state_in):
    tokens, channels = active.shape
    state_size = log_rate.shape[0]
    folded = (state_size * channels // LANES, LANES)
    return pl.pallas_call(
        functools.partial(scan_kernel, taps),
        out_shape=jax.ShapeDtypeStruct((tokens, channels), F32),
        in_specs=[WHOLE] * 4 + [FAR] * 3,
        out_specs=WHOLE,
        scratch_shapes=[
            VMEM(own.shape, F32),
            VMEM((tokens * channels // LANES, LANES), F32),
            VMEM((tokens * channels // LANES, LANES), F32),
            VMEM(folded, F32),
            VMEM(folded, F32),
            SMEM((2 * state_size, tokens), F32),
            VMEM(step_weight.shape, BF16),
            VMEM(state_in.shape, F32),
            VMEM(log_rate.shape, F32),
            pltpu.SemaphoreType.DMA((4,)),
        ],
        compiler_params=pltpu.CompilerParams(vmem_limit_bytes=16 << 20),
        cost_estimate=pl.CostEstimate(
            flops=3000 * tokens * channels * state_size,
            bytes_accessed=8 * tokens * channels,
            transcendentals=tokens * channels * state_size,
        ),
        name="scan",
    )(own, other, active, params, far(log_rate), far(step_weight), far(state_in))


def project_kernel(count, columns, splits, places, value_in, weight_hbm, *refs):
    pieces = refs[:count]
    send_out, routes_out, base_out, gated, out_weight, sem = refs[count:]
    lanes = columns // splits
    copy = pltpu.make_async_copy(weight_hbm, out_weight, sem)
    copy.start()
    tokens, channels = value_in.shape
    rows = pieces[0].shape[0]
    tile = 16
    for index in range(count):
        begin = pl.multiple_of(places[index] * rows, tile)
        routes_out[pl.ds(begin, rows), :] = pieces[index][:, channels + lanes :]

        def gate(number, carry):
            local = pl.ds(pl.multiple_of(number * tile, tile), tile)
            here = pl.ds(pl.multiple_of(begin + number * tile, tile), tile)
            z = pieces[index][local, :channels].astype(F32)
            gated[here, :] = (value_in[here, :] * (z / (1.0 + jnp.exp(-z)))).astype(BF16)
            return carry

        lax.fori_loop(0, rows // tile, gate, 0)
    copy.wait()
    for number in range(tokens // LANES):
        cut = slice(number * LANES, (number + 1) * LANES)
        base_out[cut, :] = jnp.dot(gated[cut, :], out_weight[...], preferred_element_type=F32)
    part = rows // splits
    for index in range(count):
        begin = places[index] * rows + (places[count] * part if splits > 1 else 0)
        here = pl.ds(pl.multiple_of(begin, tile), part)
        for k in range(splits):
            piece = pieces[index][k * part : (k + 1) * part, channels : channels + lanes]
            base_out[here, k * lanes : (k + 1) * lanes] += piece.astype(F32)
    for number in range(tokens // LANES):
        cut = slice(number * LANES, (number + 1) * LANES)
        send_out[cut, :] = base_out[cut, :].astype(BF16)


def project(places, value, out_weight, pieces, splits):
    tokens, channels = value.shape
    columns = out_weight.shape[1]
    count = len(pieces)
    return pl.pallas_call(
        functools.partial(project_kernel, count, columns, splits),
        out_shape=(
            jax.ShapeDtypeStruct((tokens, columns), BF16),
            jax.ShapeDtypeStruct((tokens, LANES), BF16),
        ),
        in_specs=[SCALARS, WHOLE, FAR] + [WHOLE] * count,
        out_specs=(WHOLE,) * 2,
        scratch_shapes=[
            VMEM((tokens, columns), F32),
            VMEM((tokens, channels), BF16),
            VMEM(out_weight.shape, BF16),
            pltpu.SemaphoreType.DMA,
        ],
        compiler_params=pltpu.CompilerParams(vmem_limit_bytes=16 << 20),
        cost_estimate=pl.CostEstimate(
            flops=2 * tokens * channels * columns,
            bytes_accessed=8 * tokens * channels,
            transcendentals=tokens * channels,
        ),
        name="project",
    )(places, value, far(out_weight), *pieces)


def mix_kernel(base, summand, mixed):
    mixed[...] = (base[...].astype(F32) + summand[...].astype(F32)).astype(BF16)


def mix(base, summand):
    return pl.pallas_call(
        mix_kernel,
        out_shape=jax.ShapeDtypeStruct(base.shape, BF16),
        in_specs=[WHOLE] * 2,
        out_specs=WHOLE,
        compiler_params=pltpu.CompilerParams(vmem_limit_bytes=4 << 20),
        name="mix",
    )(base, summand)


def norm_kernel(count, places, spots, gain, router, routes, *refs):
    pieces = refs[:count]
    normed, weight, own_rows = refs[count : count + 3]
    mixed = pieces[0] if count == 1 else refs[-1]
    tokens = normed.shape[0]
    columns = pieces[0].shape[1]
    for index in range(count if count > 1 else 0):
        start = pl.multiple_of(places[index] * columns, LANES)
        mixed[:, pl.ds(start, columns)] = pieces[index][...]
    mine = spots[0].astype(F32)
    step = 32

    def block(number, carry):
        cut = pl.ds(pl.multiple_of(number * step, step), step)
        value = mixed[cut, :].astype(F32)
        square = jnp.mean(value * value, axis=-1, keepdims=True) + 1e-06
        scaled = (value * lax.rsqrt(square) * gain[0:1, :]).astype(BF16)
        normed[cut, :] = scaled
        return carry

    lax.fori_loop(0, tokens // step, block, 0)
    for c in range(tokens // LANES):
        cut = slice(c * LANES, (c + 1) * LANES)
        logits = contract_last(normed[cut, :], router[...])
        first = routes[cut, 0:1].astype(F32)
        second = routes[cut, 1:2].astype(F32)
        ids = lax.broadcasted_iota(jnp.int32, logits.shape, 1).astype(F32)
        first_logit = jnp.sum(jnp.where(ids == first, logits, 0.0), axis=1, keepdims=True)
        second_logit = jnp.sum(jnp.where(ids == second, logits, 0.0), axis=1, keepdims=True)
        first_gate = jnp.where(first == mine, 1.0 / (1.0 + jnp.exp(second_logit - first_logit)), 0.0)
        second_gate = jnp.where(second == mine, 1.0 / (1.0 + jnp.exp(first_logit - second_logit)), 0.0)
        weight[cut, :] = jnp.broadcast_to(first_gate + second_gate, (LANES, LANES))
    rows = own_rows.shape[0]
    own_rows[...] = mixed[pl.ds(pl.multiple_of(spots[1] * rows, 16), rows), :]


def norm(places, spots, gain, router, routes, pieces, own):
    count = len(pieces)
    tokens = pieces[0].shape[0]
    width = count * pieces[0].shape[1]
    return pl.pallas_call(
        functools.partial(norm_kernel, count),
        out_shape=(
            jax.ShapeDtypeStruct((tokens, width), BF16),
            jax.ShapeDtypeStruct((tokens, LANES), F32),
            jax.ShapeDtypeStruct((own, width), BF16),
        ),
        in_specs=[SCALARS] * 2 + [WHOLE] * (3 + count),
        out_specs=(WHOLE,) * 3,
        scratch_shapes=[VMEM((tokens, width), BF16)] if count > 1 else [],
        compiler_params=pltpu.CompilerParams(vmem_limit_bytes=8 << 20),
        name="norm",
    )(places, spots, gain, router, routes, *pieces)


def fetch_kernel(parts, half_rows, half, *refs):
    count = len(refs) // 2 - 1
    sources, targets, done, sems = refs[:count], refs[count : 2 * count], refs[-2], refs[-1]
    rows = targets[0].shape[0]
    part = rows // parts
    copies = []
    for index in range(count):
        for k in range(parts):
            start = pl.multiple_of(half[0] * half_rows + k * part, 16)
            copies.append(
                pltpu.make_async_copy(
                    sources[index].at[pl.ds(start, part), :],
                    targets[index].at[pl.ds(k * part, part), :],
                    sems.at[index * parts + k],
                )
            )
    for copy in copies:
        copy.start()
    for copy in copies:
        copy.wait()
    done[0] = half[0]


def fetch(half, weights):
    half_rows, width = weights[0].shape[0] // 2, weights[0].shape[1]
    rows = half_rows // 2
    parts = 4
    return pl.pallas_call(
        functools.partial(fetch_kernel, parts, half_rows),
        out_shape=tuple([VMEM((rows, width), BF16)] * len(weights)) + (jax.ShapeDtypeStruct((1,), jnp.int32),),
        in_specs=[SCALARS] + [FAR] * len(weights),
        out_specs=tuple([WHOLE] * len(weights)) + (SCALARS,),
        scratch_shapes=[pltpu.SemaphoreType.DMA((parts * len(weights),))],
        compiler_params=pltpu.CompilerParams(vmem_limit_bytes=1 << 20),
        cost_estimate=pl.CostEstimate(
            flops=0, bytes_accessed=4 * rows * width * len(weights), transcendentals=0
        ),
        name="fetch",
    )(half, *[far(w) for w in weights])


def shared_kernel(half, own, other, gate_first, up_first, gate, up, down, kept, given, tokens, hidden, late, last, sems):
    rows = own.shape[0]
    quarter, width = gate_first.shape
    begin = half[0] * (2 * quarter)
    copies = []
    for index, (source, offset) in enumerate(((gate, quarter), (up, quarter), (down, 0), (down, quarter))):
        here = pl.ds(pl.multiple_of(begin + offset, 16), quarter)
        target = late.at[index] if index < 2 else last.at[index - 2]
        copies.append(pltpu.make_async_copy(source.at[here, :], target, sems.at[index]))
    for copy in copies:
        copy.start()
    tokens[0:rows, :] = own[...]
    tokens[rows:, :] = other[...]

    def activate_hidden(gate_rows, up_rows, place):
        gate_act = contract_last(tokens[...], gate_rows[...])
        up_act = contract_last(tokens[...], up_rows[...])
        value = gate_act / (1.0 + jnp.exp(-gate_act)) * up_act
        hidden[:, place * quarter : (place + 1) * quarter] = value.astype(BF16)

    activate_hidden(gate_first, up_first, 0)
    copies[0].wait()
    copies[1].wait()
    activate_hidden(late.at[0], late.at[1], 1)
    copies[2].wait()
    copies[3].wait()
    step = 256
    for start in range(0, width, step):
        here = slice(start, start + step)
        product = jnp.dot(hidden[:, :quarter], last[0, :, here], preferred_element_type=F32)
        product += jnp.dot(hidden[:, quarter:], last[1, :, here], preferred_element_type=F32)
        kept[:, here] = product[0:rows, :]
        given[:, here] = product[rows:, :].astype(BF16)


def shared_experts(half, own, other, gate_first, up_first, gate, up, down):
    rows, width = own.shape
    quarter = gate_first.shape[0]
    return pl.pallas_call(
        shared_kernel,
        out_shape=(jax.ShapeDtypeStruct((rows, width), F32), jax.ShapeDtypeStruct((rows, width), BF16)),
        in_specs=[SCALARS] + [WHOLE] * 4 + [FAR] * 3,
        out_specs=(WHOLE,) * 2,
        scratch_shapes=[
            VMEM((2 * rows, width), BF16),
            VMEM((2 * rows, 2 * quarter), BF16),
            VMEM((2, quarter, width), BF16),
            VMEM((2, quarter, width), BF16),
            pltpu.SemaphoreType.DMA((4,)),
        ],
        compiler_params=pltpu.CompilerParams(vmem_limit_bytes=36 << 20),
        cost_estimate=pl.CostEstimate(
            flops=24 * rows * quarter * width,
            bytes_accessed=8 * quarter * width,
            transcendentals=4 * rows * quarter,
        ),
        name="experts",
    )(half, own, other, gate_first, up_first, far(gate), far(up), far(down))


def expert_kernel(tokens, gate, up, down, total):
    number = pl.program_id(0)

    @pl.when(number == 0)
    def _():
        total[...] = jnp.zeros_like(total)

    for start in range(0, total.shape[0], LANES):
        cut = slice(start, start + LANES)
        gate_act = contract_last(tokens[cut, :], gate[...])
        up_act = contract_last(tokens[cut, :], up[...])
        hidden = (gate_act / (1.0 + jnp.exp(-gate_act)) * up_act).astype(BF16)
        total[cut, :] += jnp.dot(hidden, down[...], preferred_element_type=F32)


def experts(tokens, gate, up, down):
    rows, width = tokens.shape
    hidden = gate.shape[0]
    block = hidden if hidden <= 512 else math.gcd(hidden, 512)
    weights = pl.BlockSpec((block, width), lambda i: (i, 0))
    return pl.pallas_call(
        expert_kernel,
        grid=(hidden // block,),
        out_shape=jax.ShapeDtypeStruct((rows, width), F32),
        in_specs=[WHOLE] + [weights] * 3,
        out_specs=WHOLE,
        compiler_params=pltpu.CompilerParams(vmem_limit_bytes=40 << 20),
        cost_estimate=pl.CostEstimate(
            flops=6 * rows * hidden * width,
            bytes_accessed=6 * hidden * width,
            transcendentals=rows * hidden,
        ),
        name="experts",
    )(tokens, gate, up, down)


def combine_kernel(targets, own, other, weight, *outs):
    rows = outs[0].shape[0]
    for index, out in enumerate(outs):
        here = pl.ds(pl.multiple_of(targets[index] * rows, 16), rows)
        out[...] = ((own[here, :] + other[here, :].astype(F32)) * weight[here, 0:1]).astype(BF16)


def combine(targets, own, other, weight, rows):
    width = own.shape[1]
    sends = own.shape[0] // rows
    return pl.pallas_call(
        combine_kernel,
        out_shape=tuple([jax.ShapeDtypeStruct((rows, width), BF16)] * sends),
        in_specs=[SCALARS] + [WHOLE] * 3,
        out_specs=(WHOLE,) * sends,
        compiler_params=pltpu.CompilerParams(vmem_limit_bytes=8 << 20),
        name="combine",
    )(targets, own, other, weight)


def body(
    projected,
    carried_tail,
    carried_state,
    filter_taps,
    filter_bias,
    select_weight,
    step_weight,
    step_bias,
    log_rate,
    skip_gain,
    output_weight,
    residual,
    norm_gain,
    router,
    gate_weight,
    up_weight,
    down_weight,
    routes,
):
    ctx, exp = lax.axis_size("ctx"), lax.axis_size("exp")
    ctx_at, exp_at = lax.axis_index("ctx"), lax.axis_index("exp")
    places = ring_places("ctx")
    x_input, z_input = projected[0], projected[1]
    own, width = residual.shape
    columns = output_weight.shape[1]
    taps = filter_taps.shape[0]
    parts = ctx * exp
    me = ctx_at * exp + exp_at
    spots = jnp.stack([ctx_at // (ctx // EXPERTS), me]).astype(jnp.int32)
    targets = jnp.stack([(me + s) % parts for s in range(parts)]).astype(jnp.int32)

    x_pieces = spread(lambda k: x_input, "ctx", 0)
    extra = jnp.pad(routes.astype(BF16), ((0, 0), (0, LANES - 2)))
    if exp == 2:
        other = rotate(extra, "exp", 1)
        extra = jnp.where(
            exp_at == 0,
            jnp.concatenate([extra, other], axis=0),
            jnp.concatenate([other, extra], axis=0),
        )
    else:
        extra = lax.all_gather(jnp.concatenate([residual, extra], axis=1), "exp", axis=0, tiled=True)
    tail_pad = jnp.zeros((8 - carried_tail.shape[0], carried_tail.shape[1]), F32)
    params = jnp.concatenate(
        [filter_taps, filter_bias[None], step_bias[None], skip_gain[None], jnp.zeros_like(tail_pad)[: 5 - taps],
         tail_pad, carried_tail.astype(F32)]
    )
    router_rows = jnp.pad(router.T, ((0, 16 - EXPERTS), (0, 0)))
    gain = jnp.pad(norm_gain[None, :], ((0, 7), (0, 0)))
    params, router_rows, gain, spots, targets = lax.optimization_barrier(
        (params, router_rows, gain, spots, targets)
    )

    active, proj = activate(places, x_pieces, params, taps, select_weight)
    own_proj, other_proj = pair_sum(proj, "exp")

    splits = exp if exp == 2 else 1

    def bundle(k):
        rows = residual if splits > 1 else jnp.where(exp_at == 0, extra[:, :width], 0)
        piece = lax.dynamic_slice_in_dim(rows, k * columns, columns, axis=1)
        lanes = columns // splits
        piece = jnp.concatenate([piece[:, i * lanes : (i + 1) * lanes] for i in range(splits)], axis=0)
        return jnp.concatenate([z_input, piece, extra[:, -LANES:]], axis=1)

    z_pieces = spread(bundle, "ctx", 0, active)
    value = scan(own_proj, other_proj, active, params, taps, log_rate, step_weight, carried_state)
    spread_places = jnp.concatenate([places, exp_at.astype(jnp.int32)[None]])
    sent, all_routes = project(spread_places, value, output_weight, z_pieces, splits)
    shared = exp == 2 and parts <= 8 and sent.shape[0] == LANES and lax.axis_size("doc") % 2 == 0
    half = lax.rem(lax.axis_index("doc"), 2).astype(jnp.int32)[None]
    if exp == 2:
        summand = rotate(sent, "exp", 1)
        if shared:
            half, sent = lax.optimization_barrier((half, sent))
            gate_first, up_first, half = fetch(half, [gate_weight, up_weight])
            half, sent = lax.optimization_barrier((half, sent))
        mixed = mix(sent, summand)
    else:
        mixed = lax.psum(sent.astype(F32), "exp").astype(BF16)
    mixed_pieces = spread(lambda k: mixed, "ctx", 1)
    normed, weight, mine = norm(places, spots, gain, router_rows, all_routes, mixed_pieces, own)
    total = mine.astype(F32)
    axes = ("ctx", "exp")
    if shared:
        kept, given = shared_experts(half, normed, swap(normed), gate_first, up_first, gate_weight, up_weight, down_weight)
        outs = combine(targets, kept, swap(given), weight, own)
        arrived = [outs[0]]
        for s in range(1, parts):
            arrived.append(lax.ppermute(outs[s], axes, [(i, (i + s) % parts) for i in range(parts)]))
        for piece in arrived:
            total = total + piece.astype(F32)
    else:
        kept = experts(normed, gate_weight, up_weight, down_weight)
        partial = (kept * weight[:, :1]).astype(BF16)
        moved = lax.all_to_all(partial, axes, split_axis=0, concat_axis=0, tiled=True)
        total = total + jnp.sum(moved.reshape(parts, own, width).astype(F32), axis=0)
    return total.astype(BF16)


def solution(mesh):
    placed = (
        P(None, ("doc", "ctx"), "exp"),
        P("doc", "exp"),
        P("doc", "exp"),
        P(None, "exp"),
        P("exp"),
        P(None, "exp"),
        P(None, "exp"),
        P("exp"),
        P(None, "exp"),
        P("exp"),
        P("exp", "ctx"),
        P(("doc", "ctx", "exp"), None),
        P(),
        P(),
        P(("ctx", "exp"), None),
        P(("ctx", "exp"), None),
        P(("ctx", "exp"), None),
        P(("doc", "ctx", "exp"), None),
    )
    return jax.shard_map(
        body, mesh=mesh, in_specs=placed, out_specs=P(("doc", "ctx", "exp"), None), check_vma=False
    )
```

```python
import functools
import math

import jax
import jax.numpy as jnp
from jax import lax
from jax.experimental import pallas as pl
from jax.experimental.pallas import tpu as pltpu
from jax.sharding import PartitionSpec as P

EXPERTS = 4
LANES = 128
FEW = 4
LOG2E = 1.4426950408889634
VMEM = pltpu.VMEM
SMEM = pltpu.SMEM
F32 = jnp.float32
BF16 = jnp.bfloat16


def contract_last(left, right):
    return lax.dot_general(left, right, (((1,), (1,)), ((), ())), preferred_element_type=F32)


def rotate(value, axis, steps):
    count = lax.axis_size(axis)
    return lax.ppermute(value, axis, [(i, (i + steps) % count) for i in range(count)])


def partner(place, step, count):
    paired = count & (count - 1) == 0
    return place ^ step if paired else (place + step) % count


def source(place, step, count):
    paired = count & (count - 1) == 0
    return place ^ step if paired else (place - step) % count


def exchange(value, axis, step, count):
    return lax.ppermute(value, axis, [(i, partner(i, step, count)) for i in range(count)])


def ring_places(axis):
    count = lax.axis_size(axis)
    if count > FEW:
        return jnp.zeros((1,), jnp.int32)
    me = lax.axis_index(axis)
    return jnp.stack([source(me, s, count) for s in range(count)]).astype(jnp.int32)


def spread(make, axis, join, after=None):
    count = lax.axis_size(axis)
    me = lax.axis_index(axis)
    if count <= FEW:
        sent = [make(partner(me, s, count)) for s in range(1, count)]
        if after is not None:
            sent, _ = lax.optimization_barrier((sent, after))
        return [make(me)] + [exchange(sent[s - 1], axis, s, count) for s in range(1, count)]
    stacked = jnp.stack([make(jnp.int32(k)) for k in range(count)])
    moved = lax.all_to_all(stacked, axis, split_axis=0, concat_axis=0, tiled=True)
    return [jnp.concatenate([moved[k] for k in range(count)], axis=join)]


def swap(value):
    count = lax.axis_size("doc")
    return lax.ppermute(value, "doc", [(i, i + 1 - 2 * (i % 2)) for i in range(count)])


def far(value):
    return pltpu.with_memory_space_constraint(value, pltpu.HBM)


def pair_sum(value, axis):
    if lax.axis_size(axis) == 2:
        return [value, rotate(value, axis, 1)]
    total = lax.psum(value.astype(F32), axis).astype(value.dtype)
    return [total, jnp.zeros_like(total)]


FAR = pl.BlockSpec(memory_space=pltpu.HBM)
WHOLE = pl.BlockSpec(memory_space=VMEM)
SCALARS = pl.BlockSpec(memory_space=SMEM)


def activate_kernel(count, taps, places, params, select, *refs):
    pieces, (active, proj, padded, held, sem) = refs[:count], refs[count:]
    copy = pltpu.make_async_copy(select, held, sem)
    copy.start()
    rows = pieces[0].shape[0]
    padded[0:8, :] = params[8:16, :]
    for index in range(count):
        start = pl.multiple_of(8 + places[index] * rows, 8)
        padded[pl.ds(start, rows), :] = pieces[index][...].astype(F32)
    tokens = active.shape[0]
    step = 32

    def block(number, carry):
        base = pl.multiple_of(number * step, step)
        window = padded[pl.ds(base, step + 8), :]
        total = jnp.broadcast_to(params[taps : taps + 1, :], (step, params.shape[1]))
        for k in range(taps):
            offset = 8 - (taps - 1) + k
            total = total + params[k : k + 1, :] * window[offset : offset + step, :]
        value = total / (1.0 + jnp.exp(-total))
        active[pl.ds(base, step), :] = value.astype(BF16)
        return carry

    lax.fori_loop(0, tokens // step, block, 0)
    copy.wait()
    for number in range(tokens // LANES):
        cut = slice(number * LANES, (number + 1) * LANES)
        proj[:, cut] = contract_last(held[...], active[cut, :])


def activate(places, pieces, params, taps, select):
    count = len(pieces)
    tokens = count * pieces[0].shape[0]
    channels = pieces[0].shape[1]
    return pl.pallas_call(
        functools.partial(activate_kernel, count, taps),
        out_shape=(
            jax.ShapeDtypeStruct((tokens, channels), BF16),
            jax.ShapeDtypeStruct((select.shape[0], tokens), F32),
        ),
        in_specs=[SCALARS, WHOLE, FAR] + [WHOLE] * count,
        out_specs=(WHOLE,) * 2,
        scratch_shapes=[
            VMEM((tokens + 8, channels), F32),
            VMEM(select.shape, BF16),
            pltpu.SemaphoreType.DMA,
        ],
        compiler_params=pltpu.CompilerParams(vmem_limit_bytes=12 << 20),
        cost_estimate=pl.CostEstimate(
            flops=2 * tokens * channels * select.shape[0],
            bytes_accessed=4 * tokens * channels,
            transcendentals=tokens * channels,
        ),
        name="activate",
    )(places, params, far(select), *pieces)


def scan_kernel(
    taps, own, other, active, params, log_rate_hbm, step_weight_hbm, state_hbm, value_out,
    sums, steps, scaled, rates, state, coef, step_weight, state_in, log_rate, sems,
):
    tokens, channels = active.shape
    rank = step_weight.shape[0]
    state_size = log_rate.shape[0]
    folds = channels // LANES
    group = min(folds, 16)
    load_weight = pltpu.make_async_copy(step_weight_hbm, step_weight, sems.at[0])
    load_state = pltpu.make_async_copy(state_hbm, state_in, sems.at[1])
    load_rate = pltpu.make_async_copy(log_rate_hbm, log_rate, sems.at[3])
    load_rate.start()
    load_state.start()
    load_weight.start()
    sums[...] = own[...] + other[...]
    copy = pltpu.make_async_copy(sums.at[pl.ds(rank, 2 * state_size), :], coef, sems.at[2])
    copy.start()

    def scatter(target, source):
        for s8 in range(state_size // 8):
            for j in range(folds):
                lanes = slice(j * LANES, (j + 1) * LANES)
                there = slice((s8 * folds + j) * 8, (s8 * folds + j) * 8 + 8)
                target[there, :] = source[s8 * 8 : s8 * 8 + 8, lanes]

    def fold_rows(row, first):
        return pl.ds((row // 8) * (folds * 8) + row % 8 + first * 8, group, stride=8)

    load_rate.wait()
    scatter(state, log_rate)
    for s in range(state_size):
        for first in range(0, folds, group):
            rates[s * folds + first : s * folds + first + group, :] = (
                jnp.exp(state[fold_rows(s, first), :]) * (-LOG2E)
            )
    load_state.wait()
    scatter(state, state_in)
    load_weight.wait()

    for number in range(tokens // LANES):
        cut = slice(number * LANES, (number + 1) * LANES)
        low = jnp.transpose(sums[0:rank, cut]).astype(BF16)
        width = min(channels, 256)
        for w in range(channels // width):
            lanes = slice(w * width, (w + 1) * width)
            raw = jnp.dot(low, step_weight[:, lanes], preferred_element_type=F32)
            raw = raw + params[taps + 1 : taps + 2, lanes]
            size = jnp.maximum(raw, 0.0) + jnp.log(1.0 + jnp.exp(-jnp.abs(raw)))
            times = size * active[cut, lanes].astype(F32)
            for i in range(LANES // 8):
                for j in range(width // LANES):
                    block = (number * LANES // 8 + i) * folds + w * (width // LANES) + j
                    there = slice(block * 8, block * 8 + 8)
                    part = (slice(i * 8, i * 8 + 8), slice(j * LANES, (j + 1) * LANES))
                    steps[there, :] = size[part]
                    scaled[there, :] = times[part]
    copy.wait()

    for first in range(0, folds, group):
        start = tuple(state[fold_rows(s, first), :] for s in range(state_size))

        def eight(number, held):
            base = number * (folds * 8) + first * 8
            held = list(held)
            for r in range(8):
                token = number * 8 + r
                rows = pl.ds(base + r, group, stride=8)
                size, times = steps[rows, :], scaled[rows, :]
                total = None
                for s in range(state_size):
                    rate = rates[s * folds + first : s * folds + first + group, :]
                    held[s] = jnp.exp2(size * rate) * held[s] + times * coef[s, token]
                    term = held[s] * coef[state_size + s, token]
                    total = term if total is None else total + term
                steps[rows, :] = total
            return tuple(held)

        lax.fori_loop(0, tokens // 8, eight, start)

    def unfold(number, carry):
        here = pl.ds(pl.multiple_of(number * 16, 16), 16)
        for j in range(folds):
            lanes = slice(j * LANES, (j + 1) * LANES)
            found = []
            for half in range(2):
                block = pl.multiple_of((number * 2 + half) * (folds * 8) + j * 8, 8)
                found.append(steps[pl.ds(block, 8), :])
            gain = params[taps + 2 : taps + 3, lanes]
            value_out[here, lanes] = jnp.concatenate(found, axis=0) + gain * active[here, lanes].astype(F32)
        return carry

    lax.fori_loop(0, tokens // 16, unfold, 0)


def scan(own, other, active, params, taps, log_rate, step_weight, state_in):
    tokens, channels = active.shape
    state_size = log_rate.shape[0]
    folded = (state_size * channels // LANES, LANES)
    return pl.pallas_call(
        functools.partial(scan_kernel, taps),
        out_shape=jax.ShapeDtypeStruct((tokens, channels), F32),
        in_specs=[WHOLE] * 4 + [FAR] * 3,
        out_specs=WHOLE,
        scratch_shapes=[
            VMEM(own.shape, F32),
            VMEM((tokens * channels // LANES, LANES), F32),
            VMEM((tokens * channels // LANES, LANES), F32),
            VMEM(folded, F32),
            VMEM(folded, F32),
            SMEM((2 * state_size, tokens), F32),
            VMEM(step_weight.shape, BF16),
            VMEM(state_in.shape, F32),
            VMEM(log_rate.shape, F32),
            pltpu.SemaphoreType.DMA((4,)),
        ],
        compiler_params=pltpu.CompilerParams(vmem_limit_bytes=16 << 20),
        cost_estimate=pl.CostEstimate(
            flops=3000 * tokens * channels * state_size,
            bytes_accessed=8 * tokens * channels,
            transcendentals=tokens * channels * state_size,
        ),
        name="scan",
    )(own, other, active, params, far(log_rate), far(step_weight), far(state_in))


def project_kernel(count, columns, splits, places, value_in, weight_hbm, *refs):
    pieces = refs[:count]
    send_out, routes_out, base_out, gated, out_weight, sem = refs[count:]
    lanes = columns // splits
    copy = pltpu.make_async_copy(weight_hbm, out_weight, sem)
    copy.start()
    tokens, channels = value_in.shape
    rows = pieces[0].shape[0]
    tile = 16
    for index in range(count):
        begin = pl.multiple_of(places[index] * rows, tile)
        routes_out[pl.ds(begin, rows), :] = pieces[index][:, channels + lanes :]

        def gate(number, carry):
            local = pl.ds(pl.multiple_of(number * tile, tile), tile)
            here = pl.ds(pl.multiple_of(begin + number * tile, tile), tile)
            z = pieces[index][local, :channels].astype(F32)
            gated[here, :] = (value_in[here, :] * (z / (1.0 + jnp.exp(-z)))).astype(BF16)
            return carry

        lax.fori_loop(0, rows // tile, gate, 0)
    copy.wait()
    for number in range(tokens // LANES):
        cut = slice(number * LANES, (number + 1) * LANES)
        base_out[cut, :] = jnp.dot(gated[cut, :], out_weight[...], preferred_element_type=F32)
    part = rows // splits
    for index in range(count):
        begin = places[index] * rows + (places[count] * part if splits > 1 else 0)
        here = pl.ds(pl.multiple_of(begin, tile), part)
        for k in range(splits):
            piece = pieces[index][k * part : (k + 1) * part, channels : channels + lanes]
            base_out[here, k * lanes : (k + 1) * lanes] += piece.astype(F32)
    for number in range(tokens // LANES):
        cut = slice(number * LANES, (number + 1) * LANES)
        send_out[cut, :] = base_out[cut, :].astype(BF16)


def project(places, value, out_weight, pieces, splits):
    tokens, channels = value.shape
    columns = out_weight.shape[1]
    count = len(pieces)
    return pl.pallas_call(
        functools.partial(project_kernel, count, columns, splits),
        out_shape=(
            jax.ShapeDtypeStruct((tokens, columns), BF16),
            jax.ShapeDtypeStruct((tokens, LANES), BF16),
        ),
        in_specs=[SCALARS, WHOLE, FAR] + [WHOLE] * count,
        out_specs=(WHOLE,) * 2,
        scratch_shapes=[
            VMEM((tokens, columns), F32),
            VMEM((tokens, channels), BF16),
            VMEM(out_weight.shape, BF16),
            pltpu.SemaphoreType.DMA,
        ],
        compiler_params=pltpu.CompilerParams(vmem_limit_bytes=16 << 20),
        cost_estimate=pl.CostEstimate(
            flops=2 * tokens * channels * columns,
            bytes_accessed=8 * tokens * channels,
            transcendentals=tokens * channels,
        ),
        name="project",
    )(places, value, far(out_weight), *pieces)


def mix_kernel(base, summand, mixed):
    mixed[...] = (base[...].astype(F32) + summand[...].astype(F32)).astype(BF16)


def mix(base, summand):
    return pl.pallas_call(
        mix_kernel,
        out_shape=jax.ShapeDtypeStruct(base.shape, BF16),
        in_specs=[WHOLE] * 2,
        out_specs=WHOLE,
        compiler_params=pltpu.CompilerParams(vmem_limit_bytes=4 << 20),
        name="mix",
    )(base, summand)


def norm_kernel(count, places, spots, gain, router, routes, *refs):
    pieces = refs[:count]
    normed, weight, own_rows = refs[count : count + 3]
    mixed = pieces[0] if count == 1 else refs[-1]
    tokens = normed.shape[0]
    columns = pieces[0].shape[1]
    for index in range(count if count > 1 else 0):
        start = pl.multiple_of(places[index] * columns, LANES)
        mixed[:, pl.ds(start, columns)] = pieces[index][...]
    mine = spots[0].astype(F32)
    step = 32

    def block(number, carry):
        cut = pl.ds(pl.multiple_of(number * step, step), step)
        value = mixed[cut, :].astype(F32)
        square = jnp.mean(value * value, axis=-1, keepdims=True) + 1e-06
        scaled = (value * lax.rsqrt(square) * gain[0:1, :]).astype(BF16)
        normed[cut, :] = scaled
        return carry

    lax.fori_loop(0, tokens // step, block, 0)
    for c in range(tokens // LANES):
        cut = slice(c * LANES, (c + 1) * LANES)
        logits = contract_last(normed[cut, :], router[...])
        first = routes[cut, 0:1].astype(F32)
        second = routes[cut, 1:2].astype(F32)
        ids = lax.broadcasted_iota(jnp.int32, logits.shape, 1).astype(F32)
        first_logit = jnp.sum(jnp.where(ids == first, logits, 0.0), axis=1, keepdims=True)
        second_logit = jnp.sum(jnp.where(ids == second, logits, 0.0), axis=1, keepdims=True)
        first_gate = jnp.where(first == mine, 1.0 / (1.0 + jnp.exp(second_logit - first_logit)), 0.0)
        second_gate = jnp.where(second == mine, 1.0 / (1.0 + jnp.exp(first_logit - second_logit)), 0.0)
        weight[cut, :] = jnp.broadcast_to(first_gate + second_gate, (LANES, LANES))
    rows = own_rows.shape[0]
    own_rows[...] = mixed[pl.ds(pl.multiple_of(spots[1] * rows, 16), rows), :]


def norm(places, spots, gain, router, routes, pieces, own):
    count = len(pieces)
    tokens = pieces[0].shape[0]
    width = count * pieces[0].shape[1]
    return pl.pallas_call(
        functools.partial(norm_kernel, count),
        out_shape=(
            jax.ShapeDtypeStruct((tokens, width), BF16),
            jax.ShapeDtypeStruct((tokens, LANES), F32),
            jax.ShapeDtypeStruct((own, width), BF16),
        ),
        in_specs=[SCALARS] * 2 + [WHOLE] * (3 + count),
        out_specs=(WHOLE,) * 3,
        scratch_shapes=[VMEM((tokens, width), BF16)] if count > 1 else [],
        compiler_params=pltpu.CompilerParams(vmem_limit_bytes=8 << 20),
        name="norm",
    )(places, spots, gain, router, routes, *pieces)


def fetch_kernel(parts, half_rows, half, *refs):
    count = len(refs) // 2 - 1
    sources, targets, done, sems = refs[:count], refs[count : 2 * count], refs[-2], refs[-1]
    rows = targets[0].shape[0]
    part = rows // parts
    copies = []
    for index in range(count):
        for k in range(parts):
            start = pl.multiple_of(half[0] * half_rows + k * part, 16)
            copies.append(
                pltpu.make_async_copy(
                    sources[index].at[pl.ds(start, part), :],
                    targets[index].at[pl.ds(k * part, part), :],
                    sems.at[index * parts + k],
                )
            )
    for copy in copies:
        copy.start()
    for copy in copies:
        copy.wait()
    done[0] = half[0]


def fetch(half, weights):
    half_rows, width = weights[0].shape[0] // 2, weights[0].shape[1]
    rows = half_rows // 2
    parts = 4
    return pl.pallas_call(
        functools.partial(fetch_kernel, parts, half_rows),
        out_shape=tuple([VMEM((rows, width), BF16)] * len(weights)) + (jax.ShapeDtypeStruct((1,), jnp.int32),),
        in_specs=[SCALARS] + [FAR] * len(weights),
        out_specs=tuple([WHOLE] * len(weights)) + (SCALARS,),
        scratch_shapes=[pltpu.SemaphoreType.DMA((parts * len(weights),))],
        compiler_params=pltpu.CompilerParams(vmem_limit_bytes=1 << 20),
        cost_estimate=pl.CostEstimate(
            flops=0, bytes_accessed=4 * rows * width * len(weights), transcendentals=0
        ),
        name="fetch",
    )(half, *[far(w) for w in weights])


def shared_kernel(half, own, other, gate_first, up_first, gate, up, down, kept, given, tokens, hidden, late, last, sems):
    rows = own.shape[0]
    quarter, width = gate_first.shape
    begin = half[0] * (2 * quarter)
    copies = []
    for index, (source, offset) in enumerate(((gate, quarter), (up, quarter), (down, 0), (down, quarter))):
        here = pl.ds(pl.multiple_of(begin + offset, 16), quarter)
        target = late.at[index] if index < 2 else last.at[index - 2]
        copies.append(pltpu.make_async_copy(source.at[here, :], target, sems.at[index]))
    for copy in copies:
        copy.start()
    tokens[0:rows, :] = own[...]
    tokens[rows:, :] = other[...]

    def activate_hidden(gate_rows, up_rows, place):
        gate_act = contract_last(tokens[...], gate_rows[...])
        up_act = contract_last(tokens[...], up_rows[...])
        value = gate_act / (1.0 + jnp.exp(-gate_act)) * up_act
        hidden[:, place * quarter : (place + 1) * quarter] = value.astype(BF16)

    activate_hidden(gate_first, up_first, 0)
    copies[0].wait()
    copies[1].wait()
    activate_hidden(late.at[0], late.at[1], 1)
    copies[2].wait()
    copies[3].wait()
    step = 256
    for start in range(0, width, step):
        here = slice(start, start + step)
        product = jnp.dot(hidden[:, :quarter], last[0, :, here], preferred_element_type=F32)
        product += jnp.dot(hidden[:, quarter:], last[1, :, here], preferred_element_type=F32)
        kept[:, here] = product[0:rows, :]
        given[:, here] = product[rows:, :].astype(BF16)


def shared_experts(half, own, other, gate_first, up_first, gate, up, down):
    rows, width = own.shape
    quarter = gate_first.shape[0]
    return pl.pallas_call(
        shared_kernel,
        out_shape=(jax.ShapeDtypeStruct((rows, width), F32), jax.ShapeDtypeStruct((rows, width), BF16)),
        in_specs=[SCALARS] + [WHOLE] * 4 + [FAR] * 3,
        out_specs=(WHOLE,) * 2,
        scratch_shapes=[
            VMEM((2 * rows, width), BF16),
            VMEM((2 * rows, 2 * quarter), BF16),
            VMEM((2, quarter, width), BF16),
            VMEM((2, quarter, width), BF16),
            pltpu.SemaphoreType.DMA((4,)),
        ],
        compiler_params=pltpu.CompilerParams(vmem_limit_bytes=36 << 20),
        cost_estimate=pl.CostEstimate(
            flops=24 * rows * quarter * width,
            bytes_accessed=8 * quarter * width,
            transcendentals=4 * rows * quarter,
        ),
        name="experts",
    )(half, own, other, gate_first, up_first, far(gate), far(up), far(down))


def expert_kernel(tokens, gate, up, down, total):
    number = pl.program_id(0)

    @pl.when(number == 0)
    def _():
        total[...] = jnp.zeros_like(total)

    for start in range(0, total.shape[0], LANES):
        cut = slice(start, start + LANES)
        gate_act = contract_last(tokens[cut, :], gate[...])
        up_act = contract_last(tokens[cut, :], up[...])
        hidden = (gate_act / (1.0 + jnp.exp(-gate_act)) * up_act).astype(BF16)
        total[cut, :] += jnp.dot(hidden, down[...], preferred_element_type=F32)


def experts(tokens, gate, up, down):
    rows, width = tokens.shape
    hidden = gate.shape[0]
    block = hidden if hidden <= 512 else math.gcd(hidden, 512)
    weights = pl.BlockSpec((block, width), lambda i: (i, 0))
    return pl.pallas_call(
        expert_kernel,
        grid=(hidden // block,),
        out_shape=jax.ShapeDtypeStruct((rows, width), F32),
        in_specs=[WHOLE] + [weights] * 3,
        out_specs=WHOLE,
        compiler_params=pltpu.CompilerParams(vmem_limit_bytes=40 << 20),
        cost_estimate=pl.CostEstimate(
            flops=6 * rows * hidden * width,
            bytes_accessed=6 * hidden * width,
            transcendentals=rows * hidden,
        ),
        name="experts",
    )(tokens, gate, up, down)


def one_hot(*conditions):
    found = conditions[0]
    for condition in conditions[1:]:
        found = found & condition
    return found.astype(F32).astype(BF16)


def combine_kernel(targets, spots, own, other, weight, routes, *refs):
    outs, packed = refs[:-1], refs[-1]
    rows = outs[0].shape[0]
    tokens, width = own.shape
    half, eighth = width // 2, width // 8
    mine = spots[0].astype(F32)
    across = jnp.transpose(routes[...].astype(F32))
    named = (across[0:1, :] == mine) | (across[1:2, :] == mine)
    q = lax.broadcasted_iota(jnp.int32, (tokens, tokens), 0)
    t = lax.broadcasted_iota(jnp.int32, (tokens, tokens), 1)
    same = (q // rows) == (t // rows)
    counts = jnp.broadcast_to(named.astype(F32), (16, tokens)).astype(BF16)
    place = jnp.dot(counts, one_hot(same, q <= t), preferred_element_type=F32)[0:1, :] - 1.0
    named = jnp.broadcast_to(named.astype(F32), (tokens, tokens)) > 0.5
    place = jnp.broadcast_to(place, (tokens, tokens)).astype(jnp.int32)
    r = q % rows
    value = ((own[...] + other[...].astype(F32)) * weight[:, 0:1]).astype(BF16)
    low = one_hot(named, same, r < 8, place == r)
    high = one_hot(named, same, r >= 8, place == r - 8)
    packed[:, :half] = (
        jnp.dot(low, value[:, :half], preferred_element_type=F32)
        + jnp.dot(high, value[:, half:], preferred_element_type=F32)
    ).astype(BF16)
    late = jnp.zeros((tokens, eighth), F32)
    for j in range(8):
        pick = one_hot(named, same, r // 2 == j, place == 8 + r % 2)
        late = late + jnp.dot(pick, value[:, j * eighth : (j + 1) * eighth], preferred_element_type=F32)
    packed[:, half:] = late.astype(BF16)
    for index, out in enumerate(outs):
        out[...] = packed[pl.ds(pl.multiple_of(targets[index] * rows, 16), rows), :]


def combine(targets, spots, own, other, weight, routes, rows):
    tokens, width = own.shape
    sends = tokens // rows
    lanes = width // 2 + width // 8
    return pl.pallas_call(
        combine_kernel,
        out_shape=tuple([jax.ShapeDtypeStruct((rows, lanes), BF16)] * sends),
        in_specs=[SCALARS] * 2 + [WHOLE] * 4,
        out_specs=(WHOLE,) * sends,
        scratch_shapes=[VMEM((tokens, lanes), BF16)],
        compiler_params=pltpu.CompilerParams(vmem_limit_bytes=10 << 20),
        name="combine",
    )(targets, spots, own, other, weight, routes)


def unpack_kernel(named_by, mixed, routes, *refs):
    count = len(refs) - 2
    pieces, out, packed = refs[:count], refs[count], refs[count + 1]
    rows, width = mixed.shape
    half, eighth = width // 2, width // 8
    for index in range(count):
        packed[index * rows : (index + 1) * rows, :] = pieces[index][...]
    shape = (rows, count * rows)
    lane = lax.broadcasted_iota(jnp.int32, shape, 1)
    r = lane % rows
    expert = jnp.zeros(shape, F32)
    for index in range(count):
        expert = jnp.where(lane // rows == index, named_by[index].astype(F32), expert)
    named = (routes[:, 0:1].astype(F32) == expert) | (routes[:, 1:2].astype(F32) == expert)
    above = lax.broadcasted_iota(jnp.int32, (rows, rows), 0) >= lax.broadcasted_iota(jnp.int32, (rows, rows), 1)
    place = jnp.dot(one_hot(above), one_hot(named), preferred_element_type=F32) - 1.0
    place = place.astype(jnp.int32)
    low = one_hot(named, r < 8, place == r)
    high = one_hot(named, r >= 8, place == r - 8)
    for j in range(8):
        pick = one_hot(named, r // 2 == j, place == 8 + r % 2)
        here = slice(j * eighth, (j + 1) * eighth)
        there = slice((j % 4) * eighth, (j % 4 + 1) * eighth)
        total = mixed[:, here].astype(F32)
        total += jnp.dot(low if j < 4 else high, packed[:, there], preferred_element_type=F32)
        total += jnp.dot(pick, packed[:, half:], preferred_element_type=F32)
        out[:, here] = total.astype(BF16)


def unpack(named_by, mixed, routes, pieces):
    rows, width = mixed.shape
    return pl.pallas_call(
        unpack_kernel,
        out_shape=jax.ShapeDtypeStruct((rows, width), BF16),
        in_specs=[SCALARS] + [WHOLE] * (2 + len(pieces)),
        out_specs=WHOLE,
        scratch_shapes=[VMEM((rows * len(pieces), pieces[0].shape[1]), BF16)],
        compiler_params=pltpu.CompilerParams(vmem_limit_bytes=6 << 20),
        name="unpack",
    )(named_by, mixed, routes, *pieces)


def body(
    projected,
    carried_tail,
    carried_state,
    filter_taps,
    filter_bias,
    select_weight,
    step_weight,
    step_bias,
    log_rate,
    skip_gain,
    output_weight,
    residual,
    norm_gain,
    router,
    gate_weight,
    up_weight,
    down_weight,
    routes,
):
    ctx, exp = lax.axis_size("ctx"), lax.axis_size("exp")
    ctx_at, exp_at = lax.axis_index("ctx"), lax.axis_index("exp")
    places = ring_places("ctx")
    x_input, z_input = projected[0], projected[1]
    own, width = residual.shape
    columns = output_weight.shape[1]
    taps = filter_taps.shape[0]
    parts = ctx * exp
    me = ctx_at * exp + exp_at
    spots = jnp.stack([ctx_at // (ctx // EXPERTS), me]).astype(jnp.int32)
    targets = jnp.stack([(me + s) % parts for s in range(parts)]).astype(jnp.int32)
    named_by = jnp.stack([(me - s) % parts for s in range(parts)]) // exp // (ctx // EXPERTS)

    x_pieces = spread(lambda k: x_input, "ctx", 0)
    own_routes = jnp.pad(routes.astype(BF16), ((0, 0), (0, LANES - 2)))
    extra = own_routes
    if exp == 2:
        other = rotate(extra, "exp", 1)
        extra = jnp.where(
            exp_at == 0,
            jnp.concatenate([extra, other], axis=0),
            jnp.concatenate([other, extra], axis=0),
        )
    else:
        extra = lax.all_gather(jnp.concatenate([residual, extra], axis=1), "exp", axis=0, tiled=True)
    tail_pad = jnp.zeros((8 - carried_tail.shape[0], carried_tail.shape[1]), F32)
    params = jnp.concatenate(
        [filter_taps, filter_bias[None], step_bias[None], skip_gain[None], jnp.zeros_like(tail_pad)[: 5 - taps],
         tail_pad, carried_tail.astype(F32)]
    )
    router_rows = jnp.pad(router.T, ((0, 16 - EXPERTS), (0, 0)))
    gain = jnp.pad(norm_gain[None, :], ((0, 7), (0, 0)))
    params, router_rows, gain, spots, targets, named_by = lax.optimization_barrier(
        (params, router_rows, gain, spots, targets, named_by.astype(jnp.int32))
    )

    active, proj = activate(places, x_pieces, params, taps, select_weight)
    own_proj, other_proj = pair_sum(proj, "exp")

    splits = exp if exp == 2 else 1

    def bundle(k):
        rows = residual if splits > 1 else jnp.where(exp_at == 0, extra[:, :width], 0)
        piece = lax.dynamic_slice_in_dim(rows, k * columns, columns, axis=1)
        lanes = columns // splits
        piece = jnp.concatenate([piece[:, i * lanes : (i + 1) * lanes] for i in range(splits)], axis=0)
        return jnp.concatenate([z_input, piece, extra[:, -LANES:]], axis=1)

    z_pieces = spread(bundle, "ctx", 0, active)
    value = scan(own_proj, other_proj, active, params, taps, log_rate, step_weight, carried_state)
    spread_places = jnp.concatenate([places, exp_at.astype(jnp.int32)[None]])
    sent, all_routes = project(spread_places, value, output_weight, z_pieces, splits)
    shared = exp == 2 and parts <= 8 and own == 16 and sent.shape[0] == LANES and lax.axis_size("doc") % 2 == 0
    half = lax.rem(lax.axis_index("doc"), 2).astype(jnp.int32)[None]
    if exp == 2:
        summand = rotate(sent, "exp", 1)
        if shared:
            half, sent = lax.optimization_barrier((half, sent))
            gate_first, up_first, half = fetch(half, [gate_weight, up_weight])
            half, sent = lax.optimization_barrier((half, sent))
        mixed = mix(sent, summand)
    else:
        mixed = lax.psum(sent.astype(F32), "exp").astype(BF16)
    mixed_pieces = spread(lambda k: mixed, "ctx", 1)
    normed, weight, mine = norm(places, spots, gain, router_rows, all_routes, mixed_pieces, own)
    total = mine.astype(F32)
    axes = ("ctx", "exp")
    if shared:
        kept, given = shared_experts(half, normed, swap(normed), gate_first, up_first, gate_weight, up_weight, down_weight)
        outs = combine(targets, spots, kept, swap(given), weight, all_routes, own)
        arrived = [outs[0]]
        for s in range(1, parts):
            arrived.append(lax.ppermute(outs[s], axes, [(i, (i + s) % parts) for i in range(parts)]))
        return unpack(named_by, mine, own_routes, arrived)
    else:
        kept = experts(normed, gate_weight, up_weight, down_weight)
        partial = (kept * weight[:, :1]).astype(BF16)
        moved = lax.all_to_all(partial, axes, split_axis=0, concat_axis=0, tiled=True)
        total = total + jnp.sum(moved.reshape(parts, own, width).astype(F32), axis=0)
    return total.astype(BF16)


def solution(mesh):
    placed = (
        P(None, ("doc", "ctx"), "exp"),
        P("doc", "exp"),
        P("doc", "exp"),
        P(None, "exp"),
        P("exp"),
        P(None, "exp"),
        P(None, "exp"),
        P("exp"),
        P(None, "exp"),
        P("exp"),
        P("exp", "ctx"),
        P(("doc", "ctx", "exp"), None),
        P(),
        P(),
        P(("ctx", "exp"), None),
        P(("ctx", "exp"), None),
        P(("ctx", "exp"), None),
        P(("doc", "ctx", "exp"), None),
    )
    return jax.shard_map(
        body, mesh=mesh, in_specs=placed, out_specs=P(("doc", "ctx", "exp"), None), check_vma=False
    )
```

```python
import functools
import math

import jax
import jax.numpy as jnp
from jax import lax
from jax.experimental import pallas as pl
from jax.experimental.pallas import tpu as pltpu
from jax.sharding import PartitionSpec as P

EXPERTS = 4
LANES = 128
FEW = 4
LOG2E = 1.4426950408889634
VMEM = pltpu.VMEM
SMEM = pltpu.SMEM
F32 = jnp.float32
BF16 = jnp.bfloat16


def contract_last(left, right):
    return lax.dot_general(left, right, (((1,), (1,)), ((), ())), preferred_element_type=F32)


def rotate(value, axis, steps):
    count = lax.axis_size(axis)
    return lax.ppermute(value, axis, [(i, (i + steps) % count) for i in range(count)])


def partner(place, step, count):
    paired = count & (count - 1) == 0
    return place ^ step if paired else (place + step) % count


def source(place, step, count):
    paired = count & (count - 1) == 0
    return place ^ step if paired else (place - step) % count


def exchange(value, axis, step, count):
    return lax.ppermute(value, axis, [(i, partner(i, step, count)) for i in range(count)])


def ring_places(axis):
    count = lax.axis_size(axis)
    if count > FEW:
        return jnp.zeros((1,), jnp.int32)
    me = lax.axis_index(axis)
    return jnp.stack([source(me, s, count) for s in range(count)]).astype(jnp.int32)


def spread(make, axis, join, after=None):
    count = lax.axis_size(axis)
    me = lax.axis_index(axis)
    if count <= FEW:
        sent = [make(partner(me, s, count)) for s in range(1, count)]
        if after is not None:
            sent, _ = lax.optimization_barrier((sent, after))
        return [make(me)] + [exchange(sent[s - 1], axis, s, count) for s in range(1, count)]
    stacked = jnp.stack([make(jnp.int32(k)) for k in range(count)])
    moved = lax.all_to_all(stacked, axis, split_axis=0, concat_axis=0, tiled=True)
    return [jnp.concatenate([moved[k] for k in range(count)], axis=join)]


def swap(value):
    count = lax.axis_size("doc")
    return lax.ppermute(value, "doc", [(i, i + 1 - 2 * (i % 2)) for i in range(count)])


def far(value):
    return pltpu.with_memory_space_constraint(value, pltpu.HBM)


def pair_sum(value, axis):
    if lax.axis_size(axis) == 2:
        return [value, rotate(value, axis, 1)]
    total = lax.psum(value.astype(F32), axis).astype(value.dtype)
    return [total, jnp.zeros_like(total)]


FAR = pl.BlockSpec(memory_space=pltpu.HBM)
WHOLE = pl.BlockSpec(memory_space=VMEM)
SCALARS = pl.BlockSpec(memory_space=SMEM)


def activate_kernel(count, taps, places, params, select, *refs):
    pieces, (active, proj, padded, held, sem) = refs[:count], refs[count:]
    copy = pltpu.make_async_copy(select, held, sem)
    copy.start()
    rows = pieces[0].shape[0]
    padded[0:8, :] = params[8:16, :]
    for index in range(count):
        start = pl.multiple_of(8 + places[index] * rows, 8)
        padded[pl.ds(start, rows), :] = pieces[index][...].astype(F32)
    tokens = active.shape[0]
    step = 32

    def block(number, carry):
        base = pl.multiple_of(number * step, step)
        window = padded[pl.ds(base, step + 8), :]
        total = jnp.broadcast_to(params[taps : taps + 1, :], (step, params.shape[1]))
        for k in range(taps):
            offset = 8 - (taps - 1) + k
            total = total + params[k : k + 1, :] * window[offset : offset + step, :]
        value = total / (1.0 + jnp.exp(-total))
        active[pl.ds(base, step), :] = value.astype(BF16)
        return carry

    lax.fori_loop(0, tokens // step, block, 0)
    copy.wait()
    for number in range(tokens // LANES):
        cut = slice(number * LANES, (number + 1) * LANES)
        proj[:, cut] = contract_last(held[...], active[cut, :])


def activate(places, pieces, params, taps, select):
    count = len(pieces)
    tokens = count * pieces[0].shape[0]
    channels = pieces[0].shape[1]
    return pl.pallas_call(
        functools.partial(activate_kernel, count, taps),
        out_shape=(
            jax.ShapeDtypeStruct((tokens, channels), BF16),
            jax.ShapeDtypeStruct((select.shape[0], tokens), F32),
        ),
        in_specs=[SCALARS, WHOLE, FAR] + [WHOLE] * count,
        out_specs=(WHOLE,) * 2,
        scratch_shapes=[
            VMEM((tokens + 8, channels), F32),
            VMEM(select.shape, BF16),
            pltpu.SemaphoreType.DMA,
        ],
        compiler_params=pltpu.CompilerParams(vmem_limit_bytes=12 << 20),
        cost_estimate=pl.CostEstimate(
            flops=2 * tokens * channels * select.shape[0],
            bytes_accessed=4 * tokens * channels,
            transcendentals=tokens * channels,
        ),
        name="activate",
    )(places, params, far(select), *pieces)


def scan_kernel(
    taps, own, other, active, params, log_rate_hbm, step_weight_hbm, state_hbm, value_out,
    sums, steps, scaled, rates, state, coef, step_weight, state_in, log_rate, sems,
):
    tokens, channels = active.shape
    rank = step_weight.shape[0]
    state_size = log_rate.shape[0]
    folds = channels // LANES
    group = min(folds, 16)
    load_weight = pltpu.make_async_copy(step_weight_hbm, step_weight, sems.at[0])
    load_state = pltpu.make_async_copy(state_hbm, state_in, sems.at[1])
    load_rate = pltpu.make_async_copy(log_rate_hbm, log_rate, sems.at[3])
    load_rate.start()
    load_state.start()
    load_weight.start()
    sums[...] = own[...] + other[...]
    copy = pltpu.make_async_copy(sums.at[pl.ds(rank, 2 * state_size), :], coef, sems.at[2])
    copy.start()

    def scatter(target, source):
        for s8 in range(state_size // 8):
            for j in range(folds):
                lanes = slice(j * LANES, (j + 1) * LANES)
                there = slice((s8 * folds + j) * 8, (s8 * folds + j) * 8 + 8)
                target[there, :] = source[s8 * 8 : s8 * 8 + 8, lanes]

    def fold_rows(row, first):
        return pl.ds((row // 8) * (folds * 8) + row % 8 + first * 8, group, stride=8)

    load_rate.wait()
    scatter(state, log_rate)
    for s in range(state_size):
        for first in range(0, folds, group):
            rates[s * folds + first : s * folds + first + group, :] = (
                jnp.exp(state[fold_rows(s, first), :]) * (-LOG2E)
            )
    load_state.wait()
    scatter(state, state_in)
    load_weight.wait()

    for number in range(tokens // LANES):
        cut = slice(number * LANES, (number + 1) * LANES)
        low = jnp.transpose(sums[0:rank, cut]).astype(BF16)
        width = min(channels, 256)
        for w in range(channels // width):
            lanes = slice(w * width, (w + 1) * width)
            raw = jnp.dot(low, step_weight[:, lanes], preferred_element_type=F32)
            raw = raw + params[taps + 1 : taps + 2, lanes]
            size = jnp.maximum(raw, 0.0) + jnp.log(1.0 + jnp.exp(-jnp.abs(raw)))
            times = size * active[cut, lanes].astype(F32)
            for i in range(LANES // 8):
                for j in range(width // LANES):
                    block = (number * LANES // 8 + i) * folds + w * (width // LANES) + j
                    there = slice(block * 8, block * 8 + 8)
                    part = (slice(i * 8, i * 8 + 8), slice(j * LANES, (j + 1) * LANES))
                    steps[there, :] = size[part]
                    scaled[there, :] = times[part]
    copy.wait()

    for first in range(0, folds, group):
        start = tuple(state[fold_rows(s, first), :] for s in range(state_size))

        def eight(number, held):
            base = number * (folds * 8) + first * 8
            held = list(held)
            for r in range(8):
                token = number * 8 + r
                rows = pl.ds(base + r, group, stride=8)
                size, times = steps[rows, :], scaled[rows, :]
                total = None
                for s in range(state_size):
                    rate = rates[s * folds + first : s * folds + first + group, :]
                    held[s] = jnp.exp2(size * rate) * held[s] + times * coef[s, token]
                    term = held[s] * coef[state_size + s, token]
                    total = term if total is None else total + term
                steps[rows, :] = total
            return tuple(held)

        lax.fori_loop(0, tokens // 8, eight, start)

    def unfold(number, carry):
        here = pl.ds(pl.multiple_of(number * 16, 16), 16)
        for j in range(folds):
            lanes = slice(j * LANES, (j + 1) * LANES)
            found = []
            for half in range(2):
                block = pl.multiple_of((number * 2 + half) * (folds * 8) + j * 8, 8)
                found.append(steps[pl.ds(block, 8), :])
            gain = params[taps + 2 : taps + 3, lanes]
            value_out[here, lanes] = jnp.concatenate(found, axis=0) + gain * active[here, lanes].astype(F32)
        return carry

    lax.fori_loop(0, tokens // 16, unfold, 0)


def scan(own, other, active, params, taps, log_rate, step_weight, state_in):
    tokens, channels = active.shape
    state_size = log_rate.shape[0]
    folded = (state_size * channels // LANES, LANES)
    return pl.pallas_call(
        functools.partial(scan_kernel, taps),
        out_shape=jax.ShapeDtypeStruct((tokens, channels), F32),
        in_specs=[WHOLE] * 4 + [FAR] * 3,
        out_specs=WHOLE,
        scratch_shapes=[
            VMEM(own.shape, F32),
            VMEM((tokens * channels // LANES, LANES), F32),
            VMEM((tokens * channels // LANES, LANES), F32),
            VMEM(folded, F32),
            VMEM(folded, F32),
            SMEM((2 * state_size, tokens), F32),
            VMEM(step_weight.shape, BF16),
            VMEM(state_in.shape, F32),
            VMEM(log_rate.shape, F32),
            pltpu.SemaphoreType.DMA((4,)),
        ],
        compiler_params=pltpu.CompilerParams(vmem_limit_bytes=16 << 20),
        cost_estimate=pl.CostEstimate(
            flops=3000 * tokens * channels * state_size,
            bytes_accessed=8 * tokens * channels,
            transcendentals=tokens * channels * state_size,
        ),
        name="scan",
    )(own, other, active, params, far(log_rate), far(step_weight), far(state_in))


def project_kernel(count, columns, splits, places, value_in, weight_hbm, *refs):
    pieces = refs[:count]
    send_out, routes_out, base_out, gated, out_weight, sem = refs[count:]
    lanes = columns // splits
    copy = pltpu.make_async_copy(weight_hbm, out_weight, sem)
    copy.start()
    tokens, channels = value_in.shape
    rows = pieces[0].shape[0]
    tile = 16
    for index in range(count):
        begin = pl.multiple_of(places[index] * rows, tile)
        routes_out[pl.ds(begin, rows), :] = pieces[index][:, channels + lanes :]

        def gate(number, carry):
            local = pl.ds(pl.multiple_of(number * tile, tile), tile)
            here = pl.ds(pl.multiple_of(begin + number * tile, tile), tile)
            z = pieces[index][local, :channels].astype(F32)
            gated[here, :] = (value_in[here, :] * (z / (1.0 + jnp.exp(-z)))).astype(BF16)
            return carry

        lax.fori_loop(0, rows // tile, gate, 0)
    copy.wait()
    for number in range(tokens // LANES):
        cut = slice(number * LANES, (number + 1) * LANES)
        base_out[cut, :] = jnp.dot(gated[cut, :], out_weight[...], preferred_element_type=F32)
    part = rows // splits
    for index in range(count):
        begin = places[index] * rows + (places[count] * part if splits > 1 else 0)
        here = pl.ds(pl.multiple_of(begin, tile), part)
        for k in range(splits):
            piece = pieces[index][k * part : (k + 1) * part, channels : channels + lanes]
            base_out[here, k * lanes : (k + 1) * lanes] += piece.astype(F32)
    for number in range(tokens // LANES):
        cut = slice(number * LANES, (number + 1) * LANES)
        send_out[cut, :] = base_out[cut, :].astype(BF16)


def project(places, value, out_weight, pieces, splits):
    tokens, channels = value.shape
    columns = out_weight.shape[1]
    count = len(pieces)
    return pl.pallas_call(
        functools.partial(project_kernel, count, columns, splits),
        out_shape=(
            jax.ShapeDtypeStruct((tokens, columns), BF16),
            jax.ShapeDtypeStruct((tokens, LANES), BF16),
        ),
        in_specs=[SCALARS, WHOLE, FAR] + [WHOLE] * count,
        out_specs=(WHOLE,) * 2,
        scratch_shapes=[
            VMEM((tokens, columns), F32),
            VMEM((tokens, channels), BF16),
            VMEM(out_weight.shape, BF16),
            pltpu.SemaphoreType.DMA,
        ],
        compiler_params=pltpu.CompilerParams(vmem_limit_bytes=16 << 20),
        cost_estimate=pl.CostEstimate(
            flops=2 * tokens * channels * columns,
            bytes_accessed=8 * tokens * channels,
            transcendentals=tokens * channels,
        ),
        name="project",
    )(places, value, far(out_weight), *pieces)


def mix_kernel(base, summand, mixed):
    mixed[...] = (base[...].astype(F32) + summand[...].astype(F32)).astype(BF16)


def mix(base, summand):
    return pl.pallas_call(
        mix_kernel,
        out_shape=jax.ShapeDtypeStruct(base.shape, BF16),
        in_specs=[WHOLE] * 2,
        out_specs=WHOLE,
        compiler_params=pltpu.CompilerParams(vmem_limit_bytes=4 << 20),
        name="mix",
    )(base, summand)


def norm_kernel(count, places, spots, gain, router, routes, *refs):
    pieces = refs[:count]
    normed, weight, own_rows = refs[count : count + 3]
    mixed = pieces[0] if count == 1 else refs[-1]
    tokens = normed.shape[0]
    columns = pieces[0].shape[1]
    for index in range(count if count > 1 else 0):
        start = pl.multiple_of(places[index] * columns, LANES)
        mixed[:, pl.ds(start, columns)] = pieces[index][...]
    mine = spots[0].astype(F32)
    step = 32

    def block(number, carry):
        cut = pl.ds(pl.multiple_of(number * step, step), step)
        value = mixed[cut, :].astype(F32)
        square = jnp.mean(value * value, axis=-1, keepdims=True) + 1e-06
        scaled = (value * lax.rsqrt(square) * gain[0:1, :]).astype(BF16)
        normed[cut, :] = scaled
        return carry

    lax.fori_loop(0, tokens // step, block, 0)
    for c in range(tokens // LANES):
        cut = slice(c * LANES, (c + 1) * LANES)
        logits = contract_last(normed[cut, :], router[...])
        first = routes[cut, 0:1].astype(F32)
        second = routes[cut, 1:2].astype(F32)
        ids = lax.broadcasted_iota(jnp.int32, logits.shape, 1).astype(F32)
        first_logit = jnp.sum(jnp.where(ids == first, logits, 0.0), axis=1, keepdims=True)
        second_logit = jnp.sum(jnp.where(ids == second, logits, 0.0), axis=1, keepdims=True)
        first_gate = jnp.where(first == mine, 1.0 / (1.0 + jnp.exp(second_logit - first_logit)), 0.0)
        second_gate = jnp.where(second == mine, 1.0 / (1.0 + jnp.exp(first_logit - second_logit)), 0.0)
        weight[cut, :] = jnp.broadcast_to(first_gate + second_gate, (LANES, LANES))
    rows = own_rows.shape[0]
    own_rows[...] = mixed[pl.ds(pl.multiple_of(spots[1] * rows, 16), rows), :]


def norm(places, spots, gain, router, routes, pieces, own):
    count = len(pieces)
    tokens = pieces[0].shape[0]
    width = count * pieces[0].shape[1]
    return pl.pallas_call(
        functools.partial(norm_kernel, count),
        out_shape=(
            jax.ShapeDtypeStruct((tokens, width), BF16),
            jax.ShapeDtypeStruct((tokens, LANES), F32),
            jax.ShapeDtypeStruct((own, width), BF16),
        ),
        in_specs=[SCALARS] * 2 + [WHOLE] * (3 + count),
        out_specs=(WHOLE,) * 3,
        scratch_shapes=[VMEM((tokens, width), BF16)] if count > 1 else [],
        compiler_params=pltpu.CompilerParams(vmem_limit_bytes=8 << 20),
        name="norm",
    )(places, spots, gain, router, routes, *pieces)


def fetch_kernel(parts, half_rows, half, *refs):
    count = len(refs) // 2 - 1
    sources, targets, done, sems = refs[:count], refs[count : 2 * count], refs[-2], refs[-1]
    rows = targets[0].shape[0]
    part = rows // parts
    copies = []
    for index in range(count):
        for k in range(parts):
            start = pl.multiple_of(half[0] * half_rows + k * part, 16)
            copies.append(
                pltpu.make_async_copy(
                    sources[index].at[pl.ds(start, part), :],
                    targets[index].at[pl.ds(k * part, part), :],
                    sems.at[index * parts + k],
                )
            )
    for copy in copies:
        copy.start()
    for copy in copies:
        copy.wait()
    done[0] = half[0]


def fetch(half, weights):
    half_rows, width = weights[0].shape[0] // 2, weights[0].shape[1]
    rows = half_rows // 2
    parts = 4
    return pl.pallas_call(
        functools.partial(fetch_kernel, parts, half_rows),
        out_shape=tuple([VMEM((rows, width), BF16)] * len(weights)) + (jax.ShapeDtypeStruct((1,), jnp.int32),),
        in_specs=[SCALARS] + [FAR] * len(weights),
        out_specs=tuple([WHOLE] * len(weights)) + (SCALARS,),
        scratch_shapes=[pltpu.SemaphoreType.DMA((parts * len(weights),))],
        compiler_params=pltpu.CompilerParams(vmem_limit_bytes=1 << 20),
        cost_estimate=pl.CostEstimate(
            flops=0, bytes_accessed=4 * rows * width * len(weights), transcendentals=0
        ),
        name="fetch",
    )(half, *[far(w) for w in weights])


def shared_kernel(half, own, other, gate_first, up_first, gate, up, down, kept, given, tokens, hidden, late, last, sems):
    rows = own.shape[0]
    quarter, width = gate_first.shape
    begin = half[0] * (2 * quarter)
    copies = []
    for index, (source, offset) in enumerate(((gate, quarter), (up, quarter), (down, 0), (down, quarter))):
        here = pl.ds(pl.multiple_of(begin + offset, 16), quarter)
        target = late.at[index] if index < 2 else last.at[index - 2]
        copies.append(pltpu.make_async_copy(source.at[here, :], target, sems.at[index]))
    for copy in copies[:2]:
        copy.start()
    tokens[0:rows, :] = own[...]
    tokens[rows:, :] = other[...]

    def activate_hidden(gate_rows, up_rows, place):
        gate_act = contract_last(tokens[...], gate_rows[...])
        up_act = contract_last(tokens[...], up_rows[...])
        value = gate_act / (1.0 + jnp.exp(-gate_act)) * up_act
        hidden[:, place * quarter : (place + 1) * quarter] = value.astype(BF16)

    activate_hidden(gate_first, up_first, 0)
    for copy in copies[2:]:
        copy.start()
    copies[0].wait()
    copies[1].wait()
    activate_hidden(late.at[0], late.at[1], 1)
    copies[2].wait()
    copies[3].wait()
    step = 256
    for start in range(0, width, step):
        here = slice(start, start + step)
        product = jnp.dot(hidden[:, :quarter], last[0, :, here], preferred_element_type=F32)
        product += jnp.dot(hidden[:, quarter:], last[1, :, here], preferred_element_type=F32)
        kept[:, here] = product[0:rows, :]
        given[:, here] = product[rows:, :].astype(BF16)


def shared_experts(half, own, other, gate_first, up_first, gate, up, down):
    rows, width = own.shape
    quarter = gate_first.shape[0]
    return pl.pallas_call(
        shared_kernel,
        out_shape=(jax.ShapeDtypeStruct((rows, width), F32), jax.ShapeDtypeStruct((rows, width), BF16)),
        in_specs=[SCALARS] + [WHOLE] * 4 + [FAR] * 3,
        out_specs=(WHOLE,) * 2,
        scratch_shapes=[
            VMEM((2 * rows, width), BF16),
            VMEM((2 * rows, 2 * quarter), BF16),
            VMEM((2, quarter, width), BF16),
            VMEM((2, quarter, width), BF16),
            pltpu.SemaphoreType.DMA((4,)),
        ],
        compiler_params=pltpu.CompilerParams(vmem_limit_bytes=36 << 20),
        cost_estimate=pl.CostEstimate(
            flops=24 * rows * quarter * width,
            bytes_accessed=8 * quarter * width,
            transcendentals=4 * rows * quarter,
        ),
        name="experts",
    )(half, own, other, gate_first, up_first, far(gate), far(up), far(down))


def expert_kernel(tokens, gate, up, down, total):
    number = pl.program_id(0)

    @pl.when(number == 0)
    def _():
        total[...] = jnp.zeros_like(total)

    for start in range(0, total.shape[0], LANES):
        cut = slice(start, start + LANES)
        gate_act = contract_last(tokens[cut, :], gate[...])
        up_act = contract_last(tokens[cut, :], up[...])
        hidden = (gate_act / (1.0 + jnp.exp(-gate_act)) * up_act).astype(BF16)
        total[cut, :] += jnp.dot(hidden, down[...], preferred_element_type=F32)


def experts(tokens, gate, up, down):
    rows, width = tokens.shape
    hidden = gate.shape[0]
    block = hidden if hidden <= 512 else math.gcd(hidden, 512)
    weights = pl.BlockSpec((block, width), lambda i: (i, 0))
    return pl.pallas_call(
        expert_kernel,
        grid=(hidden // block,),
        out_shape=jax.ShapeDtypeStruct((rows, width), F32),
        in_specs=[WHOLE] + [weights] * 3,
        out_specs=WHOLE,
        compiler_params=pltpu.CompilerParams(vmem_limit_bytes=40 << 20),
        cost_estimate=pl.CostEstimate(
            flops=6 * rows * hidden * width,
            bytes_accessed=6 * hidden * width,
            transcendentals=rows * hidden,
        ),
        name="experts",
    )(tokens, gate, up, down)


def one_hot(*conditions):
    found = conditions[0]
    for condition in conditions[1:]:
        found = found & condition
    return found.astype(F32).astype(BF16)


def combine_kernel(targets, spots, own, other, weight, routes, *refs):
    outs, packed = refs[:-1], refs[-1]
    rows = outs[0].shape[0]
    tokens, width = own.shape
    half, eighth = width // 2, width // 8
    mine = spots[0].astype(F32)
    across = jnp.transpose(routes[...].astype(F32))
    named = (across[0:1, :] == mine) | (across[1:2, :] == mine)
    q = lax.broadcasted_iota(jnp.int32, (tokens, tokens), 0)
    t = lax.broadcasted_iota(jnp.int32, (tokens, tokens), 1)
    same = (q // rows) == (t // rows)
    counts = jnp.broadcast_to(named.astype(F32), (16, tokens)).astype(BF16)
    place = jnp.dot(counts, one_hot(same, q <= t), preferred_element_type=F32)[0:1, :] - 1.0
    named = jnp.broadcast_to(named.astype(F32), (tokens, tokens)) > 0.5
    place = jnp.broadcast_to(place, (tokens, tokens)).astype(jnp.int32)
    r = q % rows
    value = ((own[...] + other[...].astype(F32)) * weight[:, 0:1]).astype(BF16)
    low = one_hot(named, same, r < 8, place == r)
    high = one_hot(named, same, r >= 8, place == r - 8)
    packed[:, :half] = (
        jnp.dot(low, value[:, :half], preferred_element_type=F32)
        + jnp.dot(high, value[:, half:], preferred_element_type=F32)
    ).astype(BF16)
    late = jnp.zeros((tokens, eighth), F32)
    for j in range(8):
        pick = one_hot(named, same, r // 2 == j, place == 8 + r % 2)
        late = late + jnp.dot(pick, value[:, j * eighth : (j + 1) * eighth], preferred_element_type=F32)
    packed[:, half:] = late.astype(BF16)
    for index, out in enumerate(outs):
        out[...] = packed[pl.ds(pl.multiple_of(targets[index] * rows, 16), rows), :]


def combine(targets, spots, own, other, weight, routes, rows):
    tokens, width = own.shape
    sends = tokens // rows
    lanes = width // 2 + width // 8
    return pl.pallas_call(
        combine_kernel,
        out_shape=tuple([jax.ShapeDtypeStruct((rows, lanes), BF16)] * sends),
        in_specs=[SCALARS] * 2 + [WHOLE] * 4,
        out_specs=(WHOLE,) * sends,
        scratch_shapes=[VMEM((tokens, lanes), BF16)],
        compiler_params=pltpu.CompilerParams(vmem_limit_bytes=10 << 20),
        name="combine",
    )(targets, spots, own, other, weight, routes)


def unpack_kernel(named_by, mixed, routes, *refs):
    count = len(refs) - 2
    pieces, out, packed = refs[:count], refs[count], refs[count + 1]
    rows, width = mixed.shape
    half, eighth = width // 2, width // 8
    for index in range(count):
        packed[index * rows : (index + 1) * rows, :] = pieces[index][...]
    shape = (rows, count * rows)
    lane = lax.broadcasted_iota(jnp.int32, shape, 1)
    r = lane % rows
    expert = jnp.zeros(shape, F32)
    for index in range(count):
        expert = jnp.where(lane // rows == index, named_by[index].astype(F32), expert)
    named = (routes[:, 0:1].astype(F32) == expert) | (routes[:, 1:2].astype(F32) == expert)
    above = lax.broadcasted_iota(jnp.int32, (rows, rows), 0) >= lax.broadcasted_iota(jnp.int32, (rows, rows), 1)
    place = jnp.dot(one_hot(above), one_hot(named), preferred_element_type=F32) - 1.0
    place = place.astype(jnp.int32)
    low = one_hot(named, r < 8, place == r)
    high = one_hot(named, r >= 8, place == r - 8)
    for j in range(8):
        pick = one_hot(named, r // 2 == j, place == 8 + r % 2)
        here = slice(j * eighth, (j + 1) * eighth)
        there = slice((j % 4) * eighth, (j % 4 + 1) * eighth)
        total = mixed[:, here].astype(F32)
        total += jnp.dot(low if j < 4 else high, packed[:, there], preferred_element_type=F32)
        total += jnp.dot(pick, packed[:, half:], preferred_element_type=F32)
        out[:, here] = total.astype(BF16)


def unpack(named_by, mixed, routes, pieces):
    rows, width = mixed.shape
    return pl.pallas_call(
        unpack_kernel,
        out_shape=jax.ShapeDtypeStruct((rows, width), BF16),
        in_specs=[SCALARS] + [WHOLE] * (2 + len(pieces)),
        out_specs=WHOLE,
        scratch_shapes=[VMEM((rows * len(pieces), pieces[0].shape[1]), BF16)],
        compiler_params=pltpu.CompilerParams(vmem_limit_bytes=6 << 20),
        name="unpack",
    )(named_by, mixed, routes, *pieces)


def body(
    projected,
    carried_tail,
    carried_state,
    filter_taps,
    filter_bias,
    select_weight,
    step_weight,
    step_bias,
    log_rate,
    skip_gain,
    output_weight,
    residual,
    norm_gain,
    router,
    gate_weight,
    up_weight,
    down_weight,
    routes,
):
    ctx, exp = lax.axis_size("ctx"), lax.axis_size("exp")
    ctx_at, exp_at = lax.axis_index("ctx"), lax.axis_index("exp")
    places = ring_places("ctx")
    x_input, z_input = projected[0], projected[1]
    own, width = residual.shape
    columns = output_weight.shape[1]
    taps = filter_taps.shape[0]
    parts = ctx * exp
    me = ctx_at * exp + exp_at
    spots = jnp.stack([ctx_at // (ctx // EXPERTS), me]).astype(jnp.int32)
    targets = jnp.stack([(me + s) % parts for s in range(parts)]).astype(jnp.int32)
    named_by = jnp.stack([(me - s) % parts for s in range(parts)]) // exp // (ctx // EXPERTS)

    x_pieces = spread(lambda k: x_input, "ctx", 0)
    own_routes = jnp.pad(routes.astype(BF16), ((0, 0), (0, LANES - 2)))
    extra = own_routes
    if exp == 2:
        other = rotate(extra, "exp", 1)
        extra = jnp.where(
            exp_at == 0,
            jnp.concatenate([extra, other], axis=0),
            jnp.concatenate([other, extra], axis=0),
        )
    else:
        extra = lax.all_gather(jnp.concatenate([residual, extra], axis=1), "exp", axis=0, tiled=True)
    tail_pad = jnp.zeros((8 - carried_tail.shape[0], carried_tail.shape[1]), F32)
    params = jnp.concatenate(
        [filter_taps, filter_bias[None], step_bias[None], skip_gain[None], jnp.zeros_like(tail_pad)[: 5 - taps],
         tail_pad, carried_tail.astype(F32)]
    )
    router_rows = jnp.pad(router.T, ((0, 16 - EXPERTS), (0, 0)))
    gain = jnp.pad(norm_gain[None, :], ((0, 7), (0, 0)))
    params, router_rows, gain, spots, targets, named_by = lax.optimization_barrier(
        (params, router_rows, gain, spots, targets, named_by.astype(jnp.int32))
    )

    active, proj = activate(places, x_pieces, params, taps, select_weight)
    own_proj, other_proj = pair_sum(proj, "exp")

    splits = exp if exp == 2 else 1

    def bundle(k):
        rows = residual if splits > 1 else jnp.where(exp_at == 0, extra[:, :width], 0)
        piece = lax.dynamic_slice_in_dim(rows, k * columns, columns, axis=1)
        lanes = columns // splits
        piece = jnp.concatenate([piece[:, i * lanes : (i + 1) * lanes] for i in range(splits)], axis=0)
        return jnp.concatenate([z_input, piece, extra[:, -LANES:]], axis=1)

    z_pieces = spread(bundle, "ctx", 0, active)
    value = scan(own_proj, other_proj, active, params, taps, log_rate, step_weight, carried_state)
    spread_places = jnp.concatenate([places, exp_at.astype(jnp.int32)[None]])
    sent, all_routes = project(spread_places, value, output_weight, z_pieces, splits)
    shared = exp == 2 and parts <= 8 and own == 16 and sent.shape[0] == LANES and lax.axis_size("doc") % 2 == 0
    half = lax.rem(lax.axis_index("doc"), 2).astype(jnp.int32)[None]
    if exp == 2:
        summand = rotate(sent, "exp", 1)
        if shared:
            half, sent = lax.optimization_barrier((half, sent))
            gate_first, up_first, half = fetch(half, [gate_weight, up_weight])
            half, sent = lax.optimization_barrier((half, sent))
        mixed = mix(sent, summand)
    else:
        mixed = lax.psum(sent.astype(F32), "exp").astype(BF16)
    mixed_pieces = spread(lambda k: mixed, "ctx", 1)
    normed, weight, mine = norm(places, spots, gain, router_rows, all_routes, mixed_pieces, own)
    total = mine.astype(F32)
    axes = ("ctx", "exp")
    if shared:
        kept, given = shared_experts(half, normed, swap(normed), gate_first, up_first, gate_weight, up_weight, down_weight)
        outs = combine(targets, spots, kept, swap(given), weight, all_routes, own)
        arrived = [outs[0]]
        for s in range(1, parts):
            arrived.append(lax.ppermute(outs[s], axes, [(i, (i + s) % parts) for i in range(parts)]))
        return unpack(named_by, mine, own_routes, arrived)
    else:
        kept = experts(normed, gate_weight, up_weight, down_weight)
        partial = (kept * weight[:, :1]).astype(BF16)
        moved = lax.all_to_all(partial, axes, split_axis=0, concat_axis=0, tiled=True)
        total = total + jnp.sum(moved.reshape(parts, own, width).astype(F32), axis=0)
    return total.astype(BF16)


def solution(mesh):
    placed = (
        P(None, ("doc", "ctx"), "exp"),
        P("doc", "exp"),
        P("doc", "exp"),
        P(None, "exp"),
        P("exp"),
        P(None, "exp"),
        P(None, "exp"),
        P("exp"),
        P(None, "exp"),
        P("exp"),
        P("exp", "ctx"),
        P(("doc", "ctx", "exp"), None),
        P(),
        P(),
        P(("ctx", "exp"), None),
        P(("ctx", "exp"), None),
        P(("ctx", "exp"), None),
        P(("doc", "ctx", "exp"), None),
    )
    return jax.shard_map(
        body, mesh=mesh, in_specs=placed, out_specs=P(("doc", "ctx", "exp"), None), check_vma=False
    )
```

```python
import functools
import math

import jax
import jax.numpy as jnp
from jax import lax
from jax.experimental import pallas as pl
from jax.experimental.pallas import tpu as pltpu
from jax.sharding import PartitionSpec as P

EXPERTS = 4
LANES = 128
FEW = 4
LOG2E = 1.4426950408889634
VMEM = pltpu.VMEM
SMEM = pltpu.SMEM
F32 = jnp.float32
BF16 = jnp.bfloat16


def contract_last(left, right):
    return lax.dot_general(left, right, (((1,), (1,)), ((), ())), preferred_element_type=F32)


def rotate(value, axis, steps):
    count = lax.axis_size(axis)
    return lax.ppermute(value, axis, [(i, (i + steps) % count) for i in range(count)])


def partner(place, step, count):
    paired = count & (count - 1) == 0
    return place ^ step if paired else (place + step) % count


def source(place, step, count):
    paired = count & (count - 1) == 0
    return place ^ step if paired else (place - step) % count


def exchange(value, axis, step, count):
    return lax.ppermute(value, axis, [(i, partner(i, step, count)) for i in range(count)])


def ring_places(axis):
    count = lax.axis_size(axis)
    if count > FEW:
        return jnp.zeros((1,), jnp.int32)
    me = lax.axis_index(axis)
    return jnp.stack([source(me, s, count) for s in range(count)]).astype(jnp.int32)


def spread(make, axis, join, after=None):
    count = lax.axis_size(axis)
    me = lax.axis_index(axis)
    if count <= FEW:
        sent = [make(partner(me, s, count)) for s in range(1, count)]
        if after is not None:
            sent, _ = lax.optimization_barrier((sent, after))
        return [make(me)] + [exchange(sent[s - 1], axis, s, count) for s in range(1, count)]
    stacked = jnp.stack([make(jnp.int32(k)) for k in range(count)])
    moved = lax.all_to_all(stacked, axis, split_axis=0, concat_axis=0, tiled=True)
    return [jnp.concatenate([moved[k] for k in range(count)], axis=join)]


def swap(value):
    count = lax.axis_size("doc")
    return lax.ppermute(value, "doc", [(i, i + 1 - 2 * (i % 2)) for i in range(count)])


def far(value):
    return pltpu.with_memory_space_constraint(value, pltpu.HBM)


def pair_sum(value, axis):
    if lax.axis_size(axis) == 2:
        return [value, rotate(value, axis, 1)]
    total = lax.psum(value.astype(F32), axis).astype(value.dtype)
    return [total, jnp.zeros_like(total)]


FAR = pl.BlockSpec(memory_space=pltpu.HBM)
WHOLE = pl.BlockSpec(memory_space=VMEM)
SCALARS = pl.BlockSpec(memory_space=SMEM)


def activate_kernel(count, taps, places, params, select, *refs):
    pieces, (active, proj, padded, held, sem) = refs[:count], refs[count:]
    copy = pltpu.make_async_copy(select, held, sem)
    copy.start()
    rows = pieces[0].shape[0]
    padded[0:8, :] = params[8:16, :]
    for index in range(count):
        start = pl.multiple_of(8 + places[index] * rows, 8)
        padded[pl.ds(start, rows), :] = pieces[index][...].astype(F32)
    tokens = active.shape[0]
    step = 32

    def block(number, carry):
        base = pl.multiple_of(number * step, step)
        window = padded[pl.ds(base, step + 8), :]
        total = jnp.broadcast_to(params[taps : taps + 1, :], (step, params.shape[1]))
        for k in range(taps):
            offset = 8 - (taps - 1) + k
            total = total + params[k : k + 1, :] * window[offset : offset + step, :]
        value = total / (1.0 + jnp.exp(-total))
        active[pl.ds(base, step), :] = value.astype(BF16)
        return carry

    lax.fori_loop(0, tokens // step, block, 0)
    copy.wait()
    for number in range(tokens // LANES):
        cut = slice(number * LANES, (number + 1) * LANES)
        proj[:, cut] = contract_last(held[...], active[cut, :])


def activate(places, pieces, params, taps, select):
    count = len(pieces)
    tokens = count * pieces[0].shape[0]
    channels = pieces[0].shape[1]
    return pl.pallas_call(
        functools.partial(activate_kernel, count, taps),
        out_shape=(
            jax.ShapeDtypeStruct((tokens, channels), BF16),
            jax.ShapeDtypeStruct((select.shape[0], tokens), F32),
        ),
        in_specs=[SCALARS, WHOLE, FAR] + [WHOLE] * count,
        out_specs=(WHOLE,) * 2,
        scratch_shapes=[
            VMEM((tokens + 8, channels), F32),
            VMEM(select.shape, BF16),
            pltpu.SemaphoreType.DMA,
        ],
        compiler_params=pltpu.CompilerParams(vmem_limit_bytes=12 << 20),
        cost_estimate=pl.CostEstimate(
            flops=2 * tokens * channels * select.shape[0],
            bytes_accessed=4 * tokens * channels,
            transcendentals=tokens * channels,
        ),
        name="activate",
    )(places, params, far(select), *pieces)


def scan_kernel(
    taps, own, other, active, params, log_rate_hbm, step_weight_hbm, state_hbm, value_out,
    sums, steps, scaled, rates, state, coef, step_weight, state_in, log_rate, sems,
):
    tokens, channels = active.shape
    rank = step_weight.shape[0]
    state_size = log_rate.shape[0]
    folds = channels // LANES
    group = min(folds, 16)
    load_weight = pltpu.make_async_copy(step_weight_hbm, step_weight, sems.at[0])
    load_state = pltpu.make_async_copy(state_hbm, state_in, sems.at[1])
    load_rate = pltpu.make_async_copy(log_rate_hbm, log_rate, sems.at[3])
    load_rate.start()
    load_state.start()
    load_weight.start()
    sums[...] = own[...] + other[...]
    copy = pltpu.make_async_copy(sums.at[pl.ds(rank, 2 * state_size), :], coef, sems.at[2])
    copy.start()

    def scatter(target, source):
        for s8 in range(state_size // 8):
            for j in range(folds):
                lanes = slice(j * LANES, (j + 1) * LANES)
                there = slice((s8 * folds + j) * 8, (s8 * folds + j) * 8 + 8)
                target[there, :] = source[s8 * 8 : s8 * 8 + 8, lanes]

    def fold_rows(row, first):
        return pl.ds((row // 8) * (folds * 8) + row % 8 + first * 8, group, stride=8)

    load_rate.wait()
    scatter(state, log_rate)
    for s in range(state_size):
        for first in range(0, folds, group):
            rates[s * folds + first : s * folds + first + group, :] = (
                jnp.exp(state[fold_rows(s, first), :]) * (-LOG2E)
            )
    load_state.wait()
    scatter(state, state_in)
    load_weight.wait()

    for number in range(tokens // LANES):
        cut = slice(number * LANES, (number + 1) * LANES)
        low = jnp.transpose(sums[0:rank, cut]).astype(BF16)
        width = min(channels, 256)
        for w in range(channels // width):
            lanes = slice(w * width, (w + 1) * width)
            raw = jnp.dot(low, step_weight[:, lanes], preferred_element_type=F32)
            raw = raw + params[taps + 1 : taps + 2, lanes]
            size = jnp.maximum(raw, 0.0) + jnp.log(1.0 + jnp.exp(-jnp.abs(raw)))
            times = size * active[cut, lanes].astype(F32)
            for i in range(LANES // 8):
                for j in range(width // LANES):
                    block = (number * LANES // 8 + i) * folds + w * (width // LANES) + j
                    there = slice(block * 8, block * 8 + 8)
                    part = (slice(i * 8, i * 8 + 8), slice(j * LANES, (j + 1) * LANES))
                    steps[there, :] = size[part]
                    scaled[there, :] = times[part]
    copy.wait()

    for first in range(0, folds, group):
        start = tuple(state[fold_rows(s, first), :] for s in range(state_size))

        def eight(number, held):
            base = number * (folds * 8) + first * 8
            held = list(held)
            for r in range(8):
                token = number * 8 + r
                rows = pl.ds(base + r, group, stride=8)
                size, times = steps[rows, :], scaled[rows, :]
                total = None
                for s in range(state_size):
                    rate = rates[s * folds + first : s * folds + first + group, :]
                    held[s] = jnp.exp2(size * rate) * held[s] + times * coef[s, token]
                    term = held[s] * coef[state_size + s, token]
                    total = term if total is None else total + term
                steps[rows, :] = total
            return tuple(held)

        lax.fori_loop(0, tokens // 8, eight, start)

    def unfold(number, carry):
        here = pl.ds(pl.multiple_of(number * 16, 16), 16)
        for j in range(folds):
            lanes = slice(j * LANES, (j + 1) * LANES)
            found = []
            for half in range(2):
                block = pl.multiple_of((number * 2 + half) * (folds * 8) + j * 8, 8)
                found.append(steps[pl.ds(block, 8), :])
            gain = params[taps + 2 : taps + 3, lanes]
            value_out[here, lanes] = jnp.concatenate(found, axis=0) + gain * active[here, lanes].astype(F32)
        return carry

    lax.fori_loop(0, tokens // 16, unfold, 0)


def scan(own, other, active, params, taps, log_rate, step_weight, state_in):
    tokens, channels = active.shape
    state_size = log_rate.shape[0]
    folded = (state_size * channels // LANES, LANES)
    return pl.pallas_call(
        functools.partial(scan_kernel, taps),
        out_shape=jax.ShapeDtypeStruct((tokens, channels), F32),
        in_specs=[WHOLE] * 4 + [FAR] * 3,
        out_specs=WHOLE,
        scratch_shapes=[
            VMEM(own.shape, F32),
            VMEM((tokens * channels // LANES, LANES), F32),
            VMEM((tokens * channels // LANES, LANES), F32),
            VMEM(folded, F32),
            VMEM(folded, F32),
            SMEM((2 * state_size, tokens), F32),
            VMEM(step_weight.shape, BF16),
            VMEM(state_in.shape, F32),
            VMEM(log_rate.shape, F32),
            pltpu.SemaphoreType.DMA((4,)),
        ],
        compiler_params=pltpu.CompilerParams(vmem_limit_bytes=16 << 20),
        cost_estimate=pl.CostEstimate(
            flops=3000 * tokens * channels * state_size,
            bytes_accessed=8 * tokens * channels,
            transcendentals=tokens * channels * state_size,
        ),
        name="scan",
    )(own, other, active, params, far(log_rate), far(step_weight), far(state_in))


def project_kernel(count, columns, splits, places, value_in, weight_hbm, *refs):
    pieces = refs[:count]
    send_out, routes_out, base_out, gated, out_weight, sem = refs[count:]
    lanes = columns // splits
    copy = pltpu.make_async_copy(weight_hbm, out_weight, sem)
    copy.start()
    tokens, channels = value_in.shape
    rows = pieces[0].shape[0]
    tile = 16
    for index in range(count):
        begin = pl.multiple_of(places[index] * rows, tile)
        routes_out[pl.ds(begin, rows), :] = pieces[index][:, channels + lanes :]

        def gate(number, carry):
            local = pl.ds(pl.multiple_of(number * tile, tile), tile)
            here = pl.ds(pl.multiple_of(begin + number * tile, tile), tile)
            z = pieces[index][local, :channels].astype(F32)
            gated[here, :] = (value_in[here, :] * (z / (1.0 + jnp.exp(-z)))).astype(BF16)
            return carry

        lax.fori_loop(0, rows // tile, gate, 0)
    copy.wait()
    for number in range(tokens // LANES):
        cut = slice(number * LANES, (number + 1) * LANES)
        base_out[cut, :] = jnp.dot(gated[cut, :], out_weight[...], preferred_element_type=F32)
    part = rows // splits
    for index in range(count):
        begin = places[index] * rows + (places[count] * part if splits > 1 else 0)
        here = pl.ds(pl.multiple_of(begin, tile), part)
        for k in range(splits):
            piece = pieces[index][k * part : (k + 1) * part, channels : channels + lanes]
            base_out[here, k * lanes : (k + 1) * lanes] += piece.astype(F32)
    for number in range(tokens // LANES):
        cut = slice(number * LANES, (number + 1) * LANES)
        send_out[cut, :] = base_out[cut, :].astype(BF16)


def project(places, value, out_weight, pieces, splits):
    tokens, channels = value.shape
    columns = out_weight.shape[1]
    count = len(pieces)
    return pl.pallas_call(
        functools.partial(project_kernel, count, columns, splits),
        out_shape=(
            jax.ShapeDtypeStruct((tokens, columns), BF16),
            jax.ShapeDtypeStruct((tokens, LANES), BF16),
        ),
        in_specs=[SCALARS, WHOLE, FAR] + [WHOLE] * count,
        out_specs=(WHOLE,) * 2,
        scratch_shapes=[
            VMEM((tokens, columns), F32),
            VMEM((tokens, channels), BF16),
            VMEM(out_weight.shape, BF16),
            pltpu.SemaphoreType.DMA,
        ],
        compiler_params=pltpu.CompilerParams(vmem_limit_bytes=16 << 20),
        cost_estimate=pl.CostEstimate(
            flops=2 * tokens * channels * columns,
            bytes_accessed=8 * tokens * channels,
            transcendentals=tokens * channels,
        ),
        name="project",
    )(places, value, far(out_weight), *pieces)


def mix_kernel(base, summand, mixed):
    mixed[...] = (base[...].astype(F32) + summand[...].astype(F32)).astype(BF16)


def mix(base, summand):
    return pl.pallas_call(
        mix_kernel,
        out_shape=jax.ShapeDtypeStruct(base.shape, BF16),
        in_specs=[WHOLE] * 2,
        out_specs=WHOLE,
        compiler_params=pltpu.CompilerParams(vmem_limit_bytes=4 << 20),
        name="mix",
    )(base, summand)


def norm_kernel(count, places, spots, gain, router, routes, *refs):
    pieces = refs[:count]
    normed, weight, own_rows = refs[count : count + 3]
    mixed = pieces[0] if count == 1 else refs[-1]
    tokens = normed.shape[0]
    columns = pieces[0].shape[1]
    for index in range(count if count > 1 else 0):
        start = pl.multiple_of(places[index] * columns, LANES)
        mixed[:, pl.ds(start, columns)] = pieces[index][...]
    mine = spots[0].astype(F32)
    step = 32

    def block(number, carry):
        cut = pl.ds(pl.multiple_of(number * step, step), step)
        value = mixed[cut, :].astype(F32)
        square = jnp.mean(value * value, axis=-1, keepdims=True) + 1e-06
        scaled = (value * lax.rsqrt(square) * gain[0:1, :]).astype(BF16)
        normed[cut, :] = scaled
        return carry

    lax.fori_loop(0, tokens // step, block, 0)
    for c in range(tokens // LANES):
        cut = slice(c * LANES, (c + 1) * LANES)
        logits = contract_last(normed[cut, :], router[...])
        first = routes[cut, 0:1].astype(F32)
        second = routes[cut, 1:2].astype(F32)
        ids = lax.broadcasted_iota(jnp.int32, logits.shape, 1).astype(F32)
        first_logit = jnp.sum(jnp.where(ids == first, logits, 0.0), axis=1, keepdims=True)
        second_logit = jnp.sum(jnp.where(ids == second, logits, 0.0), axis=1, keepdims=True)
        first_gate = jnp.where(first == mine, 1.0 / (1.0 + jnp.exp(second_logit - first_logit)), 0.0)
        second_gate = jnp.where(second == mine, 1.0 / (1.0 + jnp.exp(first_logit - second_logit)), 0.0)
        weight[cut, :] = jnp.broadcast_to(first_gate + second_gate, (LANES, LANES))
    rows = own_rows.shape[0]
    own_rows[...] = mixed[pl.ds(pl.multiple_of(spots[1] * rows, 16), rows), :]


def norm(places, spots, gain, router, routes, pieces, own):
    count = len(pieces)
    tokens = pieces[0].shape[0]
    width = count * pieces[0].shape[1]
    return pl.pallas_call(
        functools.partial(norm_kernel, count),
        out_shape=(
            jax.ShapeDtypeStruct((tokens, width), BF16),
            jax.ShapeDtypeStruct((tokens, LANES), F32),
            jax.ShapeDtypeStruct((own, width), BF16),
        ),
        in_specs=[SCALARS] * 2 + [WHOLE] * (3 + count),
        out_specs=(WHOLE,) * 3,
        scratch_shapes=[VMEM((tokens, width), BF16)] if count > 1 else [],
        compiler_params=pltpu.CompilerParams(vmem_limit_bytes=8 << 20),
        name="norm",
    )(places, spots, gain, router, routes, *pieces)


def fetch_kernel(parts, half_rows, half, *refs):
    count = len(refs) // 2 - 1
    sources, targets, done, sems = refs[:count], refs[count : 2 * count], refs[-2], refs[-1]
    rows = targets[0].shape[0]
    part = rows // parts
    copies = []
    for index in range(count):
        for k in range(parts):
            start = pl.multiple_of(half[0] * half_rows + k * part, 16)
            copies.append(
                pltpu.make_async_copy(
                    sources[index].at[pl.ds(start, part), :],
                    targets[index].at[pl.ds(k * part, part), :],
                    sems.at[index * parts + k],
                )
            )
    for copy in copies:
        copy.start()
    for copy in copies:
        copy.wait()
    done[0] = half[0]


def fetch(half, weights):
    half_rows, width = weights[0].shape[0] // 2, weights[0].shape[1]
    rows = half_rows // 2
    parts = 4
    return pl.pallas_call(
        functools.partial(fetch_kernel, parts, half_rows),
        out_shape=tuple([VMEM((rows, width), BF16)] * len(weights)) + (jax.ShapeDtypeStruct((1,), jnp.int32),),
        in_specs=[SCALARS] + [FAR] * len(weights),
        out_specs=tuple([WHOLE] * len(weights)) + (SCALARS,),
        scratch_shapes=[pltpu.SemaphoreType.DMA((parts * len(weights),))],
        compiler_params=pltpu.CompilerParams(vmem_limit_bytes=1 << 20),
        cost_estimate=pl.CostEstimate(
            flops=0, bytes_accessed=4 * rows * width * len(weights), transcendentals=0
        ),
        name="fetch",
    )(half, *[far(w) for w in weights])


def shared_kernel(half, own, other, gate_first, up_first, gate, up, down, kept, given, tokens, hidden, late, last, sems):
    rows = own.shape[0]
    quarter, width = gate_first.shape
    begin = half[0] * (2 * quarter)
    copies = []
    for index, source in enumerate((gate, up)):
        here = pl.ds(pl.multiple_of(begin + quarter, 16), quarter)
        copies.append(pltpu.make_async_copy(source.at[here, :], late.at[index], sems.at[index]))
    parts = sems.shape[0] - 2
    lanes = width // parts
    for k in range(parts):
        here = pl.ds(pl.multiple_of(begin, 16), 2 * quarter)
        cut = pl.ds(k * lanes, lanes)
        copies.append(pltpu.make_async_copy(down.at[here, cut], last.at[:, cut], sems.at[2 + k]))
    for copy in copies[:2]:
        copy.start()
    tokens[0:rows, :] = own[...]
    tokens[rows:, :] = other[...]

    def activate_hidden(gate_rows, up_rows, place):
        gate_act = contract_last(tokens[...], gate_rows[...])
        up_act = contract_last(tokens[...], up_rows[...])
        value = gate_act / (1.0 + jnp.exp(-gate_act)) * up_act
        hidden[:, place * quarter : (place + 1) * quarter] = value.astype(BF16)

    activate_hidden(gate_first, up_first, 0)
    for copy in copies[2:]:
        copy.start()
    copies[0].wait()
    copies[1].wait()
    activate_hidden(late.at[0], late.at[1], 1)
    step = 256
    for k in range(parts):
        copies[2 + k].wait()
        for start in range(k * lanes, (k + 1) * lanes, step):
            here = slice(start, start + step)
            product = jnp.dot(hidden[...], last[:, here], preferred_element_type=F32)
            kept[:, here] = product[0:rows, :]
            given[:, here] = product[rows:, :].astype(BF16)


def shared_experts(half, own, other, gate_first, up_first, gate, up, down):
    rows, width = own.shape
    quarter = gate_first.shape[0]
    return pl.pallas_call(
        shared_kernel,
        out_shape=(jax.ShapeDtypeStruct((rows, width), F32), jax.ShapeDtypeStruct((rows, width), BF16)),
        in_specs=[SCALARS] + [WHOLE] * 4 + [FAR] * 3,
        out_specs=(WHOLE,) * 2,
        scratch_shapes=[
            VMEM((2 * rows, width), BF16),
            VMEM((2 * rows, 2 * quarter), BF16),
            VMEM((2, quarter, width), BF16),
            VMEM((2 * quarter, width), BF16),
            pltpu.SemaphoreType.DMA((6,)),
        ],
        compiler_params=pltpu.CompilerParams(vmem_limit_bytes=36 << 20),
        cost_estimate=pl.CostEstimate(
            flops=24 * rows * quarter * width,
            bytes_accessed=8 * quarter * width,
            transcendentals=4 * rows * quarter,
        ),
        name="experts",
    )(half, own, other, gate_first, up_first, far(gate), far(up), far(down))


def expert_kernel(tokens, gate, up, down, total):
    number = pl.program_id(0)

    @pl.when(number == 0)
    def _():
        total[...] = jnp.zeros_like(total)

    for start in range(0, total.shape[0], LANES):
        cut = slice(start, start + LANES)
        gate_act = contract_last(tokens[cut, :], gate[...])
        up_act = contract_last(tokens[cut, :], up[...])
        hidden = (gate_act / (1.0 + jnp.exp(-gate_act)) * up_act).astype(BF16)
        total[cut, :] += jnp.dot(hidden, down[...], preferred_element_type=F32)


def experts(tokens, gate, up, down):
    rows, width = tokens.shape
    hidden = gate.shape[0]
    block = hidden if hidden <= 512 else math.gcd(hidden, 512)
    weights = pl.BlockSpec((block, width), lambda i: (i, 0))
    return pl.pallas_call(
        expert_kernel,
        grid=(hidden // block,),
        out_shape=jax.ShapeDtypeStruct((rows, width), F32),
        in_specs=[WHOLE] + [weights] * 3,
        out_specs=WHOLE,
        compiler_params=pltpu.CompilerParams(vmem_limit_bytes=40 << 20),
        cost_estimate=pl.CostEstimate(
            flops=6 * rows * hidden * width,
            bytes_accessed=6 * hidden * width,
            transcendentals=rows * hidden,
        ),
        name="experts",
    )(tokens, gate, up, down)


def one_hot(*conditions):
    found = conditions[0]
    for condition in conditions[1:]:
        found = found & condition
    return found.astype(F32).astype(BF16)


def combine_kernel(targets, spots, own, other, weight, routes, *refs):
    outs, packed = refs[:-1], refs[-1]
    rows = outs[0].shape[0]
    tokens, width = own.shape
    half, eighth = width // 2, width // 8
    mine = spots[0].astype(F32)
    across = jnp.transpose(routes[...].astype(F32))
    named = (across[0:1, :] == mine) | (across[1:2, :] == mine)
    q = lax.broadcasted_iota(jnp.int32, (tokens, tokens), 0)
    t = lax.broadcasted_iota(jnp.int32, (tokens, tokens), 1)
    same = (q // rows) == (t // rows)
    counts = jnp.broadcast_to(named.astype(F32), (16, tokens)).astype(BF16)
    place = jnp.dot(counts, one_hot(same, q <= t), preferred_element_type=F32)[0:1, :] - 1.0
    named = jnp.broadcast_to(named.astype(F32), (tokens, tokens)) > 0.5
    place = jnp.broadcast_to(place, (tokens, tokens)).astype(jnp.int32)
    r = q % rows
    value = ((own[...] + other[...].astype(F32)) * weight[:, 0:1]).astype(BF16)
    low = one_hot(named, same, r < 8, place == r)
    high = one_hot(named, same, r >= 8, place == r - 8)
    packed[:, :half] = (
        jnp.dot(low, value[:, :half], preferred_element_type=F32)
        + jnp.dot(high, value[:, half:], preferred_element_type=F32)
    ).astype(BF16)
    late = jnp.zeros((tokens, eighth), F32)
    for j in range(8):
        pick = one_hot(named, same, r // 2 == j, place == 8 + r % 2)
        late = late + jnp.dot(pick, value[:, j * eighth : (j + 1) * eighth], preferred_element_type=F32)
    packed[:, half:] = late.astype(BF16)
    for index, out in enumerate(outs):
        out[...] = packed[pl.ds(pl.multiple_of(targets[index] * rows, 16), rows), :]


def combine(targets, spots, own, other, weight, routes, rows):
    tokens, width = own.shape
    sends = tokens // rows
    lanes = width // 2 + width // 8
    return pl.pallas_call(
        combine_kernel,
        out_shape=tuple([jax.ShapeDtypeStruct((rows, lanes), BF16)] * sends),
        in_specs=[SCALARS] * 2 + [WHOLE] * 4,
        out_specs=(WHOLE,) * sends,
        scratch_shapes=[VMEM((tokens, lanes), BF16)],
        compiler_params=pltpu.CompilerParams(vmem_limit_bytes=10 << 20),
        name="combine",
    )(targets, spots, own, other, weight, routes)


def unpack_kernel(named_by, mixed, routes, *refs):
    count = len(refs) - 2
    pieces, out, packed = refs[:count], refs[count], refs[count + 1]
    rows, width = mixed.shape
    half, eighth = width // 2, width // 8
    for index in range(count):
        packed[index * rows : (index + 1) * rows, :] = pieces[index][...]
    shape = (rows, count * rows)
    lane = lax.broadcasted_iota(jnp.int32, shape, 1)
    r = lane % rows
    expert = jnp.zeros(shape, F32)
    for index in range(count):
        expert = jnp.where(lane // rows == index, named_by[index].astype(F32), expert)
    named = (routes[:, 0:1].astype(F32) == expert) | (routes[:, 1:2].astype(F32) == expert)
    above = lax.broadcasted_iota(jnp.int32, (rows, rows), 0) >= lax.broadcasted_iota(jnp.int32, (rows, rows), 1)
    place = jnp.dot(one_hot(above), one_hot(named), preferred_element_type=F32) - 1.0
    place = place.astype(jnp.int32)
    low = one_hot(named, r < 8, place == r)
    high = one_hot(named, r >= 8, place == r - 8)
    for j in range(8):
        pick = one_hot(named, r // 2 == j, place == 8 + r % 2)
        here = slice(j * eighth, (j + 1) * eighth)
        there = slice((j % 4) * eighth, (j % 4 + 1) * eighth)
        total = mixed[:, here].astype(F32)
        total += jnp.dot(low if j < 4 else high, packed[:, there], preferred_element_type=F32)
        total += jnp.dot(pick, packed[:, half:], preferred_element_type=F32)
        out[:, here] = total.astype(BF16)


def unpack(named_by, mixed, routes, pieces):
    rows, width = mixed.shape
    return pl.pallas_call(
        unpack_kernel,
        out_shape=jax.ShapeDtypeStruct((rows, width), BF16),
        in_specs=[SCALARS] + [WHOLE] * (2 + len(pieces)),
        out_specs=WHOLE,
        scratch_shapes=[VMEM((rows * len(pieces), pieces[0].shape[1]), BF16)],
        compiler_params=pltpu.CompilerParams(vmem_limit_bytes=6 << 20),
        name="unpack",
    )(named_by, mixed, routes, *pieces)


def body(
    projected,
    carried_tail,
    carried_state,
    filter_taps,
    filter_bias,
    select_weight,
    step_weight,
    step_bias,
    log_rate,
    skip_gain,
    output_weight,
    residual,
    norm_gain,
    router,
    gate_weight,
    up_weight,
    down_weight,
    routes,
):
    ctx, exp = lax.axis_size("ctx"), lax.axis_size("exp")
    ctx_at, exp_at = lax.axis_index("ctx"), lax.axis_index("exp")
    places = ring_places("ctx")
    x_input, z_input = projected[0], projected[1]
    own, width = residual.shape
    columns = output_weight.shape[1]
    taps = filter_taps.shape[0]
    parts = ctx * exp
    me = ctx_at * exp + exp_at
    spots = jnp.stack([ctx_at // (ctx // EXPERTS), me]).astype(jnp.int32)
    targets = jnp.stack([(me + s) % parts for s in range(parts)]).astype(jnp.int32)
    named_by = jnp.stack([(me - s) % parts for s in range(parts)]) // exp // (ctx // EXPERTS)

    x_pieces = spread(lambda k: x_input, "ctx", 0)
    own_routes = jnp.pad(routes.astype(BF16), ((0, 0), (0, LANES - 2)))
    extra = own_routes
    if exp == 2:
        other = rotate(extra, "exp", 1)
        extra = jnp.where(
            exp_at == 0,
            jnp.concatenate([extra, other], axis=0),
            jnp.concatenate([other, extra], axis=0),
        )
    else:
        extra = lax.all_gather(jnp.concatenate([residual, extra], axis=1), "exp", axis=0, tiled=True)
    tail_pad = jnp.zeros((8 - carried_tail.shape[0], carried_tail.shape[1]), F32)
    params = jnp.concatenate(
        [filter_taps, filter_bias[None], step_bias[None], skip_gain[None], jnp.zeros_like(tail_pad)[: 5 - taps],
         tail_pad, carried_tail.astype(F32)]
    )
    router_rows = jnp.pad(router.T, ((0, 16 - EXPERTS), (0, 0)))
    gain = jnp.pad(norm_gain[None, :], ((0, 7), (0, 0)))
    params, router_rows, gain, spots, targets, named_by = lax.optimization_barrier(
        (params, router_rows, gain, spots, targets, named_by.astype(jnp.int32))
    )

    active, proj = activate(places, x_pieces, params, taps, select_weight)
    own_proj, other_proj = pair_sum(proj, "exp")

    splits = exp if exp == 2 else 1

    def bundle(k):
        rows = residual if splits > 1 else jnp.where(exp_at == 0, extra[:, :width], 0)
        piece = lax.dynamic_slice_in_dim(rows, k * columns, columns, axis=1)
        lanes = columns // splits
        piece = jnp.concatenate([piece[:, i * lanes : (i + 1) * lanes] for i in range(splits)], axis=0)
        return jnp.concatenate([z_input, piece, extra[:, -LANES:]], axis=1)

    z_pieces = spread(bundle, "ctx", 0, active)
    value = scan(own_proj, other_proj, active, params, taps, log_rate, step_weight, carried_state)
    spread_places = jnp.concatenate([places, exp_at.astype(jnp.int32)[None]])
    sent, all_routes = project(spread_places, value, output_weight, z_pieces, splits)
    shared = exp == 2 and parts <= 8 and own == 16 and sent.shape[0] == LANES and lax.axis_size("doc") % 2 == 0
    half = lax.rem(lax.axis_index("doc"), 2).astype(jnp.int32)[None]
    if exp == 2:
        summand = rotate(sent, "exp", 1)
        if shared:
            half, sent = lax.optimization_barrier((half, sent))
            gate_first, up_first, half = fetch(half, [gate_weight, up_weight])
            half, sent = lax.optimization_barrier((half, sent))
        mixed = mix(sent, summand)
    else:
        mixed = lax.psum(sent.astype(F32), "exp").astype(BF16)
    mixed_pieces = spread(lambda k: mixed, "ctx", 1)
    normed, weight, mine = norm(places, spots, gain, router_rows, all_routes, mixed_pieces, own)
    total = mine.astype(F32)
    axes = ("ctx", "exp")
    if shared:
        kept, given = shared_experts(half, normed, swap(normed), gate_first, up_first, gate_weight, up_weight, down_weight)
        outs = combine(targets, spots, kept, swap(given), weight, all_routes, own)
        arrived = [outs[0]]
        for s in range(1, parts):
            arrived.append(lax.ppermute(outs[s], axes, [(i, (i + s) % parts) for i in range(parts)]))
        return unpack(named_by, mine, own_routes, arrived)
    else:
        kept = experts(normed, gate_weight, up_weight, down_weight)
        partial = (kept * weight[:, :1]).astype(BF16)
        moved = lax.all_to_all(partial, axes, split_axis=0, concat_axis=0, tiled=True)
        total = total + jnp.sum(moved.reshape(parts, own, width).astype(F32), axis=0)
    return total.astype(BF16)


def solution(mesh):
    placed = (
        P(None, ("doc", "ctx"), "exp"),
        P("doc", "exp"),
        P("doc", "exp"),
        P(None, "exp"),
        P("exp"),
        P(None, "exp"),
        P(None, "exp"),
        P("exp"),
        P(None, "exp"),
        P("exp"),
        P("exp", "ctx"),
        P(("doc", "ctx", "exp"), None),
        P(),
        P(),
        P(("ctx", "exp"), None),
        P(("ctx", "exp"), None),
        P(("ctx", "exp"), None),
        P(("doc", "ctx", "exp"), None),
    )
    return jax.shard_map(
        body, mesh=mesh, in_specs=placed, out_specs=P(("doc", "ctx", "exp"), None), check_vma=False
    )
```

```python
import functools
import math

import jax
import jax.numpy as jnp
from jax import lax
from jax.experimental import pallas as pl
from jax.experimental.pallas import tpu as pltpu
from jax.sharding import PartitionSpec as P

EXPERTS = 4
LANES = 128
FEW = 4
LOG2E = 1.4426950408889634
VMEM = pltpu.VMEM
SMEM = pltpu.SMEM
F32 = jnp.float32
BF16 = jnp.bfloat16


def contract_last(left, right):
    return lax.dot_general(left, right, (((1,), (1,)), ((), ())), preferred_element_type=F32)


def rotate(value, axis, steps):
    count = lax.axis_size(axis)
    return lax.ppermute(value, axis, [(i, (i + steps) % count) for i in range(count)])


def partner(place, step, count):
    paired = count & (count - 1) == 0
    return place ^ step if paired else (place + step) % count


def source(place, step, count):
    paired = count & (count - 1) == 0
    return place ^ step if paired else (place - step) % count


def exchange(value, axis, step, count):
    return lax.ppermute(value, axis, [(i, partner(i, step, count)) for i in range(count)])


def ring_places(axis):
    count = lax.axis_size(axis)
    if count > FEW:
        return jnp.zeros((1,), jnp.int32)
    me = lax.axis_index(axis)
    return jnp.stack([source(me, s, count) for s in range(count)]).astype(jnp.int32)


def spread(make, axis, join, after=None):
    count = lax.axis_size(axis)
    me = lax.axis_index(axis)
    if count <= FEW:
        sent = [make(partner(me, s, count)) for s in range(1, count)]
        if after is not None:
            sent, _ = lax.optimization_barrier((sent, after))
        return [make(me)] + [exchange(sent[s - 1], axis, s, count) for s in range(1, count)]
    stacked = jnp.stack([make(jnp.int32(k)) for k in range(count)])
    moved = lax.all_to_all(stacked, axis, split_axis=0, concat_axis=0, tiled=True)
    return [jnp.concatenate([moved[k] for k in range(count)], axis=join)]


def swap(value):
    count = lax.axis_size("doc")
    return lax.ppermute(value, "doc", [(i, i + 1 - 2 * (i % 2)) for i in range(count)])


def far(value):
    return pltpu.with_memory_space_constraint(value, pltpu.HBM)


def pair_sum(value, axis):
    if lax.axis_size(axis) == 2:
        return [value, rotate(value, axis, 1)]
    total = lax.psum(value.astype(F32), axis).astype(value.dtype)
    return [total, jnp.zeros_like(total)]


FAR = pl.BlockSpec(memory_space=pltpu.HBM)
WHOLE = pl.BlockSpec(memory_space=VMEM)
SCALARS = pl.BlockSpec(memory_space=SMEM)


def activate_kernel(count, taps, places, params, select, *refs):
    pieces, (active, proj, padded, held, sem) = refs[:count], refs[count:]
    copy = pltpu.make_async_copy(select, held, sem)
    copy.start()
    rows = pieces[0].shape[0]
    padded[0:8, :] = params[8:16, :]
    for index in range(count):
        start = pl.multiple_of(8 + places[index] * rows, 8)
        padded[pl.ds(start, rows), :] = pieces[index][...].astype(F32)
    tokens = active.shape[0]
    step = 32

    def block(number, carry):
        base = pl.multiple_of(number * step, step)
        window = padded[pl.ds(base, step + 8), :]
        total = jnp.broadcast_to(params[taps : taps + 1, :], (step, params.shape[1]))
        for k in range(taps):
            offset = 8 - (taps - 1) + k
            total = total + params[k : k + 1, :] * window[offset : offset + step, :]
        value = total / (1.0 + jnp.exp(-total))
        active[pl.ds(base, step), :] = value.astype(BF16)
        return carry

    lax.fori_loop(0, tokens // step, block, 0)
    copy.wait()
    for number in range(tokens // LANES):
        cut = slice(number * LANES, (number + 1) * LANES)
        proj[:, cut] = contract_last(held[...], active[cut, :])


def activate(places, pieces, params, taps, select):
    count = len(pieces)
    tokens = count * pieces[0].shape[0]
    channels = pieces[0].shape[1]
    return pl.pallas_call(
        functools.partial(activate_kernel, count, taps),
        out_shape=(
            jax.ShapeDtypeStruct((tokens, channels), BF16),
            jax.ShapeDtypeStruct((select.shape[0], tokens), F32),
        ),
        in_specs=[SCALARS, WHOLE, FAR] + [WHOLE] * count,
        out_specs=(WHOLE,) * 2,
        scratch_shapes=[
            VMEM((tokens + 8, channels), F32),
            VMEM(select.shape, BF16),
            pltpu.SemaphoreType.DMA,
        ],
        compiler_params=pltpu.CompilerParams(vmem_limit_bytes=12 << 20),
        cost_estimate=pl.CostEstimate(
            flops=2 * tokens * channels * select.shape[0],
            bytes_accessed=4 * tokens * channels,
            transcendentals=tokens * channels,
        ),
        name="activate",
    )(places, params, far(select), *pieces)


def scan_kernel(
    taps, own, other, active, params, log_rate_hbm, step_weight_hbm, state_hbm, value_out,
    sums, steps, scaled, rates, state, coef, step_weight, state_in, log_rate, sems,
):
    tokens, channels = active.shape
    rank = step_weight.shape[0]
    state_size = log_rate.shape[0]
    folds = channels // LANES
    group = min(folds, 16)
    load_weight = pltpu.make_async_copy(step_weight_hbm, step_weight, sems.at[0])
    load_state = pltpu.make_async_copy(state_hbm, state_in, sems.at[1])
    load_rate = pltpu.make_async_copy(log_rate_hbm, log_rate, sems.at[3])
    load_rate.start()
    load_state.start()
    load_weight.start()
    sums[...] = own[...] + other[...]
    copy = pltpu.make_async_copy(sums.at[pl.ds(rank, 2 * state_size), :], coef, sems.at[2])
    copy.start()

    def scatter(target, source):
        for s8 in range(state_size // 8):
            for j in range(folds):
                lanes = slice(j * LANES, (j + 1) * LANES)
                there = slice((s8 * folds + j) * 8, (s8 * folds + j) * 8 + 8)
                target[there, :] = source[s8 * 8 : s8 * 8 + 8, lanes]

    def fold_rows(row, first):
        return pl.ds((row // 8) * (folds * 8) + row % 8 + first * 8, group, stride=8)

    load_rate.wait()
    scatter(state, log_rate)
    for s in range(state_size):
        for first in range(0, folds, group):
            rates[s * folds + first : s * folds + first + group, :] = (
                jnp.exp(state[fold_rows(s, first), :]) * (-LOG2E)
            )
    load_state.wait()
    scatter(state, state_in)
    load_weight.wait()

    for number in range(tokens // LANES):
        cut = slice(number * LANES, (number + 1) * LANES)
        low = jnp.transpose(sums[0:rank, cut]).astype(BF16)
        width = min(channels, 256)
        for w in range(channels // width):
            lanes = slice(w * width, (w + 1) * width)
            raw = jnp.dot(low, step_weight[:, lanes], preferred_element_type=F32)
            raw = raw + params[taps + 1 : taps + 2, lanes]
            size = jnp.maximum(raw, 0.0) + jnp.log(1.0 + jnp.exp(-jnp.abs(raw)))
            times = size * active[cut, lanes].astype(F32)
            for i in range(LANES // 8):
                for j in range(width // LANES):
                    block = (number * LANES // 8 + i) * folds + w * (width // LANES) + j
                    there = slice(block * 8, block * 8 + 8)
                    part = (slice(i * 8, i * 8 + 8), slice(j * LANES, (j + 1) * LANES))
                    steps[there, :] = size[part]
                    scaled[there, :] = times[part]
    copy.wait()

    for first in range(0, folds, group):
        start = tuple(state[fold_rows(s, first), :] for s in range(state_size))

        def eight(number, held):
            base = number * (folds * 8) + first * 8
            held = list(held)
            for r in range(8):
                token = number * 8 + r
                rows = pl.ds(base + r, group, stride=8)
                size, times = steps[rows, :], scaled[rows, :]
                total = None
                for s in range(state_size):
                    rate = rates[s * folds + first : s * folds + first + group, :]
                    held[s] = jnp.exp2(size * rate) * held[s] + times * coef[s, token]
                    term = held[s] * coef[state_size + s, token]
                    total = term if total is None else total + term
                steps[rows, :] = total
            return tuple(held)

        lax.fori_loop(0, tokens // 8, eight, start)

    def unfold(number, carry):
        here = pl.ds(pl.multiple_of(number * 16, 16), 16)
        for j in range(folds):
            lanes = slice(j * LANES, (j + 1) * LANES)
            found = []
            for half in range(2):
                block = pl.multiple_of((number * 2 + half) * (folds * 8) + j * 8, 8)
                found.append(steps[pl.ds(block, 8), :])
            gain = params[taps + 2 : taps + 3, lanes]
            value_out[here, lanes] = jnp.concatenate(found, axis=0) + gain * active[here, lanes].astype(F32)
        return carry

    lax.fori_loop(0, tokens // 16, unfold, 0)


def scan(own, other, active, params, taps, log_rate, step_weight, state_in):
    tokens, channels = active.shape
    state_size = log_rate.shape[0]
    folded = (state_size * channels // LANES + 8, LANES)
    return pl.pallas_call(
        functools.partial(scan_kernel, taps),
        out_shape=jax.ShapeDtypeStruct((tokens, channels), F32),
        in_specs=[WHOLE] * 4 + [FAR] * 3,
        out_specs=WHOLE,
        scratch_shapes=[
            VMEM(own.shape, F32),
            VMEM((tokens * channels // LANES + 8, LANES), F32),
            VMEM((tokens * channels // LANES + 8, LANES), F32),
            VMEM(folded, F32),
            VMEM(folded, F32),
            SMEM((2 * state_size, tokens), F32),
            VMEM(step_weight.shape, BF16),
            VMEM(state_in.shape, F32),
            VMEM(log_rate.shape, F32),
            pltpu.SemaphoreType.DMA((4,)),
        ],
        compiler_params=pltpu.CompilerParams(vmem_limit_bytes=16 << 20),
        cost_estimate=pl.CostEstimate(
            flops=3000 * tokens * channels * state_size,
            bytes_accessed=8 * tokens * channels,
            transcendentals=tokens * channels * state_size,
        ),
        name="scan",
    )(own, other, active, params, far(log_rate), far(step_weight), far(state_in))


def project_kernel(count, columns, splits, places, value_in, weight_hbm, *refs):
    pieces = refs[:count]
    send_out, routes_out, base_out, gated, out_weight, sem = refs[count:]
    lanes = columns // splits
    copy = pltpu.make_async_copy(weight_hbm, out_weight, sem)
    copy.start()
    tokens, channels = value_in.shape
    rows = pieces[0].shape[0]
    tile = 16
    for index in range(count):
        begin = pl.multiple_of(places[index] * rows, tile)
        routes_out[pl.ds(begin, rows), :] = pieces[index][:, channels + lanes :]

        def gate(number, carry):
            local = pl.ds(pl.multiple_of(number * tile, tile), tile)
            here = pl.ds(pl.multiple_of(begin + number * tile, tile), tile)
            z = pieces[index][local, :channels].astype(F32)
            gated[here, :] = (value_in[here, :] * (z / (1.0 + jnp.exp(-z)))).astype(BF16)
            return carry

        lax.fori_loop(0, rows // tile, gate, 0)
    copy.wait()
    for number in range(tokens // LANES):
        cut = slice(number * LANES, (number + 1) * LANES)
        base_out[cut, :] = jnp.dot(gated[cut, :], out_weight[...], preferred_element_type=F32)
    part = rows // splits
    for index in range(count):
        begin = places[index] * rows + (places[count] * part if splits > 1 else 0)
        here = pl.ds(pl.multiple_of(begin, tile), part)
        for k in range(splits):
            piece = pieces[index][k * part : (k + 1) * part, channels : channels + lanes]
            base_out[here, k * lanes : (k + 1) * lanes] += piece.astype(F32)
    for number in range(tokens // LANES):
        cut = slice(number * LANES, (number + 1) * LANES)
        send_out[cut, :] = base_out[cut, :].astype(BF16)


def project(places, value, out_weight, pieces, splits):
    tokens, channels = value.shape
    columns = out_weight.shape[1]
    count = len(pieces)
    return pl.pallas_call(
        functools.partial(project_kernel, count, columns, splits),
        out_shape=(
            jax.ShapeDtypeStruct((tokens, columns), BF16),
            jax.ShapeDtypeStruct((tokens, LANES), BF16),
        ),
        in_specs=[SCALARS, WHOLE, FAR] + [WHOLE] * count,
        out_specs=(WHOLE,) * 2,
        scratch_shapes=[
            VMEM((tokens, columns), F32),
            VMEM((tokens, channels), BF16),
            VMEM(out_weight.shape, BF16),
            pltpu.SemaphoreType.DMA,
        ],
        compiler_params=pltpu.CompilerParams(vmem_limit_bytes=16 << 20),
        cost_estimate=pl.CostEstimate(
            flops=2 * tokens * channels * columns,
            bytes_accessed=8 * tokens * channels,
            transcendentals=tokens * channels,
        ),
        name="project",
    )(places, value, far(out_weight), *pieces)


def mix_kernel(base, summand, mixed):
    mixed[...] = (base[...].astype(F32) + summand[...].astype(F32)).astype(BF16)


def mix(base, summand):
    return pl.pallas_call(
        mix_kernel,
        out_shape=jax.ShapeDtypeStruct(base.shape, BF16),
        in_specs=[WHOLE] * 2,
        out_specs=WHOLE,
        compiler_params=pltpu.CompilerParams(vmem_limit_bytes=4 << 20),
        name="mix",
    )(base, summand)


def norm_kernel(count, places, spots, gain, router, routes, *refs):
    pieces = refs[:count]
    normed, weight, own_rows = refs[count : count + 3]
    mixed = pieces[0] if count == 1 else refs[-1]
    tokens = normed.shape[0]
    columns = pieces[0].shape[1]
    for index in range(count if count > 1 else 0):
        start = pl.multiple_of(places[index] * columns, LANES)
        mixed[:, pl.ds(start, columns)] = pieces[index][...]
    mine = spots[0].astype(F32)
    step = 32

    def block(number, carry):
        cut = pl.ds(pl.multiple_of(number * step, step), step)
        value = mixed[cut, :].astype(F32)
        square = jnp.mean(value * value, axis=-1, keepdims=True) + 1e-06
        scaled = (value * lax.rsqrt(square) * gain[0:1, :]).astype(BF16)
        normed[cut, :] = scaled
        return carry

    lax.fori_loop(0, tokens // step, block, 0)
    for c in range(tokens // LANES):
        cut = slice(c * LANES, (c + 1) * LANES)
        logits = contract_last(normed[cut, :], router[...])
        first = routes[cut, 0:1].astype(F32)
        second = routes[cut, 1:2].astype(F32)
        ids = lax.broadcasted_iota(jnp.int32, logits.shape, 1).astype(F32)
        first_logit = jnp.sum(jnp.where(ids == first, logits, 0.0), axis=1, keepdims=True)
        second_logit = jnp.sum(jnp.where(ids == second, logits, 0.0), axis=1, keepdims=True)
        first_gate = jnp.where(first == mine, 1.0 / (1.0 + jnp.exp(second_logit - first_logit)), 0.0)
        second_gate = jnp.where(second == mine, 1.0 / (1.0 + jnp.exp(first_logit - second_logit)), 0.0)
        weight[cut, :] = jnp.broadcast_to(first_gate + second_gate, (LANES, LANES))
    rows = own_rows.shape[0]
    own_rows[...] = mixed[pl.ds(pl.multiple_of(spots[1] * rows, 16), rows), :]


def norm(places, spots, gain, router, routes, pieces, own):
    count = len(pieces)
    tokens = pieces[0].shape[0]
    width = count * pieces[0].shape[1]
    return pl.pallas_call(
        functools.partial(norm_kernel, count),
        out_shape=(
            jax.ShapeDtypeStruct((tokens, width), BF16),
            jax.ShapeDtypeStruct((tokens, LANES), F32),
            jax.ShapeDtypeStruct((own, width), BF16),
        ),
        in_specs=[SCALARS] * 2 + [WHOLE] * (3 + count),
        out_specs=(WHOLE,) * 3,
        scratch_shapes=[VMEM((tokens, width), BF16)] if count > 1 else [],
        compiler_params=pltpu.CompilerParams(vmem_limit_bytes=8 << 20),
        name="norm",
    )(places, spots, gain, router, routes, *pieces)


def fetch_kernel(parts, half_rows, half, *refs):
    count = len(refs) // 2 - 1
    sources, targets, done, sems = refs[:count], refs[count : 2 * count], refs[-2], refs[-1]
    rows = targets[0].shape[0]
    part = rows // parts
    copies = []
    for index in range(count):
        for k in range(parts):
            start = pl.multiple_of(half[0] * half_rows + k * part, 16)
            copies.append(
                pltpu.make_async_copy(
                    sources[index].at[pl.ds(start, part), :],
                    targets[index].at[pl.ds(k * part, part), :],
                    sems.at[index * parts + k],
                )
            )
    for copy in copies:
        copy.start()
    for copy in copies:
        copy.wait()
    done[0] = half[0]


def fetch(half, weights):
    half_rows, width = weights[0].shape[0] // 2, weights[0].shape[1]
    rows = half_rows // 2
    parts = 4
    return pl.pallas_call(
        functools.partial(fetch_kernel, parts, half_rows),
        out_shape=tuple([VMEM((rows, width), BF16)] * len(weights)) + (jax.ShapeDtypeStruct((1,), jnp.int32),),
        in_specs=[SCALARS] + [FAR] * len(weights),
        out_specs=tuple([WHOLE] * len(weights)) + (SCALARS,),
        scratch_shapes=[pltpu.SemaphoreType.DMA((parts * len(weights),))],
        compiler_params=pltpu.CompilerParams(vmem_limit_bytes=1 << 20),
        cost_estimate=pl.CostEstimate(
            flops=0, bytes_accessed=4 * rows * width * len(weights), transcendentals=0
        ),
        name="fetch",
    )(half, *[far(w) for w in weights])


def shared_kernel(half, own, other, gate_first, up_first, gate, up, down, kept, given, tokens, hidden, late, last, sems):
    rows = own.shape[0]
    quarter, width = gate_first.shape
    begin = half[0] * (2 * quarter)
    copies = []
    for index, (source, offset) in enumerate(((gate, quarter), (up, quarter), (down, 0), (down, quarter))):
        here = pl.ds(pl.multiple_of(begin + offset, 16), quarter)
        target = late.at[index] if index < 2 else last.at[index - 2]
        copies.append(pltpu.make_async_copy(source.at[here, :], target, sems.at[index]))
    for copy in copies[:2]:
        copy.start()
    tokens[0:rows, :] = own[...]
    tokens[rows:, :] = other[...]

    def activate_hidden(gate_rows, up_rows, place):
        gate_act = contract_last(tokens[...], gate_rows[...])
        up_act = contract_last(tokens[...], up_rows[...])
        value = gate_act / (1.0 + jnp.exp(-gate_act)) * up_act
        hidden[:, place * quarter : (place + 1) * quarter] = value.astype(BF16)

    activate_hidden(gate_first, up_first, 0)
    for copy in copies[2:]:
        copy.start()
    copies[0].wait()
    copies[1].wait()
    activate_hidden(late.at[0], late.at[1], 1)
    copies[2].wait()
    copies[3].wait()
    step = 256
    for start in range(0, width, step):
        here = slice(start, start + step)
        product = jnp.dot(hidden[:, :quarter], last[0, :, here], preferred_element_type=F32)
        product += jnp.dot(hidden[:, quarter:], last[1, :, here], preferred_element_type=F32)
        kept[:, here] = product[0:rows, :]
        given[:, here] = product[rows:, :].astype(BF16)


def shared_experts(half, own, other, gate_first, up_first, gate, up, down):
    rows, width = own.shape
    quarter = gate_first.shape[0]
    return pl.pallas_call(
        shared_kernel,
        out_shape=(jax.ShapeDtypeStruct((rows, width), F32), jax.ShapeDtypeStruct((rows, width), BF16)),
        in_specs=[SCALARS] + [WHOLE] * 4 + [FAR] * 3,
        out_specs=(WHOLE,) * 2,
        scratch_shapes=[
            VMEM((2 * rows, width), BF16),
            VMEM((2 * rows, 2 * quarter), BF16),
            VMEM((2, quarter, width), BF16),
            VMEM((2, quarter, width), BF16),
            pltpu.SemaphoreType.DMA((4,)),
        ],
        compiler_params=pltpu.CompilerParams(vmem_limit_bytes=36 << 20),
        cost_estimate=pl.CostEstimate(
            flops=24 * rows * quarter * width,
            bytes_accessed=8 * quarter * width,
            transcendentals=4 * rows * quarter,
        ),
        name="experts",
    )(half, own, other, gate_first, up_first, far(gate), far(up), far(down))


def expert_kernel(tokens, gate, up, down, total):
    number = pl.program_id(0)

    @pl.when(number == 0)
    def _():
        total[...] = jnp.zeros_like(total)

    for start in range(0, total.shape[0], LANES):
        cut = slice(start, start + LANES)
        gate_act = contract_last(tokens[cut, :], gate[...])
        up_act = contract_last(tokens[cut, :], up[...])
        hidden = (gate_act / (1.0 + jnp.exp(-gate_act)) * up_act).astype(BF16)
        total[cut, :] += jnp.dot(hidden, down[...], preferred_element_type=F32)


def experts(tokens, gate, up, down):
    rows, width = tokens.shape
    hidden = gate.shape[0]
    block = hidden if hidden <= 512 else math.gcd(hidden, 512)
    weights = pl.BlockSpec((block, width), lambda i: (i, 0))
    return pl.pallas_call(
        expert_kernel,
        grid=(hidden // block,),
        out_shape=jax.ShapeDtypeStruct((rows, width), F32),
        in_specs=[WHOLE] + [weights] * 3,
        out_specs=WHOLE,
        compiler_params=pltpu.CompilerParams(vmem_limit_bytes=40 << 20),
        cost_estimate=pl.CostEstimate(
            flops=6 * rows * hidden * width,
            bytes_accessed=6 * hidden * width,
            transcendentals=rows * hidden,
        ),
        name="experts",
    )(tokens, gate, up, down)


def one_hot(*conditions):
    found = conditions[0]
    for condition in conditions[1:]:
        found = found & condition
    return found.astype(F32).astype(BF16)


def combine_kernel(targets, spots, own, other, weight, routes, *refs):
    outs, packed = refs[:-1], refs[-1]
    rows = outs[0].shape[0]
    tokens, width = own.shape
    half, eighth = width // 2, width // 8
    mine = spots[0].astype(F32)
    across = jnp.transpose(routes[...].astype(F32))
    named = (across[0:1, :] == mine) | (across[1:2, :] == mine)
    q = lax.broadcasted_iota(jnp.int32, (tokens, tokens), 0)
    t = lax.broadcasted_iota(jnp.int32, (tokens, tokens), 1)
    same = (q // rows) == (t // rows)
    counts = jnp.broadcast_to(named.astype(F32), (16, tokens)).astype(BF16)
    place = jnp.dot(counts, one_hot(same, q <= t), preferred_element_type=F32)[0:1, :] - 1.0
    named = jnp.broadcast_to(named.astype(F32), (tokens, tokens)) > 0.5
    place = jnp.broadcast_to(place, (tokens, tokens)).astype(jnp.int32)
    r = q % rows
    value = ((own[...] + other[...].astype(F32)) * weight[:, 0:1]).astype(BF16)
    low = one_hot(named, same, r < 8, place == r)
    high = one_hot(named, same, r >= 8, place == r - 8)
    packed[:, :half] = (
        jnp.dot(low, value[:, :half], preferred_element_type=F32)
        + jnp.dot(high, value[:, half:], preferred_element_type=F32)
    ).astype(BF16)
    late = jnp.zeros((tokens, eighth), F32)
    for j in range(8):
        pick = one_hot(named, same, r // 2 == j, place == 8 + r % 2)
        late = late + jnp.dot(pick, value[:, j * eighth : (j + 1) * eighth], preferred_element_type=F32)
    packed[:, half:] = late.astype(BF16)
    for index, out in enumerate(outs):
        out[...] = packed[pl.ds(pl.multiple_of(targets[index] * rows, 16), rows), :]


def combine(targets, spots, own, other, weight, routes, rows):
    tokens, width = own.shape
    sends = tokens // rows
    lanes = width // 2 + width // 8
    return pl.pallas_call(
        combine_kernel,
        out_shape=tuple([jax.ShapeDtypeStruct((rows, lanes), BF16)] * sends),
        in_specs=[SCALARS] * 2 + [WHOLE] * 4,
        out_specs=(WHOLE,) * sends,
        scratch_shapes=[VMEM((tokens, lanes), BF16)],
        compiler_params=pltpu.CompilerParams(vmem_limit_bytes=10 << 20),
        name="combine",
    )(targets, spots, own, other, weight, routes)


def unpack_kernel(named_by, mixed, routes, *refs):
    count = len(refs) - 2
    pieces, out, packed = refs[:count], refs[count], refs[count + 1]
    rows, width = mixed.shape
    half, eighth = width // 2, width // 8
    for index in range(count):
        packed[index * rows : (index + 1) * rows, :] = pieces[index][...]
    shape = (rows, count * rows)
    lane = lax.broadcasted_iota(jnp.int32, shape, 1)
    r = lane % rows
    expert = jnp.zeros(shape, F32)
    for index in range(count):
        expert = jnp.where(lane // rows == index, named_by[index].astype(F32), expert)
    named = (routes[:, 0:1].astype(F32) == expert) | (routes[:, 1:2].astype(F32) == expert)
    above = lax.broadcasted_iota(jnp.int32, (rows, rows), 0) >= lax.broadcasted_iota(jnp.int32, (rows, rows), 1)
    place = jnp.dot(one_hot(above), one_hot(named), preferred_element_type=F32) - 1.0
    place = place.astype(jnp.int32)
    low = one_hot(named, r < 8, place == r)
    high = one_hot(named, r >= 8, place == r - 8)
    for j in range(8):
        pick = one_hot(named, r // 2 == j, place == 8 + r % 2)
        here = slice(j * eighth, (j + 1) * eighth)
        there = slice((j % 4) * eighth, (j % 4 + 1) * eighth)
        total = mixed[:, here].astype(F32)
        total += jnp.dot(low if j < 4 else high, packed[:, there], preferred_element_type=F32)
        total += jnp.dot(pick, packed[:, half:], preferred_element_type=F32)
        out[:, here] = total.astype(BF16)


def unpack(named_by, mixed, routes, pieces):
    rows, width = mixed.shape
    return pl.pallas_call(
        unpack_kernel,
        out_shape=jax.ShapeDtypeStruct((rows, width), BF16),
        in_specs=[SCALARS] + [WHOLE] * (2 + len(pieces)),
        out_specs=WHOLE,
        scratch_shapes=[VMEM((rows * len(pieces), pieces[0].shape[1]), BF16)],
        compiler_params=pltpu.CompilerParams(vmem_limit_bytes=6 << 20),
        name="unpack",
    )(named_by, mixed, routes, *pieces)


def body(
    projected,
    carried_tail,
    carried_state,
    filter_taps,
    filter_bias,
    select_weight,
    step_weight,
    step_bias,
    log_rate,
    skip_gain,
    output_weight,
    residual,
    norm_gain,
    router,
    gate_weight,
    up_weight,
    down_weight,
    routes,
):
    ctx, exp = lax.axis_size("ctx"), lax.axis_size("exp")
    ctx_at, exp_at = lax.axis_index("ctx"), lax.axis_index("exp")
    places = ring_places("ctx")
    x_input, z_input = projected[0], projected[1]
    own, width = residual.shape
    columns = output_weight.shape[1]
    taps = filter_taps.shape[0]
    parts = ctx * exp
    me = ctx_at * exp + exp_at
    spots = jnp.stack([ctx_at // (ctx // EXPERTS), me]).astype(jnp.int32)
    targets = jnp.stack([(me + s) % parts for s in range(parts)]).astype(jnp.int32)
    named_by = jnp.stack([(me - s) % parts for s in range(parts)]) // exp // (ctx // EXPERTS)

    x_pieces = spread(lambda k: x_input, "ctx", 0)
    own_routes = jnp.pad(routes.astype(BF16), ((0, 0), (0, LANES - 2)))
    extra = own_routes
    if exp == 2:
        other = rotate(extra, "exp", 1)
        extra = jnp.where(
            exp_at == 0,
            jnp.concatenate([extra, other], axis=0),
            jnp.concatenate([other, extra], axis=0),
        )
    else:
        extra = lax.all_gather(jnp.concatenate([residual, extra], axis=1), "exp", axis=0, tiled=True)
    tail_pad = jnp.zeros((8 - carried_tail.shape[0], carried_tail.shape[1]), F32)
    params = jnp.concatenate(
        [filter_taps, filter_bias[None], step_bias[None], skip_gain[None], jnp.zeros_like(tail_pad)[: 5 - taps],
         tail_pad, carried_tail.astype(F32)]
    )
    router_rows = jnp.pad(router.T, ((0, 16 - EXPERTS), (0, 0)))
    gain = jnp.pad(norm_gain[None, :], ((0, 7), (0, 0)))
    params, router_rows, gain, spots, targets, named_by = lax.optimization_barrier(
        (params, router_rows, gain, spots, targets, named_by.astype(jnp.int32))
    )

    active, proj = activate(places, x_pieces, params, taps, select_weight)
    own_proj, other_proj = pair_sum(proj, "exp")

    splits = exp if exp == 2 else 1

    def bundle(k):
        rows = residual if splits > 1 else jnp.where(exp_at == 0, extra[:, :width], 0)
        piece = lax.dynamic_slice_in_dim(rows, k * columns, columns, axis=1)
        lanes = columns // splits
        piece = jnp.concatenate([piece[:, i * lanes : (i + 1) * lanes] for i in range(splits)], axis=0)
        return jnp.concatenate([z_input, piece, extra[:, -LANES:]], axis=1)

    z_pieces = spread(bundle, "ctx", 0, active)
    value = scan(own_proj, other_proj, active, params, taps, log_rate, step_weight, carried_state)
    spread_places = jnp.concatenate([places, exp_at.astype(jnp.int32)[None]])
    sent, all_routes = project(spread_places, value, output_weight, z_pieces, splits)
    shared = exp == 2 and parts <= 8 and own == 16 and sent.shape[0] == LANES and lax.axis_size("doc") % 2 == 0
    half = lax.rem(lax.axis_index("doc"), 2).astype(jnp.int32)[None]
    if exp == 2:
        summand = rotate(sent, "exp", 1)
        if shared:
            half, sent = lax.optimization_barrier((half, sent))
            gate_first, up_first, half = fetch(half, [gate_weight, up_weight])
            half, sent = lax.optimization_barrier((half, sent))
        mixed = mix(sent, summand)
    else:
        mixed = lax.psum(sent.astype(F32), "exp").astype(BF16)
    mixed_pieces = spread(lambda k: mixed, "ctx", 1)
    normed, weight, mine = norm(places, spots, gain, router_rows, all_routes, mixed_pieces, own)
    total = mine.astype(F32)
    axes = ("ctx", "exp")
    if shared:
        kept, given = shared_experts(half, normed, swap(normed), gate_first, up_first, gate_weight, up_weight, down_weight)
        outs = combine(targets, spots, kept, swap(given), weight, all_routes, own)
        arrived = [outs[0]]
        for s in range(1, parts):
            arrived.append(lax.ppermute(outs[s], axes, [(i, (i + s) % parts) for i in range(parts)]))
        return unpack(named_by, mine, own_routes, arrived)
    else:
        kept = experts(normed, gate_weight, up_weight, down_weight)
        partial = (kept * weight[:, :1]).astype(BF16)
        moved = lax.all_to_all(partial, axes, split_axis=0, concat_axis=0, tiled=True)
        total = total + jnp.sum(moved.reshape(parts, own, width).astype(F32), axis=0)
    return total.astype(BF16)


def solution(mesh):
    placed = (
        P(None, ("doc", "ctx"), "exp"),
        P("doc", "exp"),
        P("doc", "exp"),
        P(None, "exp"),
        P("exp"),
        P(None, "exp"),
        P(None, "exp"),
        P("exp"),
        P(None, "exp"),
        P("exp"),
        P("exp", "ctx"),
        P(("doc", "ctx", "exp"), None),
        P(),
        P(),
        P(("ctx", "exp"), None),
        P(("ctx", "exp"), None),
        P(("ctx", "exp"), None),
        P(("doc", "ctx", "exp"), None),
    )
    return jax.shard_map(
        body, mesh=mesh, in_specs=placed, out_specs=P(("doc", "ctx", "exp"), None), check_vma=False
    )
```
